32 devices in a mesh: ctx: 8 (over z, y), exp: 4 (over x, core).
Axes of the slice: x: 2, y: 2, z: 4, core: 2. Of those that a mesh axis runs over, the one named last changes fastest.
Arguments:
- span_q: bfloat16 [512, 5120], P('ctx', 'exp'), may hold values from -12 to 12
- decode_q: bfloat16 [512, 5120], P('ctx', 'exp'), may hold values from -12 to 12
- k_cache: bfloat16 [24576, 1024], P('ctx', 'exp'), may hold values from -12 to 12
- v_cache: bfloat16 [24576, 1024], P('ctx', 'exp'), may hold values from -6 to 6
- span_k: bfloat16 [512, 1024], P('ctx', 'exp'), may hold values from -6 to 6
- span_v: bfloat16 [512, 1024], P('ctx', 'exp'), may hold values from -6 to 6
- decode_k: bfloat16 [512, 1024], P('ctx', 'exp'), may hold values from -6 to 6
- decode_v: bfloat16 [512, 1024], P('ctx', 'exp'), may hold values from -6 to 6
- decode_pos: int32 [512], replicated, may hold values from 2 to 24576
- out_weight: bfloat16 [5120, 5120], P('exp'), may hold values from -0.078125 to 0.078125
- span_resid: bfloat16 [512, 5120], P(('ctx', 'exp')), may hold values from -3 to 3
- decode_resid: bfloat16 [512, 5120], P(('ctx', 'exp')), may hold values from -3 to 3
- norm_gain: bfloat16 [5120], replicated, may hold values from 0.099609375 to 1.8984375
- router: bfloat16 [5120, 4], replicated, may hold values from -0.15625 to 0.15625
- span_expert: int32 [512, 1], P(('ctx', 'exp')), may hold values from 0 to 3; in each aligned block of 16 rows (0 to 15, 16 to 31, ...) at most 8 rows name the same one
- decode_expert: int32 [512, 1], P(('ctx', 'exp')), may hold values from 0 to 3; in each aligned block of 16 rows (0 to 15, 16 to 31, ...) at most 8 rows name the same one
- w_gate: bfloat16 [4, 5120, 8192], P('exp', None, 'ctx'), may hold values from -0.078125 to 0.078125
- w_up: bfloat16 [4, 5120, 8192], P('exp', None, 'ctx'), may hold values from -0.078125 to 0.078125
- w_down: bfloat16 [4, 8192, 5120], P('exp', 'ctx'), may hold values from -0.0625 to 0.0625
Outputs:
- span_out: bfloat16 [512, 5120], P(('ctx', 'exp'))
- decode_out: bfloat16 [512, 5120], P(('ctx', 'exp'))
The draws below stay inside these ranges and needn't reach their ends.
Inputs may be any that keep to these rules, and one draw needn't show every extreme that they name: `span_expert`: among the rows of one device, no expert is chosen by more than 8 rows. `decode_expert`: among the rows of one device, no expert is chosen by more than 8 rows.
All inputs are finite; a program needn't handle non-finite values.
Results may differ from the reference program's by a relative error of at most 0.015.
Values may be sent and summed in bfloat16 or wider, within the bound.
No kernel may reach another device: no remote copies, remote signals or barrier semaphores. Data moves between devices by JAX's collectives and lax.ppermute only.
A program may use at most 192 MiB of HBM per device.

```python
import math
import jax
import jax.numpy as jnp
import numpy as np
from jax import lax

D = 5120
HEADS = 40
KV_HEADS = 8
HEAD = 128
FF = 8192
TOK_DEV = 64
PRE_DEV = 3072
SPAN = 512
DECODE = 512
PREFIX = 24576
EXPERTS = 4
CAP = 8
N_CTX = 8
N_EXP = 4


def shared_direction(key):
    signs = jax.random.bernoulli(jax.random.fold_in(key, 50), 0.5, (HEAD,))
    return jnp.where(signs, 2.4, -2.4).astype(jnp.float32)


def shared_own(key):
    base = jax.random.normal(jax.random.fold_in(key, 60), (DECODE, KV_HEADS, HEAD), jnp.float32)
    return jnp.clip(base, -4.0, 4.0)


def plant_rows(key, values, direction, repeats):
    picked_rows = jax.random.randint(key, (8,), 0, values.shape[0])
    strength = jax.random.uniform(jax.random.fold_in(key, 1), (8,), jnp.float32, 3.0, 5.0)
    planted = strength[:, None] * jnp.tile(direction, repeats)[None, :]
    return values.at[picked_rows].set(planted)


def draw_span_q(key, part):
    direction = shared_direction(key)
    key = jax.random.fold_in(key, 1)
    values = jnp.clip(3.0 * jax.random.normal(key, (SPAN, HEADS * HEAD), jnp.float32), -12.0, 12.0)
    values = plant_rows(jax.random.fold_in(key, 9), values, direction, HEADS)
    return values.astype(jnp.bfloat16)


def draw_decode_q(key, part):
    direction = shared_direction(key)
    common = shared_own(key)
    key = jax.random.fold_in(key, 2)
    group = HEADS // KV_HEADS
    noise = jax.random.normal(key, (DECODE, KV_HEADS, group, HEAD), jnp.float32)
    values = 3.0 * (0.6 * common[:, :, None, :] + 0.8 * noise)
    values = jnp.clip(values, -12.0, 12.0).reshape(DECODE, HEADS * HEAD)
    values = plant_rows(jax.random.fold_in(key, 9), values, direction, HEADS)
    return values.astype(jnp.bfloat16)


def draw_decode_k(key, part):
    common = shared_own(key)
    values = jnp.clip(0.6 * common, -6.0, 6.0).reshape(DECODE, KV_HEADS * HEAD)
    return values.astype(jnp.bfloat16)


def draw_k_cache(key, part):
    direction = shared_direction(key)
    key = jax.random.fold_in(key, 3)
    values = jnp.clip(jax.random.normal(key, (PREFIX, KV_HEADS * HEAD), jnp.float32), -6.0, 6.0)
    jitter = 0.02 * jax.random.normal(jax.random.fold_in(key, 4), (2, KV_HEADS * HEAD), jnp.float32)
    leading_scale = jnp.array([1.875 - 0.1 / HEAD ** 0.5, 1.875], jnp.float32)
    leading = leading_scale[:, None] * jnp.tile(direction, KV_HEADS)[None, :] + jitter
    values = values.at[0:2].set(leading)
    return values.astype(jnp.bfloat16)


def touch_ends(values, own_key, low, high):
    longest = values.shape.index(max(values.shape))
    spots = []
    for shift in (0, 1):
        where = [jax.random.randint(jax.random.fold_in(own_key, axis), (), 0, length) for axis, length in enumerate(values.shape)]
        where[longest] = (where[longest] + shift) % values.shape[longest]
        spots.append(tuple(where))
    return values.at[spots[0]].set(low).at[spots[1]].set(high)


def level_of(rng, dims, shards, low, high):
    loudness = 1.0
    for position, blocks in shards:
        heights = jax.random.uniform(jax.random.fold_in(jax.random.fold_in(rng, 6), position), (blocks,), jnp.float32, low / len(shards), high / len(shards))
        loudness = loudness * jnp.repeat(jnp.exp(heights), dims[position] // blocks).reshape((-1,) + (1,) * (len(dims) - 1 - position))
    return loudness


def assign_block(stream_key, own, number, rows, number_of, top, bound, skew):
    order = jax.random.permutation(stream_key, number_of)
    crowded, usual = portions_of(number_of, rows * top, bound, skew, True), portions_of(number_of, rows * top, bound, skew, False)
    places = jnp.arange(number_of)

    def named(sizes, rotation):
        used = int((sizes > 0).sum())
        fixed = max(1, used // 4)
        moved = fixed + (places - fixed + rotation * (used - fixed)) % max(1, number_of - fixed)
        return jnp.zeros((number_of,), jnp.int32).at[order[jnp.where(places < fixed, places, moved)]].set(jnp.asarray(sizes, jnp.int32))

    sizes = jnp.where(number % 4 == 0, named(crowded, number // 4), named(usual, number - number // 4 - 1))
    mixed = jax.random.permutation(jax.random.fold_in(own, 3), number_of)
    donor, sink = mixed[0:number_of // 2 * 2:2], mixed[1:number_of // 2 * 2:2]
    margin = jnp.minimum(sizes[donor] - 1, bound - sizes[sink]) // 2
    margin = jnp.where((donor == order[0]) | (sink == order[0]) | (sizes[sink] == 0), 0, jnp.maximum(margin, 0))
    moved = jax.random.randint(jax.random.fold_in(own, 4), (number_of // 2,), 0, 1 << 20) % (margin + 1)
    sizes = sizes.at[donor].add(-moved).at[sink].add(moved)
    items = jnp.searchsorted(jnp.cumsum(sizes), jnp.arange(rows * top), side="right").astype(jnp.int32)
    listing = items.reshape(top, rows).T
    listing = listing[jax.random.permutation(jax.random.fold_in(own, 1), rows)]
    rotation = jax.random.randint(jax.random.fold_in(own, 2), (rows, 1), 0, top)
    return jnp.take_along_axis(listing, (jnp.arange(top)[None, :] + rotation) % top, axis=1)


def portions_of(count, total, reach, slope, full):
    portions = [(1 << 20) // math.isqrt(standing ** slope) + 1 for standing in range(1, count + 1)]
    largest = reach if full else min(reach, max(-(-total // count), total * portions[0] // sum(portions)))
    least = 1 if total - largest >= count - 1 else 0
    holding, spare = [largest] + [least] * (count - 1), total - largest - least * (count - 1)
    while spare > 0:
        movable = [i for i in range(1, count) if holding[i] < largest] or [i for i in range(1, count) if holding[i] < reach]
        pool, remaining = sum([portions[i] for i in movable]), spare
        for i in movable:
            more = min(reach - holding[i], max(1, remaining * portions[i] // pool), spare)
            holding[i] = holding[i] + more
            spare = spare - more
    return np.array(holding)


def bell_draw(own_key, extent, spread, most, pieces=(), kind=jnp.bfloat16):
    drawn = jax.random.normal(own_key, extent, jnp.float32) * spread
    if len(pieces) > 0:
        drawn = level_of(own_key, extent, pieces, -0.22, 0.18) * drawn
    return jnp.clip(drawn, min=-most, max=most).astype(kind)


def setup_inputs(seed: int = 0) -> dict:
    arg_keys = jax.random.split(jax.random.key(seed), 20)
    span_q = draw_span_q(jax.random.fold_in(arg_keys[19], 71), 0)
    decode_q = draw_decode_q(jax.random.fold_in(arg_keys[19], 71), 0)
    k_cache = draw_k_cache(jax.random.fold_in(arg_keys[19], 71), 0)
    v_cache = bell_draw(arg_keys[3], (PREFIX, KV_HEADS * HEAD), 1.0, 6.0, ((0, 8), (1, 4)))
    span_k = bell_draw(arg_keys[4], (SPAN, KV_HEADS * HEAD), 1.0, 6.0, ((0, 8), (1, 4)))
    span_v = bell_draw(arg_keys[5], (SPAN, KV_HEADS * HEAD), 1.0, 6.0, ((0, 8), (1, 4)))
    decode_k = draw_decode_k(jax.random.fold_in(arg_keys[19], 71), 0)
    decode_v = bell_draw(arg_keys[7], (DECODE, KV_HEADS * HEAD), 1.0, 6.0, ((0, 8), (1, 4)))
    decode_pos = touch_ends(jax.random.randint(arg_keys[8], (DECODE,), 2, PREFIX + 1), jax.random.fold_in(arg_keys[8], 1), 2, PREFIX).astype(jnp.int32)
    out_weight = bell_draw(arg_keys[9], (HEADS * HEAD, D), (HEADS * HEAD) ** -0.5, 0.078125, ((0, 4),))
    span_resid = bell_draw(arg_keys[10], (SPAN, D), 0.5, 3.0, ((0, 32),))
    decode_resid = bell_draw(arg_keys[11], (DECODE, D), 0.5, 3.0, ((0, 32),))
    norm_gain = jnp.clip(1.0 + 0.18 * jax.random.normal(arg_keys[12], (D,), jnp.float32), 0.099609375, 1.8984375).astype(jnp.bfloat16)
    router = bell_draw(arg_keys[13], (D, EXPERTS), (D // 4) ** -0.5, 0.15625)
    span_expert_keys = jax.random.split(jax.random.fold_in(arg_keys[14], 1), SPAN // (TOK_DEV // N_EXP))
    span_expert_turns = jax.random.permutation(jax.random.fold_in(arg_keys[14], 3), SPAN // (TOK_DEV // N_EXP))
    span_expert = jax.vmap(lambda own, number: assign_block(jax.random.fold_in(arg_keys[14], 2), own, number, TOK_DEV // N_EXP, EXPERTS, 1, CAP, 2))(span_expert_keys, span_expert_turns).reshape((SPAN, 1))
    decode_expert_keys = jax.random.split(jax.random.fold_in(arg_keys[15], 1), DECODE // (TOK_DEV // N_EXP))
    decode_expert_turns = jax.random.permutation(jax.random.fold_in(arg_keys[15], 3), DECODE // (TOK_DEV // N_EXP))
    decode_expert = jax.vmap(lambda own, number: assign_block(jax.random.fold_in(arg_keys[15], 2), own, number, TOK_DEV // N_EXP, EXPERTS, 1, CAP, 2))(decode_expert_keys, decode_expert_turns).reshape((DECODE, 1))
    w_gate = bell_draw(arg_keys[16], (EXPERTS, D, FF), D ** -0.5, 0.078125, ((0, 4), (2, 8)))
    w_up = bell_draw(arg_keys[17], (EXPERTS, D, FF), D ** -0.5, 0.078125, ((0, 4), (2, 8)))
    w_down = bell_draw(arg_keys[18], (EXPERTS, FF, D), FF ** -0.5, 0.0625, ((0, 4), (1, 8)))
    return {"span_q": span_q, "decode_q": decode_q, "k_cache": k_cache, "v_cache": v_cache, "span_k": span_k, "span_v": span_v, "decode_k": decode_k, "decode_v": decode_v, "decode_pos": decode_pos, "out_weight": out_weight, "span_resid": span_resid, "decode_resid": decode_resid, "norm_gain": norm_gain, "router": router, "span_expert": span_expert, "decode_expert": decode_expert, "w_gate": w_gate, "w_up": w_up, "w_down": w_down}


NEG = -1e+30
EPS = 1e-05

def block_part(queries, key_pre, val_pre, key_span, val_span, decode_pos, block_id):
    row_count = queries.shape[0]
    score_scale = HEAD ** (-0.5)
    prefix_pos = block_id * PRE_DEV + jnp.arange(PRE_DEV, dtype=jnp.int32)
    span_pos = block_id * TOK_DEV + jnp.arange(TOK_DEV, dtype=jnp.int32)
    row_ids = jnp.arange(row_count, dtype=jnp.int32)
    query_f = queries.astype(jnp.float32)
    score_pre = jnp.einsum('rsgd,jd->rsgj', query_f, key_pre.astype(jnp.float32)) * score_scale
    score_span = jnp.einsum('rsgd,jd->rsgj', query_f, key_span.astype(jnp.float32)) * score_scale
    seen_pre = jnp.stack([jnp.ones((row_count, PRE_DEV), bool), prefix_pos[None, :] < decode_pos[:, None]], 1)[:, :, None, :]
    seen_span = jnp.stack([span_pos[None, :] <= row_ids[:, None], jnp.zeros((row_count, TOK_DEV), bool)], 1)[:, :, None, :]
    score_pre = jnp.where(seen_pre, score_pre, NEG)
    score_span = jnp.where(seen_span, score_span, NEG)
    top_max = jnp.maximum(lax.optimization_barrier(jnp.max(score_pre, -1)), lax.optimization_barrier(jnp.max(score_span, -1)))
    weight_pre = jnp.where(seen_pre, jnp.exp(score_pre - top_max[..., None]), 0.0)
    weight_span = jnp.where(seen_span, jnp.exp(score_span - top_max[..., None]), 0.0)
    denom_part = lax.optimization_barrier(jnp.sum(weight_pre, -1)) + lax.optimization_barrier(jnp.sum(weight_span, -1))
    numer_part = jnp.einsum('rsgj,jd->rsgd', weight_pre.astype(jnp.bfloat16).astype(jnp.float32), val_pre.astype(jnp.float32))
    numer_part = numer_part + jnp.einsum('rsgj,jd->rsgd', weight_span.astype(jnp.bfloat16).astype(jnp.float32), val_span.astype(jnp.float32))
    return (top_max, numer_part, denom_part)

def run_expert(packed):
    rows_in, gate_w, up_w, down_w = packed
    gate_h = jnp.dot(rows_in, gate_w, preferred_element_type=jnp.float32)
    up_h = jnp.dot(rows_in, up_w, preferred_element_type=jnp.float32)
    hidden = (jax.nn.silu(gate_h) * up_h).astype(jnp.bfloat16)
    slots = hidden.shape[0]
    hidden_blocks = hidden.reshape(slots, N_CTX, FF // N_CTX).astype(jnp.float32)
    down_blocks = down_w.reshape(N_CTX, FF // N_CTX, D).astype(jnp.float32)
    partial_out = jnp.einsum('nch,chd->cnd', hidden_blocks, down_blocks)
    rounded = lax.optimization_barrier(partial_out.astype(jnp.bfloat16)).astype(jnp.float32)
    return lax.optimization_barrier(jnp.sum(rounded, 0)).astype(jnp.bfloat16)

def reference(span_q, decode_q, k_cache, v_cache, span_k, span_v, decode_k, decode_v, decode_pos, out_weight, span_resid, decode_resid, norm_gain, router, span_expert, decode_expert, w_gate, w_up, w_down):
    row_count = SPAN
    head_group = HEADS // KV_HEADS
    score_scale = HEAD ** (-0.5)
    queries = jnp.stack([span_q, decode_q], 1).reshape(row_count, 2, KV_HEADS, head_group, HEAD).transpose(2, 0, 1, 3, 4)
    keys_all = k_cache.reshape(PREFIX, KV_HEADS, HEAD).transpose(1, 0, 2)
    vals_all = v_cache.reshape(PREFIX, KV_HEADS, HEAD).transpose(1, 0, 2)
    span_keys = span_k.reshape(SPAN, KV_HEADS, HEAD).transpose(1, 0, 2)
    span_vals = span_v.reshape(SPAN, KV_HEADS, HEAD).transpose(1, 0, 2)
    block_ids = jnp.arange(N_CTX, dtype=jnp.int32)

    def all_heads(block_id):

        def head_part(packed):
            query_h, key_h, val_h, ckey_h, cval_h = packed
            key_pre = lax.dynamic_slice_in_dim(key_h, block_id * PRE_DEV, PRE_DEV, 0)
            val_pre = lax.dynamic_slice_in_dim(val_h, block_id * PRE_DEV, PRE_DEV, 0)
            key_span = lax.dynamic_slice_in_dim(ckey_h, block_id * TOK_DEV, TOK_DEV, 0)
            val_span = lax.dynamic_slice_in_dim(cval_h, block_id * TOK_DEV, TOK_DEV, 0)
            return block_part(query_h, key_pre, val_pre, key_span, val_span, decode_pos, block_id)
        return lax.map(head_part, (queries, keys_all, vals_all, span_keys, span_vals))
    block_tops = lax.map(lambda block_id: all_heads(block_id)[0], block_ids)
    top_all = lax.optimization_barrier(jnp.max(block_tops, 0))

    def accumulate(carry, block_id):
        top_b, numer_b, denom_b = all_heads(block_id)
        factor = jnp.exp(top_b - top_all)
        return ((carry[0] + numer_b * factor[..., None], carry[1] + denom_b * factor), None)
    start = (jnp.zeros((KV_HEADS, row_count, 2, head_group, HEAD), jnp.float32), jnp.zeros((KV_HEADS, row_count, 2, head_group), jnp.float32))
    (numer_sum, denom_sum), _ = lax.scan(accumulate, start, block_ids)
    dec_query = decode_q.reshape(row_count, KV_HEADS, head_group, HEAD).astype(jnp.float32)
    dec_key = decode_k.reshape(row_count, KV_HEADS, HEAD).astype(jnp.float32)
    own_score = lax.optimization_barrier(jnp.sum(dec_query * dec_key[:, :, None, :], -1)) * score_scale
    own_score = jnp.stack([jnp.full_like(own_score, NEG), own_score], 1).transpose(2, 0, 1, 3)
    dec_val = decode_v.reshape(row_count, KV_HEADS, HEAD).astype(jnp.float32)
    own_val = jnp.stack([jnp.zeros_like(dec_val), dec_val], 1).transpose(2, 0, 1, 3)
    total_max = jnp.maximum(top_all, own_score)
    scale_top = jnp.exp(top_all - total_max)
    own_weight = jnp.exp(own_score - total_max)
    numer = numer_sum * scale_top[..., None] + own_weight[..., None] * own_val[:, :, :, None, :]
    denom = denom_sum * scale_top + own_weight
    attn = (numer / denom[..., None]).astype(jnp.bfloat16)
    attn = attn.transpose(1, 2, 0, 3, 4).reshape(row_count * 2, HEADS * HEAD)
    residual = jnp.stack([span_resid, decode_resid], 1).reshape(row_count * 2, D).astype(jnp.float32)
    stream = jnp.dot(attn, out_weight, preferred_element_type=jnp.float32) + residual
    normed = (stream * lax.rsqrt(lax.optimization_barrier(jnp.mean(stream * stream, -1, keepdims=True)) + EPS) * norm_gain.astype(jnp.float32)).astype(jnp.bfloat16)
    logits = jnp.dot(normed, router, preferred_element_type=jnp.float32)
    expert_ids = jnp.stack([span_expert[:, 0], decode_expert[:, 0]], 1)
    flat_ids = expert_ids.reshape(-1)
    gate_value = jax.nn.sigmoid(jnp.take_along_axis(logits, flat_ids[:, None], 1)[:, 0])
    routed_in = (normed.astype(jnp.float32) * gate_value[:, None]).astype(jnp.bfloat16)
    block_total = N_CTX * N_EXP
    per_block = row_count // block_total
    blocked = expert_ids.reshape(block_total, per_block, 2)
    same_expert = blocked[:, :, None, :] == blocked[:, None, :, :]
    row_order = jnp.arange(per_block, dtype=jnp.int32)
    earlier = row_order[None, :] < row_order[:, None]
    slot_index = lax.optimization_barrier(jnp.sum(same_expert & earlier[None, :, :, None], 2)).astype(jnp.int32)
    column = (jnp.arange(block_total, dtype=jnp.int32)[:, None, None] * (2 * CAP) + jnp.arange(2, dtype=jnp.int32)[None, None, :] * CAP + slot_index).reshape(-1)
    buffer = jnp.zeros((EXPERTS, block_total * 2 * CAP, D), jnp.bfloat16).at[flat_ids, column].set(routed_in)
    expert_all = lax.map(run_expert, (buffer, w_gate, w_up, w_down))
    routed = expert_all[flat_ids, column].astype(jnp.float32)
    result = (stream + routed).astype(jnp.bfloat16).reshape(row_count, 2, D)
    return (result[:, 0], result[:, 1])
```

```python
import functools
import math

import jax
import jax.numpy as jnp
from jax import lax
from jax.experimental import pallas as pl
from jax.experimental.pallas import tpu as pltpu
from jax.sharding import PartitionSpec as P

HEADS = 40
KV_HEADS = 8
HEAD = 128

NEG = -1e30
EPS = 1e-05
SCALE = HEAD ** (-0.5)
EXP2_SCALE = SCALE * math.log2(math.e)
EXTRA = 128
PART = 32
CHUNK = 512
TILE = 512
VMEM_LIMIT = 48 * 1024 * 1024


def ring_order(count):
    if count % 8:
        return list(range(count))
    major, minor = 4, count // 4
    path = [(0, 0)]
    for b in range(minor):
        span = range(1, major) if b % 2 == 0 else range(major - 1, 0, -1)
        path += [(a, b) for a in span]
    path += [(0, b) for b in range(minor - 1, 0, -1)]
    return [a * minor + b for a, b in path]


def attend_kernel(info_ref, *refs, offsets, after, kv, group):
    owners = len(offsets)
    q_refs = refs[:owners]
    pos_ref, k_ref, v_ref, ks_ref, vs_ref = refs[owners : owners + 5]
    o_ref, q_scr, s_scr = refs[owners + 5 + after :]
    owner = pl.program_id(0)
    stream = pl.program_id(1)
    rows = q_scr.shape[0]
    pre = k_ref.shape[0]
    chunk = math.gcd(pre, CHUNK)
    stacked = rows * group
    span_keys = ks_ref.shape[0]
    contract = (((1,), (1,)), ((), ()))
    for i in range(owners):

        @pl.when(owner == i)
        def _(i=i):
            q_scr[...] = q_refs[i][0]

    def run(is_span):
        ctx = info_ref[info_ref.shape[0] - 1]
        if is_span:
            step = offsets[1] - offsets[0] if owners > 1 else 0
            from_here = (info_ref[offsets[0] + owner * step] - ctx) * rows
            lim = from_here + 1 + lax.broadcasted_iota(jnp.int32, (rows, 1), 0)
        else:
            lim = pos_ref[...] - ctx * pre
        lim = jnp.concatenate([lim] * group, axis=0)
        lane = lax.broadcasted_iota(jnp.int32, (rows, EXTRA), 1)
        packed = jnp.full((rows, EXTRA), NEG, jnp.float32)

        def scores(h):
            q = jnp.concatenate(
                [q_scr[:, (h * group + g) * HEAD : (h * group + g + 1) * HEAD] for g in range(group)],
                axis=0,
            )
            top = jnp.full((stacked, HEAD), NEG, jnp.float32)
            for j in range(pre // chunk):
                key = k_ref[j * chunk : (j + 1) * chunk, h * HEAD : (h + 1) * HEAD]
                s = lax.dot_general(q, key, contract, preferred_element_type=jnp.float32)
                if not is_span:
                    pos = j * chunk + lax.broadcasted_iota(jnp.int32, (stacked, chunk), 1)
                    s = jnp.where(pos < lim, s, NEG)
                s_scr[h, :, j * chunk : (j + 1) * chunk] = s
                for t in range(chunk // HEAD):
                    top = jnp.maximum(top, s[:, t * HEAD : (t + 1) * HEAD])
            m = jnp.max(top, axis=1, keepdims=True)
            s_own = None
            if is_span:
                key = ks_ref[:, h * HEAD : (h + 1) * HEAD]
                s_own = lax.dot_general(q, key, contract, preferred_element_type=jnp.float32)
                pos = lax.broadcasted_iota(jnp.int32, (stacked, span_keys), 1)
                s_own = jnp.where(pos < lim, s_own, NEG)
                m = jnp.maximum(m, jnp.max(s_own, axis=1, keepdims=True))
            return jnp.maximum(m, -1e29), s_own

        def values(h, m, s_own):
            acc = jnp.zeros((stacked, 2 * HEAD), jnp.float32)
            for j in range(pre // chunk):
                s = s_scr[h, :, j * chunk : (j + 1) * chunk]
                w = jnp.exp2((s - m) * EXP2_SCALE).astype(jnp.bfloat16)
                val = v_ref[j * chunk : (j + 1) * chunk, h * HEAD : (h + 1) * HEAD]
                val = jnp.concatenate([val, jnp.ones_like(val)], axis=1)
                acc = acc + jnp.dot(w, val, preferred_element_type=jnp.float32)
            if is_span:
                w = jnp.exp2((s_own - m) * EXP2_SCALE).astype(jnp.bfloat16)
                val = vs_ref[:, h * HEAD : (h + 1) * HEAD]
                val = jnp.concatenate([val, jnp.ones_like(val)], axis=1)
                acc = acc + jnp.dot(w, val, preferred_element_type=jnp.float32)
            total = acc[:, HEAD:]
            seen = total > 0.0
            safe = jnp.where(seen, total, 1.0)
            out = (acc[:, :HEAD] / safe).astype(jnp.bfloat16)
            lse = jnp.where(seen, m * SCALE + jnp.log(safe), NEG)
            return out, lse

        state = scores(0)
        for h in range(kv):
            following = scores(h + 1) if h + 1 < kv else None
            out, lse = values(h, *state)
            for g in range(group):
                head = h * group + g
                o_ref[0, 0, :, head * HEAD : (head + 1) * HEAD] = out[g * rows : (g + 1) * rows]
                packed = jnp.where(lane % PART == head, lse[g * rows : (g + 1) * rows], packed)
            state = following
        o_ref[0, 0, :, kv * group * HEAD :] = pack_lse(packed, lane)

    @pl.when(stream == 0)
    def _():
        run(True)

    @pl.when(stream == 1)
    def _():
        run(False)


def pack_lse(value, lane):
    first = value.astype(jnp.bfloat16)
    rest = value - first.astype(jnp.float32)
    second = rest.astype(jnp.bfloat16)
    third = rest - second.astype(jnp.float32)
    picked = jnp.where(
        lane < PART,
        first.astype(jnp.float32),
        jnp.where(lane < 2 * PART, second.astype(jnp.float32), third),
    )
    return picked.astype(jnp.bfloat16)


def unpack_lse(extra):
    value = extra.astype(jnp.float32)
    return value[:, :PART] + value[:, PART : 2 * PART] + value[:, 2 * PART : 3 * PART]


def attend(queries, offsets, info, positions, caches, kv, group, after=()):
    owners = len(queries)
    _, rows, width = queries[0].shape
    pre = caches[0].shape[0]
    step = offsets[1] - offsets[0] if owners > 1 else 0
    whole = lambda a: pl.BlockSpec(a.shape, lambda o, s, info: (0,) * a.ndim)
    flops = 4 * owners * 2 * rows * group * kv * pre * HEAD
    return pl.pallas_call(
        functools.partial(
            attend_kernel, offsets=offsets, after=len(after), kv=kv, group=group
        ),
        out_shape=jax.ShapeDtypeStruct((owners, 2, rows, width + EXTRA), jnp.bfloat16),
        grid_spec=pltpu.PrefetchScalarGridSpec(
            num_scalar_prefetch=1,
            grid=(owners, 2),
            in_specs=[pl.BlockSpec((1, rows, width), lambda o, s, info: (s, 0, 0)) for _ in queries]
            + [pl.BlockSpec((rows, 1), lambda o, s, info: (info[offsets[0] + o * step], 0))]
            + [whole(a) for a in caches]
            + [pl.BlockSpec(memory_space=pl.ANY) for _ in after],
            out_specs=pl.BlockSpec(
                (1, 1, rows, width + EXTRA), lambda o, s, info: (o, s, 0, 0)
            ),
            scratch_shapes=[
                pltpu.VMEM((rows, width), jnp.bfloat16),
                pltpu.VMEM((kv, rows * group, pre), jnp.float32),
            ],
        ),
        compiler_params=pltpu.CompilerParams(vmem_limit_bytes=VMEM_LIMIT),
        cost_estimate=pl.CostEstimate(
            flops=2 * flops,
            bytes_accessed=4 * pre * kv * HEAD,
            transcendentals=owners * 2 * rows * group * kv * pre,
        ),
        name="attend",
    )(info, *queries, positions, *caches, *after)


def relay_kernel(*refs, plans, arrays, after):
    outs = refs[arrays + after :]
    for out, plan in zip(outs, plans):
        done = 0
        for index, start, stop in plan:
            out[done : done + stop - start] = refs[index][start:stop]
            done += stop - start


def relay(arrays, plans, after=()):
    rows = [sum(stop - start for _, start, stop in plan) for plan in plans]
    outs = [jax.ShapeDtypeStruct((r, *arrays[0].shape[1:]), arrays[0].dtype) for r in rows]
    return pl.pallas_call(
        functools.partial(relay_kernel, plans=plans, arrays=len(arrays), after=len(after)),
        out_shape=outs,
        in_specs=[pl.BlockSpec(memory_space=pltpu.VMEM)] * len(arrays)
        + [pl.BlockSpec(memory_space=pl.ANY)] * len(after),
        out_specs=[pl.BlockSpec(memory_space=pltpu.VMEM)] * len(outs),
        compiler_params=pltpu.CompilerParams(vmem_limit_bytes=VMEM_LIMIT),
        cost_estimate=pl.CostEstimate(
            flops=0, bytes_accessed=4 * sum(math.prod(o.shape) for o in outs), transcendentals=0
        ),
        name="relay",
    )(*arrays, *after)


def fetch(parts, axis):
    def copy(n, i):
        source, target, sems = parts[n]
        size = target.shape[1 + axis]
        tile = pl.ds(pl.multiple_of(i * size, size), size)
        view = source.at[tile] if axis == 0 else source.at[:, tile]
        return pltpu.make_async_copy(view, target.at[i], sems.at[i])

    def start(i, carry):
        for n in range(len(parts)):
            copy(n, i).start()
        return carry

    lax.fori_loop(0, parts[0][1].shape[0], start, 0)
    return lambda n, i: copy(n, i).wait()


def project_kernel(rows_ref, weight_ref, away_ref, kept_ref, tiles, sems):
    count, _, size = tiles.shape
    wait = fetch([(weight_ref, tiles, sems)], 1)
    half = away_ref.shape[0]

    def step(i, carry):
        wait(0, i)
        out = jnp.dot(rows_ref[...], tiles[i], preferred_element_type=jnp.float32)
        part = pl.ds(pl.multiple_of(i * size, size), size)
        away_ref[:, part] = out[:half].astype(jnp.bfloat16)
        kept_ref[:, part] = out[half:]
        return carry

    lax.fori_loop(0, count, step, 0)


def project(rows, weight):
    count, depth = rows.shape
    width = weight.shape[1]
    tile = math.gcd(width, TILE)
    return pl.pallas_call(
        project_kernel,
        out_shape=[
            jax.ShapeDtypeStruct((count // 2, width), jnp.bfloat16),
            jax.ShapeDtypeStruct((count // 2, width), jnp.float32),
        ],
        in_specs=[
            pl.BlockSpec(memory_space=pltpu.VMEM),
            pl.BlockSpec(memory_space=pltpu.HBM),
        ],
        out_specs=[pl.BlockSpec(memory_space=pltpu.VMEM)] * 2,
        scratch_shapes=[
            pltpu.VMEM((width // tile, depth, tile), jnp.bfloat16),
            pltpu.SemaphoreType.DMA((width // tile,)),
        ],
        compiler_params=pltpu.CompilerParams(vmem_limit_bytes=VMEM_LIMIT),
        cost_estimate=pl.CostEstimate(
            flops=2 * count * depth * width, bytes_accessed=2 * depth * width, transcendentals=0
        ),
        name="project",
    )(rows, weight)


def expert_in_kernel(*refs, blocks):
    gate_ref, up_ref, o_ref, rows_ref, gate, up, gate_acc, up_acc, gate_sems, up_sems = refs[blocks:]
    count, size, _ = gate.shape
    wait = fetch([(gate_ref.at[0], gate, gate_sems), (up_ref.at[0], up, up_sems)], 0)
    done = 0
    for block in refs[:blocks]:
        rows_ref[done : done + block.shape[0]] = block[...]
        done += block.shape[0]
    gate_acc[...] = jnp.zeros_like(gate_acc)
    up_acc[...] = jnp.zeros_like(up_acc)

    def step(i, carry):
        rows = rows_ref[:, pl.ds(pl.multiple_of(i * size, size), size)]
        wait(0, i)
        gate_acc[...] += jnp.dot(rows, gate[i], preferred_element_type=jnp.float32)
        wait(1, i)
        up_acc[...] += jnp.dot(rows, up[i], preferred_element_type=jnp.float32)
        return carry

    lax.fori_loop(0, count, step, 0)
    gate_h = gate_acc[...]
    hidden = gate_h / (1.0 + jnp.exp(-gate_h)) * up_acc[...]
    o_ref[...] = hidden.astype(jnp.bfloat16)


def expert_in(blocks, w_gate, w_up):
    depth, units = w_gate.shape[1:]
    if any(b.shape[0] % 16 for b in blocks):
        blocks = [jnp.concatenate(blocks)]
    rows = sum(b.shape[0] for b in blocks)
    tile = math.gcd(depth, TILE)
    return pl.pallas_call(
        functools.partial(expert_in_kernel, blocks=len(blocks)),
        out_shape=jax.ShapeDtypeStruct((rows, units), jnp.bfloat16),
        in_specs=[pl.BlockSpec(memory_space=pltpu.VMEM)] * len(blocks)
        + [pl.BlockSpec(memory_space=pltpu.HBM)] * 2,
        out_specs=pl.BlockSpec(memory_space=pltpu.VMEM),
        scratch_shapes=[pltpu.VMEM((rows, depth), jnp.bfloat16)]
        + [pltpu.VMEM((depth // tile, tile, units), jnp.bfloat16)] * 2
        + [pltpu.VMEM((rows, units), jnp.float32)] * 2
        + [pltpu.SemaphoreType.DMA((depth // tile,))] * 2,
        compiler_params=pltpu.CompilerParams(vmem_limit_bytes=VMEM_LIMIT),
        cost_estimate=pl.CostEstimate(
            flops=4 * rows * depth * units,
            bytes_accessed=4 * depth * units,
            transcendentals=rows * units,
        ),
        name="expert_in",
    )(*blocks, w_gate, w_up)


def expert_out_kernel(hidden_ref, down_ref, *refs):
    o_ref, down, sems = refs[-3:]
    count, _, size = down.shape
    wait = fetch([(down_ref.at[0], down, sems)], 1)

    def step(i, carry):
        wait(0, i)
        out = jnp.dot(hidden_ref[...], down[i], preferred_element_type=jnp.float32)
        o_ref[:, pl.ds(pl.multiple_of(i * size, size), size)] = out.astype(jnp.bfloat16)
        return carry

    lax.fori_loop(0, count, step, 0)


def expert_out(hidden, w_down, after=()):
    rows, units = hidden.shape
    width = w_down.shape[2]
    tile = math.gcd(width, TILE)
    return pl.pallas_call(
        expert_out_kernel,
        out_shape=jax.ShapeDtypeStruct((rows, width), jnp.bfloat16),
        in_specs=[
            pl.BlockSpec(memory_space=pltpu.VMEM),
            pl.BlockSpec(memory_space=pltpu.HBM),
        ]
        + [pl.BlockSpec(memory_space=pl.ANY)] * len(after),
        out_specs=pl.BlockSpec(memory_space=pltpu.VMEM),
        scratch_shapes=[
            pltpu.VMEM((width // tile, units, tile), jnp.bfloat16),
            pltpu.SemaphoreType.DMA((width // tile,)),
        ],
        compiler_params=pltpu.CompilerParams(vmem_limit_bytes=VMEM_LIMIT),
        cost_estimate=pl.CostEstimate(
            flops=2 * rows * units * width, bytes_accessed=2 * units * width, transcendentals=0
        ),
        name="expert_out",
    )(hidden, w_down, *after)


def merge(parts, heads):
    for head in range(heads):
        lses = [lse[:, head : head + 1] for _, lse in parts]
        top = functools.reduce(jnp.maximum, lses)
        weights = [jnp.exp(lse - top) for lse in lses]
        total = sum(weights)
        inverse = 1.0 / total
        out = 0.0
        for (value, _), weight in zip(parts, weights):
            out = out + value(head).astype(jnp.float32) * (weight * inverse)
        yield head, out, top + jnp.log(total)


def combine_kernel(recv_ref, part_ref, o_ref, *, heads, only):
    rows = part_ref.shape[2]
    width = heads * HEAD
    stream = pl.program_id(0)

    def both():
        def reader(ref):
            return lambda head: ref[:, head * HEAD : (head + 1) * HEAD]

        recv, part = recv_ref.at[0], part_ref.at[0, 0]
        parts = [(reader(ref), unpack_lse(ref[:, width:])) for ref in (recv, part)]
        lane = lax.broadcasted_iota(jnp.int32, (rows, EXTRA), 1)
        packed = jnp.full((rows, EXTRA), NEG, jnp.float32)
        for head, out, lse in merge(parts, heads):
            o_ref[0, :, head * HEAD : (head + 1) * HEAD] = out.astype(jnp.bfloat16)
            packed = jnp.where(lane % PART == head, lse, packed)
        o_ref[0, :, width:] = pack_lse(packed, lane)

    if only is None:
        both()
    else:
        pl.when(stream == only)(both)

        @pl.when(stream != only)
        def _():
            o_ref[...] = part_ref[0]


def combine(recv, part, index, heads, only=None):
    _, _, rows, width = part.shape
    return pl.pallas_call(
        functools.partial(combine_kernel, heads=heads, only=only),
        out_shape=jax.ShapeDtypeStruct((2, rows, width), jnp.bfloat16),
        grid=(2,),
        in_specs=[
            pl.BlockSpec((1, rows, width), lambda s: (s if only is None else 0, 0, 0)),
            pl.BlockSpec((1, 1, rows, width), lambda s: (index, s, 0, 0)),
        ],
        out_specs=pl.BlockSpec((1, rows, width), lambda s: (s, 0, 0)),
        compiler_params=pltpu.CompilerParams(vmem_limit_bytes=VMEM_LIMIT),
        cost_estimate=pl.CostEstimate(
            flops=16 * rows * width, bytes_accessed=12 * rows * width, transcendentals=0
        ),
        name="combine",
    )(recv, part)


def finish_kernel(own_ref, left_ref, right_ref, q_ref, k_ref, v_ref, o_ref, *, heads, group):
    width = heads * HEAD
    stream = pl.program_id(0)

    def run(decode):
        def reader(ref):
            return lambda head: ref[:, head * HEAD : (head + 1) * HEAD]

        refs = [own_ref.at[0, 0], left_ref.at[0], right_ref.at[0]]
        parts = [(reader(ref), unpack_lse(ref[:, width:])) for ref in refs]
        if decode:
            scores = []
            for head in range(heads):
                kv = head // group
                q = q_ref[:, head * HEAD : (head + 1) * HEAD].astype(jnp.float32)
                k = k_ref[:, kv * HEAD : (kv + 1) * HEAD].astype(jnp.float32)
                scores.append(jnp.sum(q * k, axis=1, keepdims=True) * SCALE)
            own_value = lambda head: v_ref[:, (head // group) * HEAD : (head // group + 1) * HEAD]
            parts.append((own_value, jnp.concatenate(scores, axis=1)))
        for head, out, _ in merge(parts, heads):
            o_ref[0, :, head * HEAD : (head + 1) * HEAD] = out.astype(jnp.bfloat16)

    @pl.when(stream == 0)
    def _():
        run(False)

    @pl.when(stream == 1)
    def _():
        run(True)


def finish(own, left, right, decode_q, decode_k, decode_v, heads, group):
    _, _, rows, width = own.shape
    whole = lambda a: pl.BlockSpec(a.shape, lambda s: (0,) * a.ndim)
    part = pl.BlockSpec((1, rows, width), lambda s: (s, 0, 0))
    return pl.pallas_call(
        functools.partial(finish_kernel, heads=heads, group=group),
        out_shape=jax.ShapeDtypeStruct((2, rows, heads * HEAD), jnp.bfloat16),
        grid=(2,),
        in_specs=[pl.BlockSpec((1, 1, rows, width), lambda s: (0, s, 0, 0)), part, part]
        + [whole(a) for a in (decode_q, decode_k, decode_v)],
        out_specs=pl.BlockSpec((1, rows, heads * HEAD), lambda s: (s, 0, 0)),
        compiler_params=pltpu.CompilerParams(vmem_limit_bytes=VMEM_LIMIT),
        cost_estimate=pl.CostEstimate(
            flops=16 * rows * width, bytes_accessed=16 * rows * width, transcendentals=0
        ),
        name="finish",
    )(own, left, right, decode_q, decode_k, decode_v)


def on_device(
    span_q,
    decode_q,
    k_cache,
    v_cache,
    span_k,
    span_v,
    decode_k,
    decode_v,
    decode_pos,
    out_weight,
    span_resid,
    decode_resid,
    norm_gain,
    router,
    span_expert,
    decode_expert,
    w_gate,
    w_up,
    w_down,
):
    f32, bf16 = jnp.float32, jnp.bfloat16
    tok_rows, row_width = span_q.shape
    pre_rows = k_cache.shape[0]
    kv = k_cache.shape[1] // HEAD
    group = HEADS // KV_HEADS
    heads = kv * group
    model_width = span_resid.shape[1]
    ctx_count, exp_count = lax.axis_size("ctx"), lax.axis_size("exp")
    ctx, exp = lax.axis_index("ctx"), lax.axis_index("exp")
    x_count = exp_count // 2
    x, core = exp // 2, exp % 2

    ring = ring_order(ctx_count)
    half = ctx_count // 2
    forward = [(ring[i], ring[(i + 1) % ctx_count]) for i in range(ctx_count)]
    backward = [(b, a) for a, b in forward]
    place = [0] * ctx_count
    for i, c in enumerate(ring):
        place[c] = i
    here = sum(jnp.where(ctx == c, i, 0) for c, i in enumerate(place) if i)
    spot = (here + jnp.arange(ctx_count + 1, dtype=jnp.int32)) % ctx_count
    owner = sum(jnp.where(spot == i, c, 0) for i, c in enumerate(ring) if c)
    info = jnp.where(jnp.arange(ctx_count + 1) == ctx_count, ctx, owner).astype(jnp.int32)
    positions = decode_pos[:, None]
    caches = (k_cache, v_cache, span_k, span_v)

    def ahead(value):
        return lax.ppermute(value, "ctx", forward)

    def back(value):
        return lax.ppermute(value, "ctx", backward)

    other_core = [(e, e ^ 1) for e in range(exp_count)]

    def shift_x(step):
        return [(e, ((e // 2 + step) % x_count) * 2 + e % 2) for e in range(exp_count)]

    def attend_for(queries, offsets, after=()):
        offsets = tuple(offset % ctx_count for offset in offsets)
        return attend(queries, offsets, info, positions, caches, kv, group, after)

    queries = jnp.stack([span_q, decode_q])
    both = [((0, 0, 2),), ((1, 0, 2),)]
    from_back, from_ahead = ahead(queries), back(queries)
    own_part = attend_for([queries], [0])
    from_back, from_ahead = relay([from_back, from_ahead], both, [own_part])
    parts = {}
    for step in range(1, half - 1):
        arrived = ahead(from_back), back(from_ahead)
        done = attend_for([from_ahead, from_back], [step, -step])
        plans = both if step < half - 2 else both + [((0, 0, 1),), ((1, 1, 2),)]
        from_back, from_ahead, *sent = relay(arrived, plans, [done])
        parts[step] = (done, 0), (done, 1)
    arrived = ahead(sent[0]), back(sent[1])
    near = half - 1
    (far,) = relay(arrived, [((0, 0, 1), (1, 0, 1))], [done])
    far_part = attend_for([far], [half])
    done = attend_for([from_ahead, from_back], [near, -near])
    parts[near] = (done, 0), (done, 1)

    to_ahead, to_back = ahead(far_part[0, 0:1]), back(far_part[0, 1:2])
    for step in range(near, 0, -1):
        first = step == near
        to_ahead = ahead(combine(to_ahead, *parts[step][0], heads, 0 if first else None))
        to_back = back(combine(to_back, *parts[step][1], heads, 1 if first else None))
    attn = finish(own_part, to_ahead, to_back, decode_q, decode_k, decode_v, heads, group)

    rows_here = span_resid.shape[0]
    by_owner = attn.reshape(2, x_count, 2, rows_here, row_width)

    def rows_for(core_index):
        picked = lax.dynamic_index_in_dim(by_owner, core_index, 2, keepdims=False)
        turned = [
            lax.dynamic_index_in_dim(picked, (x + k) % x_count, 1, keepdims=False)
            for k in range(x_count)
        ]
        return turned

    ordered = jnp.stack(rows_for(1 - core) + rows_for(core))
    away, kept = project(ordered.reshape(-1, row_width), out_weight)
    arrived = lax.ppermute(away, "exp", other_core)
    chip_sum = (kept + arrived.astype(f32)).reshape(x_count, 2 * rows_here, model_width)
    total = chip_sum[x_count - 1]
    for k in range(x_count - 2, -1, -1):
        moved = lax.ppermute(total.astype(bf16), "exp", shift_x(1))
        total = chip_sum[k] + moved.astype(f32)
    resid = jnp.concatenate([span_resid, decode_resid]).astype(f32)
    stream = total + resid
    normed = (
        stream
        * lax.rsqrt(jnp.mean(stream * stream, -1, keepdims=True) + EPS)
        * norm_gain.astype(f32)
    ).astype(bf16)

    expert_ids = jnp.stack([span_expert[:, 0], decode_expert[:, 0]])
    expert_total = router.shape[1]
    logits = jnp.dot(normed, router, preferred_element_type=f32)
    flat_ids = expert_ids.reshape(-1)
    expert_iota = jnp.arange(expert_total, dtype=jnp.int32)
    picked = jnp.sum(jnp.where(flat_ids[:, None] == expert_iota, logits, 0.0), -1)
    routed_in = (normed.astype(f32) * jax.nn.sigmoid(picked)[:, None]).astype(bf16)
    capacity = 2 * tok_rows // (exp_count * exp_count)
    row_order = jnp.arange(rows_here, dtype=jnp.int32)
    same_expert = expert_ids[:, :, None] == expert_ids[:, None, :]
    slot = jnp.sum(same_expert & (row_order[None, :] < row_order[:, None])[None], 2)
    x_turn = (expert_ids // 2 - x + x_count) % x_count
    core_turn = (expert_ids % 2 + core) % 2
    column = (
        ((core_turn * x_count + x_turn) * 2 + jnp.arange(2, dtype=jnp.int32)[:, None]) * capacity
        + slot
    ).reshape(-1)
    core_slots = x_count * 2 * capacity
    onehot = (column[:, None] == jnp.arange(2 * core_slots, dtype=jnp.int32)[None, :]).astype(bf16)

    def slots(which):
        chosen = onehot[:, which * core_slots : (which + 1) * core_slots]
        filled = jnp.einsum("rc,rd->cd", chosen, routed_in, preferred_element_type=f32)
        return filled.astype(bf16).reshape(x_count, 1, 2 * capacity, model_width)

    swapped = lax.ppermute(slots(1), "exp", other_core)
    by_x = jnp.concatenate([slots(0), swapped], 1)

    near_block = by_x[0].reshape(-1, model_width)
    near_in = {1: (ahead(near_block), back(near_block))}
    later_block = jnp.concatenate(
        [
            lax.ppermute(by_x[k], "exp", shift_x(k)).reshape(-1, model_width)
            for k in range(1, x_count)
        ]
    )
    near_rows, later_rows = near_block.shape[0], later_block.shape[0]
    half_near, half_later = near_rows // 2, later_rows // 2
    later_in = {1: (ahead(later_block), back(later_block))}
    for step in range(2, half):
        near_in[step] = ahead(near_in[step - 1][0]), back(near_in[step - 1][1])
        if step < half - 1:
            later_in[step] = ahead(later_in[step - 1][0]), back(later_in[step - 1][1])

    def pair(arrived):
        return [arrived[1], arrived[0]]

    blocks = [near_block, later_block]
    for step in range(1, half - 1):
        blocks += pair(near_in[step])
    for step in range(1, half - 2):
        blocks += pair(later_in[step])
    first = expert_in(blocks, w_gate, w_up)
    sent = relay(
        near_in[near],
        [((0, 0, half_near),), ((1, half_near, near_rows),)],
        [first],
    )
    near_half = ahead(sent[0]), back(sent[1])
    later_in[near] = ahead(later_in[near - 1][0]), back(later_in[near - 1][1])
    second = expert_in(pair(near_in[near]) + pair(later_in[near - 1]), w_gate, w_up)
    sent = relay(
        later_in[near],
        [((0, 0, half_later),), ((1, half_later, later_rows),)],
        [second],
    )
    later_half = ahead(sent[0]), back(sent[1])
    last = expert_in([*later_half, *near_half, *pair(later_in[near])], w_gate, w_up)

    def add(a, b):
        return (a.astype(f32) + b.astype(f32)).astype(bf16)

    def cut(array, sizes):
        done, out = 0, []
        for size in sizes:
            out.append(array[done : done + size])
            done += size
        return out

    near_part, later_part = {}, {}
    out = expert_out(last, w_down)
    after = [out]
    out = cut(
        out,
        [half_later] * 2 + [half_near] * 2 + [later_rows] * 2,
    )
    later_part[half], near_part[half], later_part[near] = out[:2], out[2:4], out[4:]
    out = cut(expert_out(second, w_down, after), [near_rows] * 2 + [later_rows] * 2)
    near_part[near], later_part[near - 1] = out[:2], out[2:]
    sizes = [near_rows, later_rows] + [near_rows] * (2 * half - 4) + [later_rows] * (2 * half - 6)
    out = cut(expert_out(first, w_down, after), sizes)
    near_part[0], later_part[0] = out[0], out[1]
    for step in range(1, half - 1):
        near_part[step] = out[2 * step : 2 * step + 2]
    for step in range(1, half - 2):
        place_of = 2 * (half - 2) + 2 * step
        later_part[step] = out[place_of : place_of + 2]

    def home_step(part, moving, step):
        to_ahead, to_back = part[step]
        if step == near:
            size = moving[0].shape[0]
            to_ahead = jnp.concatenate([add(to_ahead[:size], moving[0]), to_ahead[size:]])
            to_back = jnp.concatenate([to_back[:size], add(to_back[size:], moving[1])])
        elif step < near:
            to_ahead, to_back = add(to_ahead, moving[0]), add(to_back, moving[1])
        return ahead(to_ahead), back(to_back)

    later_moving = near_moving = None
    for step in range(half, 0, -1):
        later_moving = home_step(later_part, later_moving, step)
        near_moving = home_step(near_part, near_moving, step)

    def total_of(own, moving):
        return (own.astype(f32) + moving[0].astype(f32) + moving[1].astype(f32)).astype(bf16)

    later_sum, near_sum = total_of(later_part[0], later_moving), total_of(near_part[0], near_moving)

    later_sum = later_sum.reshape(x_count - 1, 2, 2 * capacity, model_width)
    home = [
        lax.ppermute(later_sum[k - 1], "exp", shift_x(-k)) for k in range(1, x_count)
    ]
    home = jnp.stack([near_sum.reshape(2, 2 * capacity, model_width)] + home)
    swapped = lax.ppermute(home[:, 1], "exp", other_core)
    returned = jnp.stack([home[:, 0], swapped]).reshape(-1, model_width)
    routed = jnp.dot(onehot, returned, preferred_element_type=f32)
    result = (stream + routed).astype(bf16)
    return (result[:rows_here], result[rows_here:])


def solution(mesh):
    in_specs = (
        P("ctx", "exp"),
        P("ctx", "exp"),
        P("ctx", "exp"),
        P("ctx", "exp"),
        P("ctx", "exp"),
        P("ctx", "exp"),
        P("ctx", "exp"),
        P("ctx", "exp"),
        P(),
        P("exp", None),
        P(("ctx", "exp"), None),
        P(("ctx", "exp"), None),
        P(),
        P(),
        P(("ctx", "exp"), None),
        P(("ctx", "exp"), None),
        P("exp", None, "ctx"),
        P("exp", None, "ctx"),
        P("exp", "ctx", None),
    )
    out_specs = (P(("ctx", "exp"), None), P(("ctx", "exp"), None))
    return jax.shard_map(
        on_device, mesh=mesh, in_specs=in_specs, out_specs=out_specs, check_vma=False
    )
```

```python
import functools
import math

import jax
import jax.numpy as jnp
from jax import lax
from jax.experimental import pallas as pl
from jax.experimental.pallas import tpu as pltpu
from jax.sharding import PartitionSpec as P

HEADS = 40
KV_HEADS = 8
HEAD = 128

NEG = -1e30
EPS = 1e-05
SCALE = HEAD ** (-0.5)
EXP2_SCALE = SCALE * math.log2(math.e)
EXTRA = 128
PART = 32
CHUNK = 512
TILE = 512
VMEM_LIMIT = 48 * 1024 * 1024


def ring_order(count):
    if count % 8:
        return list(range(count))
    major, minor = 4, count // 4
    path = [(0, 0)]
    for b in range(minor):
        span = range(1, major) if b % 2 == 0 else range(major - 1, 0, -1)
        path += [(a, b) for a in span]
    path += [(0, b) for b in range(minor - 1, 0, -1)]
    return [a * minor + b for a, b in path]


def attend_kernel(info_ref, *refs, offsets, after, kv, group):
    owners = len(offsets)
    q_refs = refs[:owners]
    pos_ref, k_ref, v_ref, ks_ref, vs_ref = refs[owners : owners + 5]
    o_ref, q_scr, s_scr = refs[owners + 5 + after :]
    owner = pl.program_id(0)
    stream = pl.program_id(1)
    rows = q_scr.shape[0]
    pre = k_ref.shape[0]
    chunk = math.gcd(pre, CHUNK)
    stacked = rows * group
    span_keys = ks_ref.shape[0]
    contract = (((1,), (1,)), ((), ()))
    for i in range(owners):

        @pl.when(owner == i)
        def _(i=i):
            q_scr[...] = q_refs[i][0]

    def run(is_span):
        ctx = info_ref[info_ref.shape[0] - 1]
        if is_span:
            step = offsets[1] - offsets[0] if owners > 1 else 0
            from_here = (info_ref[offsets[0] + owner * step] - ctx) * rows
            lim = from_here + 1 + lax.broadcasted_iota(jnp.int32, (rows, 1), 0)
        else:
            lim = pos_ref[...] - ctx * pre
        lim = jnp.concatenate([lim] * group, axis=0)
        lane = lax.broadcasted_iota(jnp.int32, (rows, EXTRA), 1)
        packed = jnp.full((rows, EXTRA), NEG, jnp.float32)

        def scores(h):
            q = jnp.concatenate(
                [q_scr[:, (h * group + g) * HEAD : (h * group + g + 1) * HEAD] for g in range(group)],
                axis=0,
            )
            top = jnp.full((stacked, HEAD), NEG, jnp.float32)
            for j in range(pre // chunk):
                key = k_ref[j * chunk : (j + 1) * chunk, h * HEAD : (h + 1) * HEAD]
                s = lax.dot_general(q, key, contract, preferred_element_type=jnp.float32)
                if not is_span:
                    pos = j * chunk + lax.broadcasted_iota(jnp.int32, (stacked, chunk), 1)
                    s = jnp.where(pos < lim, s, NEG)
                s_scr[h, :, j * chunk : (j + 1) * chunk] = s
                for t in range(chunk // HEAD):
                    top = jnp.maximum(top, s[:, t * HEAD : (t + 1) * HEAD])
            m = jnp.max(top, axis=1, keepdims=True)
            s_own = None
            if is_span:
                key = ks_ref[:, h * HEAD : (h + 1) * HEAD]
                s_own = lax.dot_general(q, key, contract, preferred_element_type=jnp.float32)
                pos = lax.broadcasted_iota(jnp.int32, (stacked, span_keys), 1)
                s_own = jnp.where(pos < lim, s_own, NEG)
                m = jnp.maximum(m, jnp.max(s_own, axis=1, keepdims=True))
            return jnp.maximum(m, -1e29), s_own

        def values(h, m, s_own):
            acc = jnp.zeros((stacked, 2 * HEAD), jnp.float32)
            for j in range(pre // chunk):
                s = s_scr[h, :, j * chunk : (j + 1) * chunk]
                w = jnp.exp2(((s - m) * EXP2_SCALE).astype(jnp.bfloat16))
                val = v_ref[j * chunk : (j + 1) * chunk, h * HEAD : (h + 1) * HEAD]
                val = jnp.concatenate([val, jnp.ones_like(val)], axis=1)
                acc = acc + jnp.dot(w, val, preferred_element_type=jnp.float32)
            if is_span:
                w = jnp.exp2((s_own - m) * EXP2_SCALE).astype(jnp.bfloat16)
                val = vs_ref[:, h * HEAD : (h + 1) * HEAD]
                val = jnp.concatenate([val, jnp.ones_like(val)], axis=1)
                acc = acc + jnp.dot(w, val, preferred_element_type=jnp.float32)
            total = acc[:, HEAD:]
            seen = total > 0.0
            safe = jnp.where(seen, total, 1.0)
            out = (acc[:, :HEAD] / safe).astype(jnp.bfloat16)
            lse = jnp.where(seen, m * SCALE + jnp.log(safe), NEG)
            return out, lse

        state = scores(0)
        for h in range(kv):
            following = scores(h + 1) if h + 1 < kv else None
            out, lse = values(h, *state)
            for g in range(group):
                head = h * group + g
                o_ref[0, 0, :, head * HEAD : (head + 1) * HEAD] = out[g * rows : (g + 1) * rows]
                packed = jnp.where(lane % PART == head, lse[g * rows : (g + 1) * rows], packed)
            state = following
        o_ref[0, 0, :, kv * group * HEAD :] = pack_lse(packed, lane)

    @pl.when(stream == 0)
    def _():
        run(True)

    @pl.when(stream == 1)
    def _():
        run(False)


def pack_lse(value, lane):
    first = value.astype(jnp.bfloat16)
    rest = value - first.astype(jnp.float32)
    second = rest.astype(jnp.bfloat16)
    third = rest - second.astype(jnp.float32)
    picked = jnp.where(
        lane < PART,
        first.astype(jnp.float32),
        jnp.where(lane < 2 * PART, second.astype(jnp.float32), third),
    )
    return picked.astype(jnp.bfloat16)


def unpack_lse(extra):
    value = extra.astype(jnp.float32)
    return value[:, :PART] + value[:, PART : 2 * PART] + value[:, 2 * PART : 3 * PART]


def attend(queries, offsets, info, positions, caches, kv, group, after=()):
    owners = len(queries)
    _, rows, width = queries[0].shape
    pre = caches[0].shape[0]
    step = offsets[1] - offsets[0] if owners > 1 else 0
    whole = lambda a: pl.BlockSpec(a.shape, lambda o, s, info: (0,) * a.ndim)
    flops = 4 * owners * 2 * rows * group * kv * pre * HEAD
    return pl.pallas_call(
        functools.partial(
            attend_kernel, offsets=offsets, after=len(after), kv=kv, group=group
        ),
        out_shape=jax.ShapeDtypeStruct((owners, 2, rows, width + EXTRA), jnp.bfloat16),
        grid_spec=pltpu.PrefetchScalarGridSpec(
            num_scalar_prefetch=1,
            grid=(owners, 2),
            in_specs=[pl.BlockSpec((1, rows, width), lambda o, s, info: (s, 0, 0)) for _ in queries]
            + [pl.BlockSpec((rows, 1), lambda o, s, info: (info[offsets[0] + o * step], 0))]
            + [whole(a) for a in caches]
            + [pl.BlockSpec(memory_space=pl.ANY) for _ in after],
            out_specs=pl.BlockSpec(
                (1, 1, rows, width + EXTRA), lambda o, s, info: (o, s, 0, 0)
            ),
            scratch_shapes=[
                pltpu.VMEM((rows, width), jnp.bfloat16),
                pltpu.VMEM((kv, rows * group, pre), jnp.float32),
            ],
        ),
        compiler_params=pltpu.CompilerParams(vmem_limit_bytes=VMEM_LIMIT),
        cost_estimate=pl.CostEstimate(
            flops=2 * flops,
            bytes_accessed=4 * pre * kv * HEAD,
            transcendentals=owners * 2 * rows * group * kv * pre,
        ),
        name="attend",
    )(info, *queries, positions, *caches, *after)


def relay_kernel(*refs, plans, arrays, after):
    outs = refs[arrays + after :]
    for out, plan in zip(outs, plans):
        done = 0
        for index, start, stop in plan:
            out[done : done + stop - start] = refs[index][start:stop]
            done += stop - start


def relay(arrays, plans, after=()):
    rows = [sum(stop - start for _, start, stop in plan) for plan in plans]
    outs = [jax.ShapeDtypeStruct((r, *arrays[0].shape[1:]), arrays[0].dtype) for r in rows]
    return pl.pallas_call(
        functools.partial(relay_kernel, plans=plans, arrays=len(arrays), after=len(after)),
        out_shape=outs,
        in_specs=[pl.BlockSpec(memory_space=pltpu.VMEM)] * len(arrays)
        + [pl.BlockSpec(memory_space=pl.ANY)] * len(after),
        out_specs=[pl.BlockSpec(memory_space=pltpu.VMEM)] * len(outs),
        compiler_params=pltpu.CompilerParams(vmem_limit_bytes=VMEM_LIMIT),
        cost_estimate=pl.CostEstimate(
            flops=0, bytes_accessed=4 * sum(math.prod(o.shape) for o in outs), transcendentals=0
        ),
        name="relay",
    )(*arrays, *after)


def blend_kernel(base_ref, *refs, plans, arrived):
    for out, plan in zip(refs[arrived:], plans):
        done = 0
        for start, rows, adds in plan:
            value = base_ref[start : start + rows].astype(jnp.float32)
            for index, offset in adds:
                value = value + refs[index][offset : offset + rows].astype(jnp.float32)
            out[done : done + rows] = value.astype(jnp.bfloat16)
            done += rows


def blend(base, arrived, plans):
    outs = [
        jax.ShapeDtypeStruct((sum(part[1] for part in plan), base.shape[1]), base.dtype)
        for plan in plans
    ]
    return pl.pallas_call(
        functools.partial(blend_kernel, plans=plans, arrived=len(arrived)),
        out_shape=outs,
        in_specs=[pl.BlockSpec(memory_space=pltpu.VMEM)] * (1 + len(arrived)),
        out_specs=[pl.BlockSpec(memory_space=pltpu.VMEM)] * len(outs),
        compiler_params=pltpu.CompilerParams(vmem_limit_bytes=VMEM_LIMIT),
        cost_estimate=pl.CostEstimate(
            flops=0, bytes_accessed=6 * sum(math.prod(o.shape) for o in outs), transcendentals=0
        ),
        name="blend",
    )(base, *arrived)


def fetch(parts, axis):
    def copy(n, i):
        source, target, sems = parts[n]
        size = target.shape[1 + axis]
        tile = pl.ds(pl.multiple_of(i * size, size), size)
        view = source.at[tile] if axis == 0 else source.at[:, tile]
        return pltpu.make_async_copy(view, target.at[i], sems.at[i])

    def start(i, carry):
        for n in range(len(parts)):
            copy(n, i).start()
        return carry

    lax.fori_loop(0, parts[0][1].shape[0], start, 0)
    return lambda n, i: copy(n, i).wait()


def project_kernel(rows_ref, weight_ref, away_ref, kept_ref, tiles, sems):
    count, _, size = tiles.shape
    wait = fetch([(weight_ref, tiles, sems)], 1)
    half = away_ref.shape[0]

    def step(i, carry):
        wait(0, i)
        out = jnp.dot(rows_ref[...], tiles[i], preferred_element_type=jnp.float32)
        part = pl.ds(pl.multiple_of(i * size, size), size)
        away_ref[:, part] = out[:half].astype(jnp.bfloat16)
        kept_ref[:, part] = out[half:]
        return carry

    lax.fori_loop(0, count, step, 0)


def project(rows, weight):
    count, depth = rows.shape
    width = weight.shape[1]
    tile = math.gcd(width, TILE)
    return pl.pallas_call(
        project_kernel,
        out_shape=[
            jax.ShapeDtypeStruct((count // 2, width), jnp.bfloat16),
            jax.ShapeDtypeStruct((count // 2, width), jnp.float32),
        ],
        in_specs=[
            pl.BlockSpec(memory_space=pltpu.VMEM),
            pl.BlockSpec(memory_space=pltpu.HBM),
        ],
        out_specs=[pl.BlockSpec(memory_space=pltpu.VMEM)] * 2,
        scratch_shapes=[
            pltpu.VMEM((width // tile, depth, tile), jnp.bfloat16),
            pltpu.SemaphoreType.DMA((width // tile,)),
        ],
        compiler_params=pltpu.CompilerParams(vmem_limit_bytes=VMEM_LIMIT),
        cost_estimate=pl.CostEstimate(
            flops=2 * count * depth * width, bytes_accessed=2 * depth * width, transcendentals=0
        ),
        name="project",
    )(rows, weight)


def expert_in_kernel(*refs, blocks):
    gate_ref, up_ref, o_ref, rows_ref, gate, up, gate_acc, up_acc, gate_sems, up_sems = refs[blocks:]
    count, size, _ = gate.shape
    wait = fetch([(gate_ref.at[0], gate, gate_sems), (up_ref.at[0], up, up_sems)], 0)
    done = 0
    for block in refs[:blocks]:
        rows_ref[done : done + block.shape[0]] = block[...]
        done += block.shape[0]
    gate_acc[...] = jnp.zeros_like(gate_acc)
    up_acc[...] = jnp.zeros_like(up_acc)

    def step(i, carry):
        rows = rows_ref[:, pl.ds(pl.multiple_of(i * size, size), size)]
        wait(0, i)
        gate_acc[...] += jnp.dot(rows, gate[i], preferred_element_type=jnp.float32)
        wait(1, i)
        up_acc[...] += jnp.dot(rows, up[i], preferred_element_type=jnp.float32)
        return carry

    lax.fori_loop(0, count, step, 0)
    gate_h = gate_acc[...]
    hidden = gate_h / (1.0 + jnp.exp(-gate_h)) * up_acc[...]
    o_ref[...] = hidden.astype(jnp.bfloat16)


def expert_in(blocks, w_gate, w_up):
    depth, units = w_gate.shape[1:]
    if any(b.shape[0] % 16 for b in blocks):
        blocks = [jnp.concatenate(blocks)]
    rows = sum(b.shape[0] for b in blocks)
    tile = math.gcd(depth, TILE)
    return pl.pallas_call(
        functools.partial(expert_in_kernel, blocks=len(blocks)),
        out_shape=jax.ShapeDtypeStruct((rows, units), jnp.bfloat16),
        in_specs=[pl.BlockSpec(memory_space=pltpu.VMEM)] * len(blocks)
        + [pl.BlockSpec(memory_space=pltpu.HBM)] * 2,
        out_specs=pl.BlockSpec(memory_space=pltpu.VMEM),
        scratch_shapes=[pltpu.VMEM((rows, depth), jnp.bfloat16)]
        + [pltpu.VMEM((depth // tile, tile, units), jnp.bfloat16)] * 2
        + [pltpu.VMEM((rows, units), jnp.float32)] * 2
        + [pltpu.SemaphoreType.DMA((depth // tile,))] * 2,
        compiler_params=pltpu.CompilerParams(vmem_limit_bytes=VMEM_LIMIT),
        cost_estimate=pl.CostEstimate(
            flops=4 * rows * depth * units,
            bytes_accessed=4 * depth * units,
            transcendentals=rows * units,
        ),
        name="expert_in",
    )(*blocks, w_gate, w_up)


def expert_out_kernel(hidden_ref, down_ref, *refs):
    o_ref, down, sems = refs[-3:]
    count, _, size = down.shape
    wait = fetch([(down_ref.at[0], down, sems)], 1)

    def step(i, carry):
        wait(0, i)
        out = jnp.dot(hidden_ref[...], down[i], preferred_element_type=jnp.float32)
        o_ref[:, pl.ds(pl.multiple_of(i * size, size), size)] = out.astype(jnp.bfloat16)
        return carry

    lax.fori_loop(0, count, step, 0)


def expert_out(hidden, w_down, after=()):
    rows, units = hidden.shape
    width = w_down.shape[2]
    tile = math.gcd(width, TILE)
    return pl.pallas_call(
        expert_out_kernel,
        out_shape=jax.ShapeDtypeStruct((rows, width), jnp.bfloat16),
        in_specs=[
            pl.BlockSpec(memory_space=pltpu.VMEM),
            pl.BlockSpec(memory_space=pltpu.HBM),
        ]
        + [pl.BlockSpec(memory_space=pl.ANY)] * len(after),
        out_specs=pl.BlockSpec(memory_space=pltpu.VMEM),
        scratch_shapes=[
            pltpu.VMEM((width // tile, units, tile), jnp.bfloat16),
            pltpu.SemaphoreType.DMA((width // tile,)),
        ],
        compiler_params=pltpu.CompilerParams(vmem_limit_bytes=VMEM_LIMIT),
        cost_estimate=pl.CostEstimate(
            flops=2 * rows * units * width, bytes_accessed=2 * units * width, transcendentals=0
        ),
        name="expert_out",
    )(hidden, w_down, *after)


def merge(parts, heads):
    for head in range(heads):
        lses = [lse[:, head : head + 1] for _, lse in parts]
        top = functools.reduce(jnp.maximum, lses)
        weights = [jnp.exp(lse - top) for lse in lses]
        total = sum(weights)
        inverse = 1.0 / total
        out = 0.0
        for (value, _), weight in zip(parts, weights):
            out = out + value(head).astype(jnp.float32) * (weight * inverse)
        yield head, out, top + jnp.log(total)


def reader(ref):
    return lambda head: ref[:, head * HEAD : (head + 1) * HEAD]


def combine_kernel(part_ref, *refs, heads, present):
    rows = part_ref.shape[2]
    width = heads * HEAD
    recv_refs, outs = refs[: sum(present)], refs[sum(present) :]
    lane = lax.broadcasted_iota(jnp.int32, (rows, EXTRA), 1)
    taken = 0
    for way, there in enumerate(present):
        part, out_ref = part_ref.at[way, 0], outs[way]
        if not there:
            out_ref[...] = part[...]
            continue
        recv = recv_refs[taken]
        taken += 1
        parts = [(reader(ref), unpack_lse(ref[:, width:])) for ref in (recv, part)]
        packed = jnp.full((rows, EXTRA), NEG, jnp.float32)
        for head, out, lse in merge(parts, heads):
            out_ref[:, head * HEAD : (head + 1) * HEAD] = out.astype(jnp.bfloat16)
            packed = jnp.where(lane % PART == head, lse, packed)
        out_ref[:, width:] = pack_lse(packed, lane)


def combine(recvs, part, stream, heads):
    _, _, rows, width = part.shape
    there = [r for r in recvs if r is not None]
    return pl.pallas_call(
        functools.partial(
            combine_kernel, heads=heads, present=tuple(r is not None for r in recvs)
        ),
        out_shape=[jax.ShapeDtypeStruct((rows, width), jnp.bfloat16)] * 2,
        grid=(1,),
        in_specs=[pl.BlockSpec((2, 1, rows, width), lambda i: (0, stream, 0, 0))]
        + [pl.BlockSpec((rows, width), lambda i: (0, 0)) for _ in there],
        out_specs=[pl.BlockSpec((rows, width), lambda i: (0, 0))] * 2,
        compiler_params=pltpu.CompilerParams(vmem_limit_bytes=VMEM_LIMIT),
        cost_estimate=pl.CostEstimate(
            flops=16 * rows * width, bytes_accessed=12 * rows * width, transcendentals=0
        ),
        name="combine",
    )(part, *there)


def finish_kernel(own_ref, s_left, s_right, d_left, d_right, q_ref, k_ref, v_ref, o_ref, *, heads, group):
    width = heads * HEAD
    for stream, arrived in enumerate([(s_left, s_right), (d_left, d_right)]):
        refs = [own_ref.at[0, stream], *arrived]
        parts = [(reader(ref), unpack_lse(ref[:, width:])) for ref in refs]
        if stream == 1:
            scores = []
            for head in range(heads):
                kv = head // group
                q = q_ref[:, head * HEAD : (head + 1) * HEAD].astype(jnp.float32)
                k = k_ref[:, kv * HEAD : (kv + 1) * HEAD].astype(jnp.float32)
                scores.append(jnp.sum(q * k, axis=1, keepdims=True) * SCALE)
            own_value = lambda head: v_ref[:, (head // group) * HEAD : (head // group + 1) * HEAD]
            parts.append((own_value, jnp.concatenate(scores, axis=1)))
        for head, out, _ in merge(parts, heads):
            o_ref[stream, :, head * HEAD : (head + 1) * HEAD] = out.astype(jnp.bfloat16)


def finish(own, span_arrived, decode_arrived, decode_q, decode_k, decode_v, heads, group):
    _, _, rows, width = own.shape
    return pl.pallas_call(
        functools.partial(finish_kernel, heads=heads, group=group),
        out_shape=jax.ShapeDtypeStruct((2, rows, heads * HEAD), jnp.bfloat16),
        in_specs=[pl.BlockSpec(memory_space=pltpu.VMEM)] * 8,
        out_specs=pl.BlockSpec(memory_space=pltpu.VMEM),
        compiler_params=pltpu.CompilerParams(vmem_limit_bytes=VMEM_LIMIT),
        cost_estimate=pl.CostEstimate(
            flops=16 * rows * width, bytes_accessed=16 * rows * width, transcendentals=0
        ),
        name="finish",
    )(own, *span_arrived, *decode_arrived, decode_q, decode_k, decode_v)


def on_device(
    span_q,
    decode_q,
    k_cache,
    v_cache,
    span_k,
    span_v,
    decode_k,
    decode_v,
    decode_pos,
    out_weight,
    span_resid,
    decode_resid,
    norm_gain,
    router,
    span_expert,
    decode_expert,
    w_gate,
    w_up,
    w_down,
):
    f32, bf16 = jnp.float32, jnp.bfloat16
    tok_rows, row_width = span_q.shape
    pre_rows = k_cache.shape[0]
    kv = k_cache.shape[1] // HEAD
    group = HEADS // KV_HEADS
    heads = kv * group
    model_width = span_resid.shape[1]
    ctx_count, exp_count = lax.axis_size("ctx"), lax.axis_size("exp")
    ctx, exp = lax.axis_index("ctx"), lax.axis_index("exp")
    x_count = exp_count // 2
    x, core = exp // 2, exp % 2

    ring = ring_order(ctx_count)
    half = ctx_count // 2
    forward = [(ring[i], ring[(i + 1) % ctx_count]) for i in range(ctx_count)]
    backward = [(b, a) for a, b in forward]
    place = [0] * ctx_count
    for i, c in enumerate(ring):
        place[c] = i
    here = sum(jnp.where(ctx == c, i, 0) for c, i in enumerate(place) if i)
    spot = (here + jnp.arange(ctx_count + 1, dtype=jnp.int32)) % ctx_count
    owner = sum(jnp.where(spot == i, c, 0) for i, c in enumerate(ring) if c)
    info = jnp.where(jnp.arange(ctx_count + 1) == ctx_count, ctx, owner).astype(jnp.int32)
    positions = decode_pos[:, None]
    caches = (k_cache, v_cache, span_k, span_v)

    def ahead(value):
        return lax.ppermute(value, "ctx", forward)

    def back(value):
        return lax.ppermute(value, "ctx", backward)

    other_core = [(e, e ^ 1) for e in range(exp_count)]

    def shift_x(step):
        return [(e, ((e // 2 + step) % x_count) * 2 + e % 2) for e in range(exp_count)]

    def attend_for(queries, offsets, after=()):
        offsets = tuple(offset % ctx_count for offset in offsets)
        return attend(queries, offsets, info, positions, caches, kv, group, after)

    queries = jnp.stack([span_q, decode_q])
    both = [((0, 0, 2),), ((1, 0, 2),)]
    from_back, from_ahead = ahead(queries), back(queries)
    own_part = attend_for([queries], [0])
    from_back, from_ahead = relay([from_back, from_ahead], both, [own_part])
    parts = {}
    for step in range(1, half - 1):
        arrived = ahead(from_back), back(from_ahead)
        done = attend_for([from_ahead, from_back], [step, -step])
        plans = both if step < half - 2 else both + [((0, 0, 1),), ((1, 1, 2),)]
        from_back, from_ahead, *sent = relay(arrived, plans, [done])
        parts[step] = done
    arrived = ahead(sent[0]), back(sent[1])
    near = half - 1
    (far,) = relay(arrived, [((0, 0, 1), (1, 0, 1))], [done])
    far_part = attend_for([far], [half])
    parts[near] = attend_for([from_ahead, from_back], [near, -near])

    moving = [(ahead(far_part[0, 0]), None), (None, back(far_part[0, 1]))]
    for step in range(near, 0, -1):
        for stream in range(2):
            sent = combine(moving[stream], parts[step], stream, heads)
            moving[stream] = ahead(sent[0]), back(sent[1])
    attn = finish(own_part, *moving, decode_q, decode_k, decode_v, heads, group)

    rows_here = span_resid.shape[0]
    by_owner = attn.reshape(2, x_count, 2, rows_here, row_width)

    def rows_for(core_index):
        picked = lax.dynamic_index_in_dim(by_owner, core_index, 2, keepdims=False)
        turned = [
            lax.dynamic_index_in_dim(picked, (x + k) % x_count, 1, keepdims=False)
            for k in range(x_count)
        ]
        return turned

    ordered = jnp.stack(rows_for(1 - core) + rows_for(core))
    away, kept = project(ordered.reshape(-1, row_width), out_weight)
    arrived = lax.ppermute(away, "exp", other_core)
    chip_sum = (kept + arrived.astype(f32)).reshape(x_count, 2 * rows_here, model_width)
    total = chip_sum[x_count - 1]
    for k in range(x_count - 2, -1, -1):
        moved = lax.ppermute(total.astype(bf16), "exp", shift_x(1))
        total = chip_sum[k] + moved.astype(f32)
    resid = jnp.concatenate([span_resid, decode_resid]).astype(f32)
    stream = total + resid
    normed = (
        stream
        * lax.rsqrt(jnp.mean(stream * stream, -1, keepdims=True) + EPS)
        * norm_gain.astype(f32)
    ).astype(bf16)

    expert_ids = jnp.stack([span_expert[:, 0], decode_expert[:, 0]])
    expert_total = router.shape[1]
    logits = jnp.dot(normed, router, preferred_element_type=f32)
    flat_ids = expert_ids.reshape(-1)
    expert_iota = jnp.arange(expert_total, dtype=jnp.int32)
    picked = jnp.sum(jnp.where(flat_ids[:, None] == expert_iota, logits, 0.0), -1)
    routed_in = (normed.astype(f32) * jax.nn.sigmoid(picked)[:, None]).astype(bf16)
    capacity = 2 * tok_rows // (exp_count * exp_count)
    row_order = jnp.arange(rows_here, dtype=jnp.int32)
    same_expert = expert_ids[:, :, None] == expert_ids[:, None, :]
    slot = jnp.sum(same_expert & (row_order[None, :] < row_order[:, None])[None], 2)
    x_turn = (expert_ids // 2 - x + x_count) % x_count
    core_turn = (expert_ids % 2 + core) % 2
    column = (
        ((core_turn * x_count + x_turn) * 2 + jnp.arange(2, dtype=jnp.int32)[:, None]) * capacity
        + slot
    ).reshape(-1)
    core_slots = x_count * 2 * capacity
    onehot = (column[:, None] == jnp.arange(2 * core_slots, dtype=jnp.int32)[None, :]).astype(bf16)

    def slots(which):
        chosen = onehot[:, which * core_slots : (which + 1) * core_slots]
        filled = jnp.einsum("rc,rd->cd", chosen, routed_in, preferred_element_type=f32)
        return filled.astype(bf16).reshape(x_count, 1, 2 * capacity, model_width)

    swapped = lax.ppermute(slots(1), "exp", other_core)
    by_x = jnp.concatenate([slots(0), swapped], 1)

    near_block = by_x[0].reshape(-1, model_width)
    near_in = {1: (ahead(near_block), back(near_block))}
    later_block = jnp.concatenate(
        [
            lax.ppermute(by_x[k], "exp", shift_x(k)).reshape(-1, model_width)
            for k in range(1, x_count)
        ]
    )
    near_rows, later_rows = near_block.shape[0], later_block.shape[0]
    half_near, half_later = near_rows // 2, later_rows // 2
    later_in = {1: (ahead(later_block), back(later_block))}
    near_in[2] = ahead(near_in[1][0]), back(near_in[1][1])

    def pair(arrived):
        return [arrived[1], arrived[0]]

    hidden = {1: expert_in([near_block, later_block] + pair(near_in[1]), w_gate, w_up)}
    straight = [((0, 0, near_rows),), ((1, 0, near_rows),)]
    cut_near = [((0, 0, half_near),), ((1, half_near, near_rows),)]
    cut_later = [((0, 0, half_later),), ((1, half_later, later_rows),)]
    for step in range(2, half):
        sent = relay(near_in[step], straight if step < near else cut_near, [hidden[step - 1]])
        near_in[step + 1] = ahead(sent[0]), back(sent[1])
        sent = relay(later_in[step - 1], [((0, 0, later_rows),), ((1, 0, later_rows),)], [hidden[step - 1]])
        later_in[step] = ahead(sent[0]), back(sent[1])
        hidden[step] = expert_in(pair(near_in[step]) + pair(later_in[step - 1]), w_gate, w_up)
    sent = relay(later_in[near], cut_later, [hidden[near]])
    later_in[half] = ahead(sent[0]), back(sent[1])
    last = [*later_in[half], *near_in[half], *pair(later_in[near])]
    hidden[half] = expert_in(last, w_gate, w_up)

    near_spots = {half: (half, 2 * half_later, 2 * half_later + half_near)}
    later_spots = {half: (half, 0, half_later)}
    start = 2 * half_later + 2 * half_near
    later_spots[near] = (half, start, start + later_rows)
    for step in range(2, half):
        near_spots[step] = (step, 0, near_rows)
        start = 2 * near_rows
        later_spots[step - 1] = (step, start, start + later_rows)
    near_spots[1] = (1, near_rows + later_rows, 2 * near_rows + later_rows)
    outs = {half: expert_out(hidden[half], w_down)}
    outs[near] = expert_out(hidden[near], w_down, [outs[half]])

    def home_step(spots, rows, moving, step, offset):
        call, first, second = spots[step]
        half_rows = rows // 2
        if step == near:
            plans = [
                ((first, half_rows, ((0, offset),)), (first + half_rows, half_rows, ())),
                ((second, half_rows, ()), (second + half_rows, half_rows, ((1, offset),))),
            ]
        else:
            plans = [((first, rows, ((0, 0),)),), ((second, rows, ((1, 0),)),)]
        sent = blend(outs[call], moving, plans)
        return ahead(sent[0]), back(sent[1])

    plans = [
        tuple((spots[half][way], rows // 2, ()) for spots, rows in ((later_spots, later_rows), (near_spots, near_rows)))
        for way in (1, 2)
    ]
    sent = blend(outs[half], (), plans)
    later_moving = near_moving = ahead(sent[0]), back(sent[1])
    for step in range(near, 0, -1):
        later_moving = home_step(later_spots, later_rows, later_moving, step, 0)
        if step > 1:
            outs[step - 1] = expert_out(hidden[step - 1], w_down, [later_moving[0]])
        near_moving = home_step(near_spots, near_rows, near_moving, step, half_later)
    (later_sum,) = blend(outs[1], later_moving, [((near_rows, later_rows, ((0, 0), (1, 0))),)])
    (near_sum,) = blend(outs[1], near_moving, [((0, near_rows, ((0, 0), (1, 0))),)])

    later_sum = later_sum.reshape(x_count - 1, 2, 2 * capacity, model_width)
    home = [
        lax.ppermute(later_sum[k - 1], "exp", shift_x(-k)) for k in range(1, x_count)
    ]
    home = jnp.stack([near_sum.reshape(2, 2 * capacity, model_width)] + home)
    swapped = lax.ppermute(home[:, 1], "exp", other_core)
    returned = jnp.stack([home[:, 0], swapped]).reshape(-1, model_width)
    routed = jnp.dot(onehot, returned, preferred_element_type=f32)
    result = (stream + routed).astype(bf16)
    return (result[:rows_here], result[rows_here:])


def solution(mesh):
    in_specs = (
        P("ctx", "exp"),
        P("ctx", "exp"),
        P("ctx", "exp"),
        P("ctx", "exp"),
        P("ctx", "exp"),
        P("ctx", "exp"),
        P("ctx", "exp"),
        P("ctx", "exp"),
        P(),
        P("exp", None),
        P(("ctx", "exp"), None),
        P(("ctx", "exp"), None),
        P(),
        P(),
        P(("ctx", "exp"), None),
        P(("ctx", "exp"), None),
        P("exp", None, "ctx"),
        P("exp", None, "ctx"),
        P("exp", "ctx", None),
    )
    out_specs = (P(("ctx", "exp"), None), P(("ctx", "exp"), None))
    return jax.shard_map(
        on_device, mesh=mesh, in_specs=in_specs, out_specs=out_specs, check_vma=False
    )
```

```python
import functools
import math

import jax
import jax.numpy as jnp
from jax import lax
from jax.experimental import pallas as pl
from jax.experimental.pallas import tpu as pltpu
from jax.sharding import PartitionSpec as P

HEADS = 40
KV_HEADS = 8
HEAD = 128

NEG = -1e30
EPS = 1e-05
SCALE = HEAD ** (-0.5)
EXP2_SCALE = SCALE * math.log2(math.e)
EXTRA = 128
PART = 32
CHUNK = 1024
TILE = 512
VMEM_LIMIT = 48 * 1024 * 1024


def ring_order(count):
    if count % 8:
        return list(range(count))
    major, minor = 4, count // 4
    path = [(0, 0)]
    for b in range(minor):
        span = range(1, major) if b % 2 == 0 else range(major - 1, 0, -1)
        path += [(a, b) for a in span]
    path += [(0, b) for b in range(minor - 1, 0, -1)]
    return [a * minor + b for a, b in path]


def attend_kernel(info_ref, *refs, offsets, after, kv, group):
    owners = len(offsets)
    q_refs = refs[:owners]
    pos_ref, k_ref, v_ref, ks_ref, vs_ref = refs[owners : owners + 5]
    o_ref, q_scr = refs[owners + 5 + after :]
    owner = pl.program_id(0)
    stream = pl.program_id(1)
    rows = q_scr.shape[0]
    pre = k_ref.shape[0]
    chunk = math.gcd(pre, CHUNK)
    stacked = rows * group
    contract = (((1,), (1,)), ((), ()))
    for i in range(owners):

        @pl.when(owner == i)
        def _(i=i):
            q_scr[...] = q_refs[i][0]

    def run(is_span):
        ctx = info_ref[info_ref.shape[0] - 1]
        if is_span:
            step = offsets[1] - offsets[0] if owners > 1 else 0
            from_here = (info_ref[offsets[0] + owner * step] - ctx) * rows
            lim = from_here + 1 + lax.broadcasted_iota(jnp.int32, (rows, 1), 0)
        else:
            lim = pos_ref[...] - ctx * pre
        lim = jnp.concatenate([lim] * group, axis=0)
        lane = lax.broadcasted_iota(jnp.int32, (rows, EXTRA), 1)
        packed = jnp.full((rows, EXTRA), NEG, jnp.float32)

        queries = [
            jnp.concatenate(
                [q_scr[:, (h * group + g) * HEAD : (h * group + g + 1) * HEAD] for g in range(group)],
                axis=0,
            )
            for h in range(kv)
        ]

        def step(h, state, key, val, limit):
            m, acc = state
            key = key[:, h * HEAD : (h + 1) * HEAD]
            val = val[:, h * HEAD : (h + 1) * HEAD]
            s = lax.dot_general(queries[h], key, contract, preferred_element_type=jnp.float32)
            if limit is not None:
                pos = lax.broadcasted_iota(jnp.int32, s.shape, 1)
                s = jnp.where(pos < limit, s, NEG)
            top = jnp.maximum(m, jnp.max(s, axis=1, keepdims=True))
            w = jnp.exp2((s - top) * EXP2_SCALE).astype(jnp.bfloat16)
            val = jnp.concatenate([val, jnp.ones_like(val)], axis=1)
            add = jnp.dot(w, val, preferred_element_type=jnp.float32)
            if acc is not None:
                add = add + acc * jnp.exp2((m - top) * EXP2_SCALE)
            return top, add

        states = [(jnp.full((stacked, 1), -1e29, jnp.float32), None)] * kv
        if is_span:
            states = [step(h, states[h], ks_ref[...], vs_ref[...], lim) for h in range(kv)]
        for j in range(pre // chunk):
            here = slice(j * chunk, (j + 1) * chunk)
            limit = None if is_span else lim - j * chunk
            states = [
                step(h, states[h], k_ref.at[here], v_ref.at[here], limit) for h in range(kv)
            ]
        for h, (m, acc) in enumerate(states):
            total = acc[:, HEAD:]
            seen = total > 0.0
            safe = jnp.where(seen, total, 1.0)
            out = (acc[:, :HEAD] / safe).astype(jnp.bfloat16)
            lse = jnp.where(seen, m * SCALE + jnp.log(safe), NEG)
            for g in range(group):
                head = h * group + g
                o_ref[0, 0, :, head * HEAD : (head + 1) * HEAD] = out[g * rows : (g + 1) * rows]
                packed = jnp.where(lane % PART == head, lse[g * rows : (g + 1) * rows], packed)
        o_ref[0, 0, :, kv * group * HEAD :] = pack_lse(packed, lane)

    @pl.when(stream == 0)
    def _():
        run(True)

    @pl.when(stream == 1)
    def _():
        run(False)


def pack_lse(value, lane):
    first = value.astype(jnp.bfloat16)
    rest = value - first.astype(jnp.float32)
    second = rest.astype(jnp.bfloat16)
    third = rest - second.astype(jnp.float32)
    picked = jnp.where(
        lane < PART,
        first.astype(jnp.float32),
        jnp.where(lane < 2 * PART, second.astype(jnp.float32), third),
    )
    return picked.astype(jnp.bfloat16)


def unpack_lse(extra):
    value = extra.astype(jnp.float32)
    return value[:, :PART] + value[:, PART : 2 * PART] + value[:, 2 * PART : 3 * PART]


def attend(queries, offsets, info, positions, caches, kv, group, after=()):
    owners = len(queries)
    _, rows, width = queries[0].shape
    pre = caches[0].shape[0]
    step = offsets[1] - offsets[0] if owners > 1 else 0
    whole = lambda a: pl.BlockSpec(a.shape, lambda o, s, info: (0,) * a.ndim)
    flops = 4 * owners * 2 * rows * group * kv * pre * HEAD
    return pl.pallas_call(
        functools.partial(
            attend_kernel, offsets=offsets, after=len(after), kv=kv, group=group
        ),
        out_shape=jax.ShapeDtypeStruct((owners, 2, rows, width + EXTRA), jnp.bfloat16),
        grid_spec=pltpu.PrefetchScalarGridSpec(
            num_scalar_prefetch=1,
            grid=(owners, 2),
            in_specs=[pl.BlockSpec((1, rows, width), lambda o, s, info: (s, 0, 0)) for _ in queries]
            + [pl.BlockSpec((rows, 1), lambda o, s, info: (info[offsets[0] + o * step], 0))]
            + [whole(a) for a in caches]
            + [pl.BlockSpec(memory_space=pl.ANY) for _ in after],
            out_specs=pl.BlockSpec(
                (1, 1, rows, width + EXTRA), lambda o, s, info: (o, s, 0, 0)
            ),
            scratch_shapes=[
                pltpu.VMEM((rows, width), jnp.bfloat16),
            ],
        ),
        compiler_params=pltpu.CompilerParams(vmem_limit_bytes=VMEM_LIMIT),
        cost_estimate=pl.CostEstimate(
            flops=2 * flops,
            bytes_accessed=4 * pre * kv * HEAD,
            transcendentals=owners * 2 * rows * group * kv * pre,
        ),
        name="attend",
    )(info, *queries, positions, *caches, *after)


def relay_kernel(*refs, plans, arrays, after):
    outs = refs[arrays + after :]
    for out, plan in zip(outs, plans):
        done = 0
        for index, start, stop in plan:
            out[done : done + stop - start] = refs[index][start:stop]
            done += stop - start


def relay(arrays, plans, after=()):
    rows = [sum(stop - start for _, start, stop in plan) for plan in plans]
    outs = [jax.ShapeDtypeStruct((r, *arrays[0].shape[1:]), arrays[0].dtype) for r in rows]
    return pl.pallas_call(
        functools.partial(relay_kernel, plans=plans, arrays=len(arrays), after=len(after)),
        out_shape=outs,
        in_specs=[pl.BlockSpec(memory_space=pltpu.VMEM)] * len(arrays)
        + [pl.BlockSpec(memory_space=pl.ANY)] * len(after),
        out_specs=[pl.BlockSpec(memory_space=pltpu.VMEM)] * len(outs),
        compiler_params=pltpu.CompilerParams(vmem_limit_bytes=VMEM_LIMIT),
        cost_estimate=pl.CostEstimate(
            flops=0, bytes_accessed=4 * sum(math.prod(o.shape) for o in outs), transcendentals=0
        ),
        name="relay",
    )(*arrays, *after)


def blend_kernel(base_ref, *refs, plans, arrived):
    for out, plan in zip(refs[arrived:], plans):
        done = 0
        for start, rows, adds in plan:
            value = base_ref[start : start + rows].astype(jnp.float32)
            for index, offset in adds:
                value = value + refs[index][offset : offset + rows].astype(jnp.float32)
            out[done : done + rows] = value.astype(jnp.bfloat16)
            done += rows


def blend(base, arrived, plans):
    outs = [
        jax.ShapeDtypeStruct((sum(part[1] for part in plan), base.shape[1]), base.dtype)
        for plan in plans
    ]
    return pl.pallas_call(
        functools.partial(blend_kernel, plans=plans, arrived=len(arrived)),
        out_shape=outs,
        in_specs=[pl.BlockSpec(memory_space=pltpu.VMEM)] * (1 + len(arrived)),
        out_specs=[pl.BlockSpec(memory_space=pltpu.VMEM)] * len(outs),
        compiler_params=pltpu.CompilerParams(vmem_limit_bytes=VMEM_LIMIT),
        cost_estimate=pl.CostEstimate(
            flops=0, bytes_accessed=6 * sum(math.prod(o.shape) for o in outs), transcendentals=0
        ),
        name="blend",
    )(base, *arrived)


def fetch(parts, axis):
    def copy(n, i):
        source, target, sems = parts[n]
        size = target.shape[1 + axis]
        tile = pl.ds(pl.multiple_of(i * size, size), size)
        view = source.at[tile] if axis == 0 else source.at[:, tile]
        return pltpu.make_async_copy(view, target.at[i], sems.at[i])

    def start(i, carry):
        for n in range(len(parts)):
            copy(n, i).start()
        return carry

    lax.fori_loop(0, parts[0][1].shape[0], start, 0)
    return lambda n, i: copy(n, i).wait()


def project_kernel(rows_ref, weight_ref, away_ref, kept_ref, tiles, sems):
    count, _, size = tiles.shape
    wait = fetch([(weight_ref, tiles, sems)], 1)
    half = away_ref.shape[0]

    def step(i, carry):
        wait(0, i)
        out = jnp.dot(rows_ref[...], tiles[i], preferred_element_type=jnp.float32)
        part = pl.ds(pl.multiple_of(i * size, size), size)
        away_ref[:, part] = out[:half].astype(jnp.bfloat16)
        kept_ref[:, part] = out[half:]
        return carry

    lax.fori_loop(0, count, step, 0)


def project(rows, weight):
    count, depth = rows.shape
    width = weight.shape[1]
    tile = math.gcd(width, TILE)
    return pl.pallas_call(
        project_kernel,
        out_shape=[
            jax.ShapeDtypeStruct((count // 2, width), jnp.bfloat16),
            jax.ShapeDtypeStruct((count // 2, width), jnp.float32),
        ],
        in_specs=[
            pl.BlockSpec(memory_space=pltpu.VMEM),
            pl.BlockSpec(memory_space=pltpu.HBM),
        ],
        out_specs=[pl.BlockSpec(memory_space=pltpu.VMEM)] * 2,
        scratch_shapes=[
            pltpu.VMEM((width // tile, depth, tile), jnp.bfloat16),
            pltpu.SemaphoreType.DMA((width // tile,)),
        ],
        compiler_params=pltpu.CompilerParams(vmem_limit_bytes=VMEM_LIMIT),
        cost_estimate=pl.CostEstimate(
            flops=2 * count * depth * width, bytes_accessed=2 * depth * width, transcendentals=0
        ),
        name="project",
    )(rows, weight)


def expert_in_kernel(*refs, blocks):
    gate_ref, up_ref, o_ref, rows_ref, gate, up, gate_acc, up_acc, gate_sems, up_sems = refs[blocks:]
    count, size, _ = gate.shape
    wait = fetch([(gate_ref.at[0], gate, gate_sems), (up_ref.at[0], up, up_sems)], 0)
    done = 0
    for block in refs[:blocks]:
        rows_ref[done : done + block.shape[0]] = block[...]
        done += block.shape[0]
    gate_acc[...] = jnp.zeros_like(gate_acc)
    up_acc[...] = jnp.zeros_like(up_acc)

    def step(i, carry):
        rows = rows_ref[:, pl.ds(pl.multiple_of(i * size, size), size)]
        wait(0, i)
        gate_acc[...] += jnp.dot(rows, gate[i], preferred_element_type=jnp.float32)
        wait(1, i)
        up_acc[...] += jnp.dot(rows, up[i], preferred_element_type=jnp.float32)
        return carry

    lax.fori_loop(0, count, step, 0)
    gate_h = gate_acc[...]
    hidden = gate_h / (1.0 + jnp.exp(-gate_h)) * up_acc[...]
    o_ref[...] = hidden.astype(jnp.bfloat16)


def expert_in(blocks, w_gate, w_up):
    depth, units = w_gate.shape[1:]
    if any(b.shape[0] % 16 for b in blocks):
        blocks = [jnp.concatenate(blocks)]
    rows = sum(b.shape[0] for b in blocks)
    tile = math.gcd(depth, TILE)
    return pl.pallas_call(
        functools.partial(expert_in_kernel, blocks=len(blocks)),
        out_shape=jax.ShapeDtypeStruct((rows, units), jnp.bfloat16),
        in_specs=[pl.BlockSpec(memory_space=pltpu.VMEM)] * len(blocks)
        + [pl.BlockSpec(memory_space=pltpu.HBM)] * 2,
        out_specs=pl.BlockSpec(memory_space=pltpu.VMEM),
        scratch_shapes=[pltpu.VMEM((rows, depth), jnp.bfloat16)]
        + [pltpu.VMEM((depth // tile, tile, units), jnp.bfloat16)] * 2
        + [pltpu.VMEM((rows, units), jnp.float32)] * 2
        + [pltpu.SemaphoreType.DMA((depth // tile,))] * 2,
        compiler_params=pltpu.CompilerParams(vmem_limit_bytes=VMEM_LIMIT),
        cost_estimate=pl.CostEstimate(
            flops=4 * rows * depth * units,
            bytes_accessed=4 * depth * units,
            transcendentals=rows * units,
        ),
        name="expert_in",
    )(*blocks, w_gate, w_up)


def expert_out_kernel(hidden_ref, down_ref, *refs):
    o_ref, down, sems = refs[-3:]
    count, _, size = down.shape
    wait = fetch([(down_ref.at[0], down, sems)], 1)

    def step(i, carry):
        wait(0, i)
        out = jnp.dot(hidden_ref[...], down[i], preferred_element_type=jnp.float32)
        o_ref[:, pl.ds(pl.multiple_of(i * size, size), size)] = out.astype(jnp.bfloat16)
        return carry

    lax.fori_loop(0, count, step, 0)


def expert_out(hidden, w_down, after=()):
    rows, units = hidden.shape
    width = w_down.shape[2]
    tile = math.gcd(width, TILE)
    return pl.pallas_call(
        expert_out_kernel,
        out_shape=jax.ShapeDtypeStruct((rows, width), jnp.bfloat16),
        in_specs=[
            pl.BlockSpec(memory_space=pltpu.VMEM),
            pl.BlockSpec(memory_space=pltpu.HBM),
        ]
        + [pl.BlockSpec(memory_space=pl.ANY)] * len(after),
        out_specs=pl.BlockSpec(memory_space=pltpu.VMEM),
        scratch_shapes=[
            pltpu.VMEM((width // tile, units, tile), jnp.bfloat16),
            pltpu.SemaphoreType.DMA((width // tile,)),
        ],
        compiler_params=pltpu.CompilerParams(vmem_limit_bytes=VMEM_LIMIT),
        cost_estimate=pl.CostEstimate(
            flops=2 * rows * units * width, bytes_accessed=2 * units * width, transcendentals=0
        ),
        name="expert_out",
    )(hidden, w_down, *after)


def merge(parts, heads):
    for head in range(heads):
        lses = [lse[:, head : head + 1] for _, lse in parts]
        top = functools.reduce(jnp.maximum, lses)
        weights = [jnp.exp(lse - top) for lse in lses]
        total = sum(weights)
        inverse = 1.0 / total
        out = 0.0
        for (value, _), weight in zip(parts, weights):
            out = out + value(head).astype(jnp.float32) * (weight * inverse)
        yield head, out, top + jnp.log(total)


def reader(ref):
    return lambda head: ref[:, head * HEAD : (head + 1) * HEAD]


def combine_kernel(part_ref, *refs, heads, present):
    rows = part_ref.shape[2]
    width = heads * HEAD
    recv_refs, outs = refs[: sum(present)], refs[sum(present) :]
    lane = lax.broadcasted_iota(jnp.int32, (rows, EXTRA), 1)
    taken = 0
    for way, there in enumerate(present):
        part, out_ref = part_ref.at[way, 0], outs[way]
        if not there:
            out_ref[...] = part[...]
            continue
        recv = recv_refs[taken]
        taken += 1
        parts = [(reader(ref), unpack_lse(ref[:, width:])) for ref in (recv, part)]
        packed = jnp.full((rows, EXTRA), NEG, jnp.float32)
        for head, out, lse in merge(parts, heads):
            out_ref[:, head * HEAD : (head + 1) * HEAD] = out.astype(jnp.bfloat16)
            packed = jnp.where(lane % PART == head, lse, packed)
        out_ref[:, width:] = pack_lse(packed, lane)


def combine(recvs, part, stream, heads):
    _, _, rows, width = part.shape
    there = [r for r in recvs if r is not None]
    return pl.pallas_call(
        functools.partial(
            combine_kernel, heads=heads, present=tuple(r is not None for r in recvs)
        ),
        out_shape=[jax.ShapeDtypeStruct((rows, width), jnp.bfloat16)] * 2,
        grid=(1,),
        in_specs=[pl.BlockSpec((2, 1, rows, width), lambda i: (0, stream, 0, 0))]
        + [pl.BlockSpec((rows, width), lambda i: (0, 0)) for _ in there],
        out_specs=[pl.BlockSpec((rows, width), lambda i: (0, 0))] * 2,
        compiler_params=pltpu.CompilerParams(vmem_limit_bytes=VMEM_LIMIT),
        cost_estimate=pl.CostEstimate(
            flops=16 * rows * width, bytes_accessed=12 * rows * width, transcendentals=0
        ),
        name="combine",
    )(part, *there)


def finish_kernel(own_ref, s_left, s_right, d_left, d_right, q_ref, k_ref, v_ref, o_ref, *, heads, group):
    width = heads * HEAD
    for stream, arrived in enumerate([(s_left, s_right), (d_left, d_right)]):
        refs = [own_ref.at[0, stream], *arrived]
        parts = [(reader(ref), unpack_lse(ref[:, width:])) for ref in refs]
        if stream == 1:
            scores = []
            for head in range(heads):
                kv = head // group
                q = q_ref[:, head * HEAD : (head + 1) * HEAD].astype(jnp.float32)
                k = k_ref[:, kv * HEAD : (kv + 1) * HEAD].astype(jnp.float32)
                scores.append(jnp.sum(q * k, axis=1, keepdims=True) * SCALE)
            own_value = lambda head: v_ref[:, (head // group) * HEAD : (head // group + 1) * HEAD]
            parts.append((own_value, jnp.concatenate(scores, axis=1)))
        for head, out, _ in merge(parts, heads):
            o_ref[stream, :, head * HEAD : (head + 1) * HEAD] = out.astype(jnp.bfloat16)


def finish(own, span_arrived, decode_arrived, decode_q, decode_k, decode_v, heads, group):
    _, _, rows, width = own.shape
    return pl.pallas_call(
        functools.partial(finish_kernel, heads=heads, group=group),
        out_shape=jax.ShapeDtypeStruct((2, rows, heads * HEAD), jnp.bfloat16),
        in_specs=[pl.BlockSpec(memory_space=pltpu.VMEM)] * 8,
        out_specs=pl.BlockSpec(memory_space=pltpu.VMEM),
        compiler_params=pltpu.CompilerParams(vmem_limit_bytes=VMEM_LIMIT),
        cost_estimate=pl.CostEstimate(
            flops=16 * rows * width, bytes_accessed=16 * rows * width, transcendentals=0
        ),
        name="finish",
    )(own, *span_arrived, *decode_arrived, decode_q, decode_k, decode_v)


def on_device(
    span_q,
    decode_q,
    k_cache,
    v_cache,
    span_k,
    span_v,
    decode_k,
    decode_v,
    decode_pos,
    out_weight,
    span_resid,
    decode_resid,
    norm_gain,
    router,
    span_expert,
    decode_expert,
    w_gate,
    w_up,
    w_down,
):
    f32, bf16 = jnp.float32, jnp.bfloat16
    tok_rows, row_width = span_q.shape
    pre_rows = k_cache.shape[0]
    kv = k_cache.shape[1] // HEAD
    group = HEADS // KV_HEADS
    heads = kv * group
    model_width = span_resid.shape[1]
    ctx_count, exp_count = lax.axis_size("ctx"), lax.axis_size("exp")
    ctx, exp = lax.axis_index("ctx"), lax.axis_index("exp")
    x_count = exp_count // 2
    x, core = exp // 2, exp % 2

    ring = ring_order(ctx_count)
    half = ctx_count // 2
    forward = [(ring[i], ring[(i + 1) % ctx_count]) for i in range(ctx_count)]
    backward = [(b, a) for a, b in forward]
    place = [0] * ctx_count
    for i, c in enumerate(ring):
        place[c] = i
    here = sum(jnp.where(ctx == c, i, 0) for c, i in enumerate(place) if i)
    spot = (here + jnp.arange(ctx_count + 1, dtype=jnp.int32)) % ctx_count
    owner = sum(jnp.where(spot == i, c, 0) for i, c in enumerate(ring) if c)
    info = jnp.where(jnp.arange(ctx_count + 1) == ctx_count, ctx, owner).astype(jnp.int32)
    positions = decode_pos[:, None]
    caches = (k_cache, v_cache, span_k, span_v)

    def ahead(value):
        return lax.ppermute(value, "ctx", forward)

    def back(value):
        return lax.ppermute(value, "ctx", backward)

    other_core = [(e, e ^ 1) for e in range(exp_count)]

    def shift_x(step):
        return [(e, ((e // 2 + step) % x_count) * 2 + e % 2) for e in range(exp_count)]

    def attend_for(queries, offsets, after=()):
        offsets = tuple(offset % ctx_count for offset in offsets)
        return attend(queries, offsets, info, positions, caches, kv, group, after)

    queries = jnp.stack([span_q, decode_q])
    both = [((0, 0, 2),), ((1, 0, 2),)]
    from_back, from_ahead = ahead(queries), back(queries)
    own_part = attend_for([queries], [0])
    from_back, from_ahead = relay([from_back, from_ahead], both, [own_part])
    parts = {}
    for step in range(1, half - 1):
        arrived = ahead(from_back), back(from_ahead)
        done = attend_for([from_ahead, from_back], [step, -step])
        plans = both if step < half - 2 else both + [((0, 0, 1),), ((1, 1, 2),)]
        from_back, from_ahead, *sent = relay(arrived, plans, [done])
        parts[step] = done
    arrived = ahead(sent[0]), back(sent[1])
    near = half - 1
    (far,) = relay(arrived, [((0, 0, 1), (1, 0, 1))], [done])
    far_part = attend_for([far], [half])
    parts[near] = attend_for([from_ahead, from_back], [near, -near])

    moving = [(ahead(far_part[0, 0]), None), (None, back(far_part[0, 1]))]
    for step in range(near, 0, -1):
        for stream in range(2):
            sent = combine(moving[stream], parts[step], stream, heads)
            moving[stream] = ahead(sent[0]), back(sent[1])
    attn = finish(own_part, *moving, decode_q, decode_k, decode_v, heads, group)

    rows_here = span_resid.shape[0]
    by_owner = attn.reshape(2, x_count, 2, rows_here, row_width)

    def rows_for(core_index):
        picked = lax.dynamic_index_in_dim(by_owner, core_index, 2, keepdims=False)
        turned = [
            lax.dynamic_index_in_dim(picked, (x + k) % x_count, 1, keepdims=False)
            for k in range(x_count)
        ]
        return turned

    ordered = jnp.stack(rows_for(1 - core) + rows_for(core))
    away, kept = project(ordered.reshape(-1, row_width), out_weight)
    arrived = lax.ppermute(away, "exp", other_core)
    chip_sum = (kept + arrived.astype(f32)).reshape(x_count, 2 * rows_here, model_width)
    total = chip_sum[x_count - 1]
    for k in range(x_count - 2, -1, -1):
        moved = lax.ppermute(total.astype(bf16), "exp", shift_x(1))
        total = chip_sum[k] + moved.astype(f32)
    resid = jnp.concatenate([span_resid, decode_resid]).astype(f32)
    stream = total + resid
    normed = (
        stream
        * lax.rsqrt(jnp.mean(stream * stream, -1, keepdims=True) + EPS)
        * norm_gain.astype(f32)
    ).astype(bf16)

    expert_ids = jnp.stack([span_expert[:, 0], decode_expert[:, 0]])
    expert_total = router.shape[1]
    logits = jnp.dot(normed, router, preferred_element_type=f32)
    flat_ids = expert_ids.reshape(-1)
    expert_iota = jnp.arange(expert_total, dtype=jnp.int32)
    picked = jnp.sum(jnp.where(flat_ids[:, None] == expert_iota, logits, 0.0), -1)
    routed_in = (normed.astype(f32) * jax.nn.sigmoid(picked)[:, None]).astype(bf16)
    capacity = 2 * tok_rows // (exp_count * exp_count)
    row_order = jnp.arange(rows_here, dtype=jnp.int32)
    same_expert = expert_ids[:, :, None] == expert_ids[:, None, :]
    slot = jnp.sum(same_expert & (row_order[None, :] < row_order[:, None])[None], 2)
    x_turn = (expert_ids // 2 - x + x_count) % x_count
    core_turn = (expert_ids % 2 + core) % 2
    column = (
        ((core_turn * x_count + x_turn) * 2 + jnp.arange(2, dtype=jnp.int32)[:, None]) * capacity
        + slot
    ).reshape(-1)
    core_slots = x_count * 2 * capacity
    onehot = (column[:, None] == jnp.arange(2 * core_slots, dtype=jnp.int32)[None, :]).astype(bf16)

    def slots(which):
        chosen = onehot[:, which * core_slots : (which + 1) * core_slots]
        filled = jnp.einsum("rc,rd->cd", chosen, routed_in, preferred_element_type=f32)
        return filled.astype(bf16).reshape(x_count, 1, 2 * capacity, model_width)

    swapped = lax.ppermute(slots(1), "exp", other_core)
    by_x = jnp.concatenate([slots(0), swapped], 1)

    near_block = by_x[0].reshape(-1, model_width)
    near_in = {1: (ahead(near_block), back(near_block))}
    later_block = jnp.concatenate(
        [
            lax.ppermute(by_x[k], "exp", shift_x(k)).reshape(-1, model_width)
            for k in range(1, x_count)
        ]
    )
    near_rows, later_rows = near_block.shape[0], later_block.shape[0]
    half_near, half_later = near_rows // 2, later_rows // 2
    later_in = {1: (ahead(later_block), back(later_block))}
    near_in[2] = ahead(near_in[1][0]), back(near_in[1][1])

    def pair(arrived):
        return [arrived[1], arrived[0]]

    hidden = {1: expert_in([near_block, later_block] + pair(near_in[1]), w_gate, w_up)}
    straight = [((0, 0, near_rows),), ((1, 0, near_rows),)]
    cut_near = [((0, 0, half_near),), ((1, half_near, near_rows),)]
    cut_later = [((0, 0, half_later),), ((1, half_later, later_rows),)]
    for step in range(2, half):
        sent = relay(near_in[step], straight if step < near else cut_near, [hidden[step - 1]])
        near_in[step + 1] = ahead(sent[0]), back(sent[1])
        sent = relay(later_in[step - 1], [((0, 0, later_rows),), ((1, 0, later_rows),)], [hidden[step - 1]])
        later_in[step] = ahead(sent[0]), back(sent[1])
        hidden[step] = expert_in(pair(near_in[step]) + pair(later_in[step - 1]), w_gate, w_up)
    sent = relay(later_in[near], cut_later, [hidden[near]])
    later_in[half] = ahead(sent[0]), back(sent[1])
    last = [*later_in[half], *near_in[half], *pair(later_in[near])]
    hidden[half] = expert_in(last, w_gate, w_up)

    near_spots = {half: (half, 2 * half_later, 2 * half_later + half_near)}
    later_spots = {half: (half, 0, half_later)}
    start = 2 * half_later + 2 * half_near
    later_spots[near] = (half, start, start + later_rows)
    for step in range(2, half):
        near_spots[step] = (step, 0, near_rows)
        start = 2 * near_rows
        later_spots[step - 1] = (step, start, start + later_rows)
    near_spots[1] = (1, near_rows + later_rows, 2 * near_rows + later_rows)
    outs = {half: expert_out(hidden[half], w_down)}
    outs[near] = expert_out(hidden[near], w_down, [outs[half]])

    def home_step(spots, rows, moving, step, offset):
        call, first, second = spots[step]
        half_rows = rows // 2
        if step == near:
            plans = [
                ((first, half_rows, ((0, offset),)), (first + half_rows, half_rows, ())),
                ((second, half_rows, ()), (second + half_rows, half_rows, ((1, offset),))),
            ]
        else:
            plans = [((first, rows, ((0, 0),)),), ((second, rows, ((1, 0),)),)]
        sent = blend(outs[call], moving, plans)
        return ahead(sent[0]), back(sent[1])

    plans = [
        tuple((spots[half][way], rows // 2, ()) for spots, rows in ((later_spots, later_rows), (near_spots, near_rows)))
        for way in (1, 2)
    ]
    sent = blend(outs[half], (), plans)
    later_moving = near_moving = ahead(sent[0]), back(sent[1])
    for step in range(near, 0, -1):
        later_moving = home_step(later_spots, later_rows, later_moving, step, 0)
        if step > 1:
            outs[step - 1] = expert_out(hidden[step - 1], w_down, [later_moving[0]])
        near_moving = home_step(near_spots, near_rows, near_moving, step, half_later)
    (later_sum,) = blend(outs[1], later_moving, [((near_rows, later_rows, ((0, 0), (1, 0))),)])
    (near_sum,) = blend(outs[1], near_moving, [((0, near_rows, ((0, 0), (1, 0))),)])

    later_sum = later_sum.reshape(x_count - 1, 2, 2 * capacity, model_width)
    home = [
        lax.ppermute(later_sum[k - 1], "exp", shift_x(-k)) for k in range(1, x_count)
    ]
    home = jnp.stack([near_sum.reshape(2, 2 * capacity, model_width)] + home)
    swapped = lax.ppermute(home[:, 1], "exp", other_core)
    returned = jnp.stack([home[:, 0], swapped]).reshape(-1, model_width)
    routed = jnp.dot(onehot, returned, preferred_element_type=f32)
    result = (stream + routed).astype(bf16)
    return (result[:rows_here], result[rows_here:])


def solution(mesh):
    in_specs = (
        P("ctx", "exp"),
        P("ctx", "exp"),
        P("ctx", "exp"),
        P("ctx", "exp"),
        P("ctx", "exp"),
        P("ctx", "exp"),
        P("ctx", "exp"),
        P("ctx", "exp"),
        P(),
        P("exp", None),
        P(("ctx", "exp"), None),
        P(("ctx", "exp"), None),
        P(),
        P(),
        P(("ctx", "exp"), None),
        P(("ctx", "exp"), None),
        P("exp", None, "ctx"),
        P("exp", None, "ctx"),
        P("exp", "ctx", None),
    )
    out_specs = (P(("ctx", "exp"), None), P(("ctx", "exp"), None))
    return jax.shard_map(
        on_device, mesh=mesh, in_specs=in_specs, out_specs=out_specs, check_vma=False
    )
```

```python
import functools
import math

import jax
import jax.numpy as jnp
from jax import lax
from jax.experimental import pallas as pl
from jax.experimental.pallas import tpu as pltpu
from jax.sharding import PartitionSpec as P

HEADS = 40
KV_HEADS = 8
HEAD = 128

NEG = -1e30
EPS = 1e-05
SCALE = HEAD ** (-0.5)
EXP2_SCALE = SCALE * math.log2(math.e)
EXTRA = 128
PART = 32
KEY_CHUNK = 256
VALUE_CHUNK = 1024
TILE = 512
VMEM_LIMIT = 48 * 1024 * 1024


def ring_order(count):
    if count % 8:
        return list(range(count))
    major, minor = 4, count // 4
    path = [(0, 0)]
    for b in range(minor):
        span = range(1, major) if b % 2 == 0 else range(major - 1, 0, -1)
        path += [(a, b) for a in span]
    path += [(0, b) for b in range(minor - 1, 0, -1)]
    return [a * minor + b for a, b in path]


def attend_kernel(info_ref, *refs, offsets, after, kv, group):
    owners = len(offsets)
    q_refs = refs[:owners]
    pos_ref, k_ref, v_ref, ks_ref, vs_ref = refs[owners : owners + 5]
    o_ref, q_scr, s_scr = refs[owners + 5 + after :]
    owner = pl.program_id(0)
    stream = pl.program_id(1)
    rows = q_scr.shape[0]
    pre = k_ref.shape[0]
    key_chunk, value_chunk = math.gcd(pre, KEY_CHUNK), math.gcd(pre, VALUE_CHUNK)
    stacked = rows * group
    span_keys = ks_ref.shape[0]
    contract = (((1,), (1,)), ((), ()))
    for i in range(owners):

        @pl.when(owner == i)
        def _(i=i):
            q_scr[...] = q_refs[i][0]

    def run(is_span):
        ctx = info_ref[info_ref.shape[0] - 1]
        if is_span:
            step = offsets[1] - offsets[0] if owners > 1 else 0
            from_here = (info_ref[offsets[0] + owner * step] - ctx) * rows
            lim = from_here + 1 + lax.broadcasted_iota(jnp.int32, (rows, 1), 0)
        else:
            lim = pos_ref[...] - ctx * pre
        lim = jnp.concatenate([lim] * group, axis=0)
        lane = lax.broadcasted_iota(jnp.int32, (rows, EXTRA), 1)
        packed = jnp.full((rows, EXTRA), NEG, jnp.float32)

        def scores(h):
            q = jnp.concatenate(
                [q_scr[:, (h * group + g) * HEAD : (h * group + g + 1) * HEAD] for g in range(group)],
                axis=0,
            )
            top = jnp.full((stacked, HEAD), NEG, jnp.float32)
            for j in range(pre // key_chunk):
                key = k_ref[j * key_chunk : (j + 1) * key_chunk, h * HEAD : (h + 1) * HEAD]
                s = lax.dot_general(q, key, contract, preferred_element_type=jnp.float32)
                if not is_span:
                    pos = j * key_chunk + lax.broadcasted_iota(jnp.int32, (stacked, key_chunk), 1)
                    s = jnp.where(pos < lim, s, NEG)
                s_scr[h, :, j * key_chunk : (j + 1) * key_chunk] = s
                for t in range(key_chunk // HEAD):
                    top = jnp.maximum(top, s[:, t * HEAD : (t + 1) * HEAD])
            m = jnp.max(top, axis=1, keepdims=True)
            s_own = None
            if is_span:
                key = ks_ref[:, h * HEAD : (h + 1) * HEAD]
                s_own = lax.dot_general(q, key, contract, preferred_element_type=jnp.float32)
                pos = lax.broadcasted_iota(jnp.int32, (stacked, span_keys), 1)
                s_own = jnp.where(pos < lim, s_own, NEG)
                m = jnp.maximum(m, jnp.max(s_own, axis=1, keepdims=True))
            return jnp.maximum(m, -1e29), s_own

        def values(h, m, s_own):
            acc = jnp.zeros((stacked, 2 * HEAD), jnp.float32)
            for j in range(pre // value_chunk):
                s = s_scr[h, :, j * value_chunk : (j + 1) * value_chunk]
                w = jnp.exp2((s - m) * EXP2_SCALE).astype(jnp.bfloat16)
                val = v_ref[j * value_chunk : (j + 1) * value_chunk, h * HEAD : (h + 1) * HEAD]
                val = jnp.concatenate([val, jnp.ones_like(val)], axis=1)
                acc = acc + jnp.dot(w, val, preferred_element_type=jnp.float32)
            if is_span:
                w = jnp.exp2((s_own - m) * EXP2_SCALE).astype(jnp.bfloat16)
                val = vs_ref[:, h * HEAD : (h + 1) * HEAD]
                val = jnp.concatenate([val, jnp.ones_like(val)], axis=1)
                acc = acc + jnp.dot(w, val, preferred_element_type=jnp.float32)
            total = acc[:, HEAD:]
            seen = total > 0.0
            safe = jnp.where(seen, total, 1.0)
            out = (acc[:, :HEAD] / safe).astype(jnp.bfloat16)
            lse = jnp.where(seen, m * SCALE + jnp.log(safe), NEG)
            return out, lse

        state = scores(0)
        for h in range(kv):
            following = scores(h + 1) if h + 1 < kv else None
            out, lse = values(h, *state)
            for g in range(group):
                head = h * group + g
                o_ref[0, 0, :, head * HEAD : (head + 1) * HEAD] = out[g * rows : (g + 1) * rows]
                packed = jnp.where(lane % PART == head, lse[g * rows : (g + 1) * rows], packed)
            state = following
        o_ref[0, 0, :, kv * group * HEAD :] = pack_lse(packed, lane)

    @pl.when(stream == 0)
    def _():
        run(True)

    @pl.when(stream == 1)
    def _():
        run(False)


def pack_lse(value, lane):
    first = value.astype(jnp.bfloat16)
    rest = value - first.astype(jnp.float32)
    second = rest.astype(jnp.bfloat16)
    third = rest - second.astype(jnp.float32)
    picked = jnp.where(
        lane < PART,
        first.astype(jnp.float32),
        jnp.where(lane < 2 * PART, second.astype(jnp.float32), third),
    )
    return picked.astype(jnp.bfloat16)


def unpack_lse(extra):
    value = extra.astype(jnp.float32)
    return value[:, :PART] + value[:, PART : 2 * PART] + value[:, 2 * PART : 3 * PART]


def attend(queries, offsets, info, positions, caches, kv, group, after=()):
    owners = len(queries)
    _, rows, width = queries[0].shape
    pre = caches[0].shape[0]
    step = offsets[1] - offsets[0] if owners > 1 else 0
    whole = lambda a: pl.BlockSpec(a.shape, lambda o, s, info: (0,) * a.ndim)
    flops = 4 * owners * 2 * rows * group * kv * pre * HEAD
    return pl.pallas_call(
        functools.partial(
            attend_kernel, offsets=offsets, after=len(after), kv=kv, group=group
        ),
        out_shape=jax.ShapeDtypeStruct((owners, 2, rows, width + EXTRA), jnp.bfloat16),
        grid_spec=pltpu.PrefetchScalarGridSpec(
            num_scalar_prefetch=1,
            grid=(owners, 2),
            in_specs=[pl.BlockSpec((1, rows, width), lambda o, s, info: (s, 0, 0)) for _ in queries]
            + [pl.BlockSpec((rows, 1), lambda o, s, info: (info[offsets[0] + o * step], 0))]
            + [whole(a) for a in caches]
            + [pl.BlockSpec(memory_space=pl.ANY) for _ in after],
            out_specs=pl.BlockSpec(
                (1, 1, rows, width + EXTRA), lambda o, s, info: (o, s, 0, 0)
            ),
            scratch_shapes=[
                pltpu.VMEM((rows, width), jnp.bfloat16),
                pltpu.VMEM((kv, rows * group, pre), jnp.float32),
            ],
        ),
        compiler_params=pltpu.CompilerParams(vmem_limit_bytes=VMEM_LIMIT),
        cost_estimate=pl.CostEstimate(
            flops=2 * flops,
            bytes_accessed=4 * pre * kv * HEAD,
            transcendentals=owners * 2 * rows * group * kv * pre,
        ),
        name="attend",
    )(info, *queries, positions, *caches, *after)


def relay_kernel(*refs, plans, arrays, after):
    outs = refs[arrays + after :]
    for out, plan in zip(outs, plans):
        done = 0
        for index, start, stop in plan:
            out[done : done + stop - start] = refs[index][start:stop]
            done += stop - start


def relay(arrays, plans, after=()):
    rows = [sum(stop - start for _, start, stop in plan) for plan in plans]
    outs = [jax.ShapeDtypeStruct((r, *arrays[0].shape[1:]), arrays[0].dtype) for r in rows]
    return pl.pallas_call(
        functools.partial(relay_kernel, plans=plans, arrays=len(arrays), after=len(after)),
        out_shape=outs,
        in_specs=[pl.BlockSpec(memory_space=pltpu.VMEM)] * len(arrays)
        + [pl.BlockSpec(memory_space=pl.ANY)] * len(after),
        out_specs=[pl.BlockSpec(memory_space=pltpu.VMEM)] * len(outs),
        compiler_params=pltpu.CompilerParams(vmem_limit_bytes=VMEM_LIMIT),
        cost_estimate=pl.CostEstimate(
            flops=0, bytes_accessed=4 * sum(math.prod(o.shape) for o in outs), transcendentals=0
        ),
        name="relay",
    )(*arrays, *after)


def blend_kernel(base_ref, *refs, plans, arrived):
    for out, plan in zip(refs[arrived:], plans):
        done = 0
        for start, rows, adds in plan:
            value = base_ref[start : start + rows].astype(jnp.float32)
            for index, offset in adds:
                value = value + refs[index][offset : offset + rows].astype(jnp.float32)
            out[done : done + rows] = value.astype(jnp.bfloat16)
            done += rows


def blend(base, arrived, plans):
    outs = [
        jax.ShapeDtypeStruct((sum(part[1] for part in plan), base.shape[1]), base.dtype)
        for plan in plans
    ]
    return pl.pallas_call(
        functools.partial(blend_kernel, plans=plans, arrived=len(arrived)),
        out_shape=outs,
        in_specs=[pl.BlockSpec(memory_space=pltpu.VMEM)] * (1 + len(arrived)),
        out_specs=[pl.BlockSpec(memory_space=pltpu.VMEM)] * len(outs),
        compiler_params=pltpu.CompilerParams(vmem_limit_bytes=VMEM_LIMIT),
        cost_estimate=pl.CostEstimate(
            flops=0, bytes_accessed=6 * sum(math.prod(o.shape) for o in outs), transcendentals=0
        ),
        name="blend",
    )(base, *arrived)


def fetch(parts, axis):
    def copy(n, i):
        source, target, sems = parts[n]
        size = target.shape[1 + axis]
        tile = pl.ds(pl.multiple_of(i * size, size), size)
        view = source.at[tile] if axis == 0 else source.at[:, tile]
        return pltpu.make_async_copy(view, target.at[i], sems.at[i])

    def start(i, carry):
        for n in range(len(parts)):
            copy(n, i).start()
        return carry

    lax.fori_loop(0, parts[0][1].shape[0], start, 0)
    return lambda n, i: copy(n, i).wait()


def project_kernel(rows_ref, weight_ref, away_ref, kept_ref, tiles, sems):
    count, _, size = tiles.shape
    wait = fetch([(weight_ref, tiles, sems)], 1)
    half = away_ref.shape[0]

    def step(i, carry):
        wait(0, i)
        out = jnp.dot(rows_ref[...], tiles[i], preferred_element_type=jnp.float32)
        part = pl.ds(pl.multiple_of(i * size, size), size)
        away_ref[:, part] = out[:half].astype(jnp.bfloat16)
        kept_ref[:, part] = out[half:]
        return carry

    lax.fori_loop(0, count, step, 0)


def project(rows, weight):
    count, depth = rows.shape
    width = weight.shape[1]
    tile = math.gcd(width, TILE)
    return pl.pallas_call(
        project_kernel,
        out_shape=[
            jax.ShapeDtypeStruct((count // 2, width), jnp.bfloat16),
            jax.ShapeDtypeStruct((count // 2, width), jnp.float32),
        ],
        in_specs=[
            pl.BlockSpec(memory_space=pltpu.VMEM),
            pl.BlockSpec(memory_space=pltpu.HBM),
        ],
        out_specs=[pl.BlockSpec(memory_space=pltpu.VMEM)] * 2,
        scratch_shapes=[
            pltpu.VMEM((width // tile, depth, tile), jnp.bfloat16),
            pltpu.SemaphoreType.DMA((width // tile,)),
        ],
        compiler_params=pltpu.CompilerParams(vmem_limit_bytes=VMEM_LIMIT),
        cost_estimate=pl.CostEstimate(
            flops=2 * count * depth * width, bytes_accessed=2 * depth * width, transcendentals=0
        ),
        name="project",
    )(rows, weight)


def expert_in_kernel(*refs, blocks, follow=None):
    gate_ref, up_ref, o_ref, rows_ref, gate, up, gate_acc, up_acc, gate_sems, up_sems = refs[blocks:]
    count, size, _ = gate.shape
    wait = fetch([(gate_ref.at[0], gate, gate_sems), (up_ref.at[0], up, up_sems)], 0)
    if follow:
        follow()
    done = 0
    for block in refs[:blocks]:
        rows_ref[done : done + block.shape[0]] = block[...]
        done += block.shape[0]
    gate_acc[...] = jnp.zeros_like(gate_acc)
    up_acc[...] = jnp.zeros_like(up_acc)

    def step(i, carry):
        rows = rows_ref[:, pl.ds(pl.multiple_of(i * size, size), size)]
        wait(0, i)
        gate_acc[...] += jnp.dot(rows, gate[i], preferred_element_type=jnp.float32)
        wait(1, i)
        up_acc[...] += jnp.dot(rows, up[i], preferred_element_type=jnp.float32)
        return carry

    lax.fori_loop(0, count, step, 0)
    gate_h = gate_acc[...]
    hidden = gate_h / (1.0 + jnp.exp(-gate_h)) * up_acc[...]
    o_ref[...] = hidden.astype(jnp.bfloat16)


def expert_in(blocks, w_gate, w_up):
    depth, units = w_gate.shape[1:]
    if any(b.shape[0] % 16 for b in blocks):
        blocks = [jnp.concatenate(blocks)]
    rows = sum(b.shape[0] for b in blocks)
    tile = math.gcd(depth, TILE)
    return pl.pallas_call(
        functools.partial(expert_in_kernel, blocks=len(blocks)),
        out_shape=jax.ShapeDtypeStruct((rows, units), jnp.bfloat16),
        in_specs=[pl.BlockSpec(memory_space=pltpu.VMEM)] * len(blocks)
        + [pl.BlockSpec(memory_space=pltpu.HBM)] * 2,
        out_specs=pl.BlockSpec(memory_space=pltpu.VMEM),
        scratch_shapes=[pltpu.VMEM((rows, depth), jnp.bfloat16)]
        + [pltpu.VMEM((depth // tile, tile, units), jnp.bfloat16)] * 2
        + [pltpu.VMEM((rows, units), jnp.float32)] * 2
        + [pltpu.SemaphoreType.DMA((depth // tile,))] * 2,
        compiler_params=pltpu.CompilerParams(vmem_limit_bytes=VMEM_LIMIT),
        cost_estimate=pl.CostEstimate(
            flops=4 * rows * depth * units,
            bytes_accessed=4 * depth * units,
            transcendentals=rows * units,
        ),
        name="expert_in",
    )(*blocks, w_gate, w_up)


def expert_both_kernel(*refs, blocks):
    gate_ref, up_ref, down_ref, o_ref, hidden_ref, down, down_sems = refs[blocks : blocks + 7]
    inner = refs[:blocks] + (gate_ref, up_ref, hidden_ref) + refs[blocks + 7 :]
    holder = {}

    def follow():
        holder["wait"] = fetch([(down_ref.at[0], down, down_sems)], 1)

    expert_in_kernel(*inner, blocks=blocks, follow=follow)
    count, _, size = down.shape

    def step(i, carry):
        holder["wait"](0, i)
        out = jnp.dot(hidden_ref[...], down[i], preferred_element_type=jnp.float32)
        o_ref[:, pl.ds(pl.multiple_of(i * size, size), size)] = out.astype(jnp.bfloat16)
        return carry

    lax.fori_loop(0, count, step, 0)


def expert_both(blocks, w_gate, w_up, w_down, after=()):
    depth, units = w_gate.shape[1:]
    width = w_down.shape[2]
    if any(b.shape[0] % 16 for b in blocks):
        blocks = [jnp.concatenate(blocks)]
    rows = sum(b.shape[0] for b in blocks)
    tile, out_tile = math.gcd(depth, TILE), math.gcd(width, TILE)

    def kernel(*refs):
        count = len(blocks) + 3
        expert_both_kernel(*refs[:count], *refs[count + len(after) :], blocks=len(blocks))

    return pl.pallas_call(
        kernel,
        out_shape=jax.ShapeDtypeStruct((rows, width), jnp.bfloat16),
        in_specs=[pl.BlockSpec(memory_space=pltpu.VMEM)] * len(blocks)
        + [pl.BlockSpec(memory_space=pltpu.HBM)] * 3
        + [pl.BlockSpec(memory_space=pl.ANY)] * len(after),
        out_specs=pl.BlockSpec(memory_space=pltpu.VMEM),
        scratch_shapes=[
            pltpu.VMEM((rows, units), jnp.bfloat16),
            pltpu.VMEM((width // out_tile, units, out_tile), jnp.bfloat16),
            pltpu.SemaphoreType.DMA((width // out_tile,)),
            pltpu.VMEM((rows, depth), jnp.bfloat16),
        ]
        + [pltpu.VMEM((depth // tile, tile, units), jnp.bfloat16)] * 2
        + [pltpu.VMEM((rows, units), jnp.float32)] * 2
        + [pltpu.SemaphoreType.DMA((depth // tile,))] * 2,
        compiler_params=pltpu.CompilerParams(vmem_limit_bytes=VMEM_LIMIT),
        cost_estimate=pl.CostEstimate(
            flops=4 * rows * depth * units + 2 * rows * units * width,
            bytes_accessed=4 * depth * units + 2 * units * width,
            transcendentals=rows * units,
        ),
        name="expert_both",
    )(*blocks, w_gate, w_up, w_down, *after)


def expert_out_kernel(hidden_ref, down_ref, *refs):
    o_ref, down, sems = refs[-3:]
    count, _, size = down.shape
    wait = fetch([(down_ref.at[0], down, sems)], 1)

    def step(i, carry):
        wait(0, i)
        out = jnp.dot(hidden_ref[...], down[i], preferred_element_type=jnp.float32)
        o_ref[:, pl.ds(pl.multiple_of(i * size, size), size)] = out.astype(jnp.bfloat16)
        return carry

    lax.fori_loop(0, count, step, 0)


def expert_out(hidden, w_down, after=()):
    rows, units = hidden.shape
    width = w_down.shape[2]
    tile = math.gcd(width, TILE)
    return pl.pallas_call(
        expert_out_kernel,
        out_shape=jax.ShapeDtypeStruct((rows, width), jnp.bfloat16),
        in_specs=[
            pl.BlockSpec(memory_space=pltpu.VMEM),
            pl.BlockSpec(memory_space=pltpu.HBM),
        ]
        + [pl.BlockSpec(memory_space=pl.ANY)] * len(after),
        out_specs=pl.BlockSpec(memory_space=pltpu.VMEM),
        scratch_shapes=[
            pltpu.VMEM((width // tile, units, tile), jnp.bfloat16),
            pltpu.SemaphoreType.DMA((width // tile,)),
        ],
        compiler_params=pltpu.CompilerParams(vmem_limit_bytes=VMEM_LIMIT),
        cost_estimate=pl.CostEstimate(
            flops=2 * rows * units * width, bytes_accessed=2 * units * width, transcendentals=0
        ),
        name="expert_out",
    )(hidden, w_down, *after)


def merge(parts, heads):
    for head in range(heads):
        lses = [lse[:, head : head + 1] for _, lse in parts]
        top = functools.reduce(jnp.maximum, lses)
        weights = [jnp.exp(lse - top) for lse in lses]
        total = sum(weights)
        inverse = 1.0 / total
        out = 0.0
        for (value, _), weight in zip(parts, weights):
            out = out + value(head).astype(jnp.float32) * (weight * inverse)
        yield head, out, top + jnp.log(total)


def reader(ref):
    return lambda head: ref[:, head * HEAD : (head + 1) * HEAD]


def combine_kernel(part_ref, *refs, heads, present):
    rows = part_ref.shape[2]
    width = heads * HEAD
    recv_refs, outs = refs[: sum(present)], refs[sum(present) :]
    lane = lax.broadcasted_iota(jnp.int32, (rows, EXTRA), 1)
    taken = 0
    for way, there in enumerate(present):
        part, out_ref = part_ref.at[way, 0], outs[way]
        if not there:
            out_ref[...] = part[...]
            continue
        recv = recv_refs[taken]
        taken += 1
        parts = [(reader(ref), unpack_lse(ref[:, width:])) for ref in (recv, part)]
        packed = jnp.full((rows, EXTRA), NEG, jnp.float32)
        for head, out, lse in merge(parts, heads):
            out_ref[:, head * HEAD : (head + 1) * HEAD] = out.astype(jnp.bfloat16)
            packed = jnp.where(lane % PART == head, lse, packed)
        out_ref[:, width:] = pack_lse(packed, lane)


def combine(recvs, part, stream, heads):
    _, _, rows, width = part.shape
    there = [r for r in recvs if r is not None]
    return pl.pallas_call(
        functools.partial(
            combine_kernel, heads=heads, present=tuple(r is not None for r in recvs)
        ),
        out_shape=[jax.ShapeDtypeStruct((rows, width), jnp.bfloat16)] * 2,
        grid=(1,),
        in_specs=[pl.BlockSpec((2, 1, rows, width), lambda i: (0, stream, 0, 0))]
        + [pl.BlockSpec((rows, width), lambda i: (0, 0)) for _ in there],
        out_specs=[pl.BlockSpec((rows, width), lambda i: (0, 0))] * 2,
        compiler_params=pltpu.CompilerParams(vmem_limit_bytes=VMEM_LIMIT),
        cost_estimate=pl.CostEstimate(
            flops=16 * rows * width, bytes_accessed=12 * rows * width, transcendentals=0
        ),
        name="combine",
    )(part, *there)


def finish_kernel(own_ref, s_left, s_right, d_left, d_right, q_ref, k_ref, v_ref, o_ref, *, heads, group):
    width = heads * HEAD
    for stream, arrived in enumerate([(s_left, s_right), (d_left, d_right)]):
        refs = [own_ref.at[0, stream], *arrived]
        parts = [(reader(ref), unpack_lse(ref[:, width:])) for ref in refs]
        if stream == 1:
            scores = []
            for head in range(heads):
                kv = head // group
                q = q_ref[:, head * HEAD : (head + 1) * HEAD].astype(jnp.float32)
                k = k_ref[:, kv * HEAD : (kv + 1) * HEAD].astype(jnp.float32)
                scores.append(jnp.sum(q * k, axis=1, keepdims=True) * SCALE)
            own_value = lambda head: v_ref[:, (head // group) * HEAD : (head // group + 1) * HEAD]
            parts.append((own_value, jnp.concatenate(scores, axis=1)))
        for head, out, _ in merge(parts, heads):
            o_ref[stream, :, head * HEAD : (head + 1) * HEAD] = out.astype(jnp.bfloat16)


def finish(own, span_arrived, decode_arrived, decode_q, decode_k, decode_v, heads, group):
    _, _, rows, width = own.shape
    return pl.pallas_call(
        functools.partial(finish_kernel, heads=heads, group=group),
        out_shape=jax.ShapeDtypeStruct((2, rows, heads * HEAD), jnp.bfloat16),
        in_specs=[pl.BlockSpec(memory_space=pltpu.VMEM)] * 8,
        out_specs=pl.BlockSpec(memory_space=pltpu.VMEM),
        compiler_params=pltpu.CompilerParams(vmem_limit_bytes=VMEM_LIMIT),
        cost_estimate=pl.CostEstimate(
            flops=16 * rows * width, bytes_accessed=16 * rows * width, transcendentals=0
        ),
        name="finish",
    )(own, *span_arrived, *decode_arrived, decode_q, decode_k, decode_v)


def on_device(
    span_q,
    decode_q,
    k_cache,
    v_cache,
    span_k,
    span_v,
    decode_k,
    decode_v,
    decode_pos,
    out_weight,
    span_resid,
    decode_resid,
    norm_gain,
    router,
    span_expert,
    decode_expert,
    w_gate,
    w_up,
    w_down,
):
    f32, bf16 = jnp.float32, jnp.bfloat16
    tok_rows, row_width = span_q.shape
    pre_rows = k_cache.shape[0]
    kv = k_cache.shape[1] // HEAD
    group = HEADS // KV_HEADS
    heads = kv * group
    model_width = span_resid.shape[1]
    ctx_count, exp_count = lax.axis_size("ctx"), lax.axis_size("exp")
    ctx, exp = lax.axis_index("ctx"), lax.axis_index("exp")
    x_count = exp_count // 2
    x, core = exp // 2, exp % 2

    ring = ring_order(ctx_count)
    half = ctx_count // 2
    forward = [(ring[i], ring[(i + 1) % ctx_count]) for i in range(ctx_count)]
    backward = [(b, a) for a, b in forward]
    place = [0] * ctx_count
    for i, c in enumerate(ring):
        place[c] = i
    here = sum(jnp.where(ctx == c, i, 0) for c, i in enumerate(place) if i)
    spot = (here + jnp.arange(ctx_count + 1, dtype=jnp.int32)) % ctx_count
    owner = sum(jnp.where(spot == i, c, 0) for i, c in enumerate(ring) if c)
    info = jnp.where(jnp.arange(ctx_count + 1) == ctx_count, ctx, owner).astype(jnp.int32)
    positions = decode_pos[:, None]
    caches = (k_cache, v_cache, span_k, span_v)

    def ahead(value):
        return lax.ppermute(value, "ctx", forward)

    def back(value):
        return lax.ppermute(value, "ctx", backward)

    other_core = [(e, e ^ 1) for e in range(exp_count)]

    def shift_x(step):
        return [(e, ((e // 2 + step) % x_count) * 2 + e % 2) for e in range(exp_count)]

    def attend_for(queries, offsets, after=()):
        offsets = tuple(offset % ctx_count for offset in offsets)
        return attend(queries, offsets, info, positions, caches, kv, group, after)

    queries = jnp.stack([span_q, decode_q])
    both = [((0, 0, 2),), ((1, 0, 2),)]
    from_back, from_ahead = ahead(queries), back(queries)
    own_part = attend_for([queries], [0])
    from_back, from_ahead = relay([from_back, from_ahead], both, [own_part])
    parts = {}
    for step in range(1, half - 1):
        arrived = ahead(from_back), back(from_ahead)
        done = attend_for([from_ahead, from_back], [step, -step])
        plans = both if step < half - 2 else both + [((0, 0, 1),), ((1, 1, 2),)]
        from_back, from_ahead, *sent = relay(arrived, plans, [done])
        parts[step] = done
    arrived = ahead(sent[0]), back(sent[1])
    near = half - 1
    (far,) = relay(arrived, [((0, 0, 1), (1, 0, 1))], [done])
    far_part = attend_for([far], [half])
    parts[near] = attend_for([from_ahead, from_back], [near, -near])

    moving = [(ahead(far_part[0, 0]), None), (None, back(far_part[0, 1]))]
    for step in range(near, 0, -1):
        for stream in range(2):
            sent = combine(moving[stream], parts[step], stream, heads)
            moving[stream] = ahead(sent[0]), back(sent[1])
    attn = finish(own_part, *moving, decode_q, decode_k, decode_v, heads, group)

    rows_here = span_resid.shape[0]
    by_owner = attn.reshape(2, x_count, 2, rows_here, row_width)

    def rows_for(core_index):
        picked = lax.dynamic_index_in_dim(by_owner, core_index, 2, keepdims=False)
        turned = [
            lax.dynamic_index_in_dim(picked, (x + k) % x_count, 1, keepdims=False)
            for k in range(x_count)
        ]
        return turned

    ordered = jnp.stack(rows_for(1 - core) + rows_for(core))
    away, kept = project(ordered.reshape(-1, row_width), out_weight)
    arrived = lax.ppermute(away, "exp", other_core)
    chip_sum = (kept + arrived.astype(f32)).reshape(x_count, 2 * rows_here, model_width)
    total = chip_sum[x_count - 1]
    for k in range(x_count - 2, -1, -1):
        moved = lax.ppermute(total.astype(bf16), "exp", shift_x(1))
        total = chip_sum[k] + moved.astype(f32)
    resid = jnp.concatenate([span_resid, decode_resid]).astype(f32)
    stream = total + resid
    normed = (
        stream
        * lax.rsqrt(jnp.mean(stream * stream, -1, keepdims=True) + EPS)
        * norm_gain.astype(f32)
    ).astype(bf16)

    expert_ids = jnp.stack([span_expert[:, 0], decode_expert[:, 0]])
    expert_total = router.shape[1]
    logits = jnp.dot(normed, router, preferred_element_type=f32)
    flat_ids = expert_ids.reshape(-1)
    expert_iota = jnp.arange(expert_total, dtype=jnp.int32)
    picked = jnp.sum(jnp.where(flat_ids[:, None] == expert_iota, logits, 0.0), -1)
    routed_in = (normed.astype(f32) * jax.nn.sigmoid(picked)[:, None]).astype(bf16)
    capacity = 2 * tok_rows // (exp_count * exp_count)
    row_order = jnp.arange(rows_here, dtype=jnp.int32)
    same_expert = expert_ids[:, :, None] == expert_ids[:, None, :]
    slot = jnp.sum(same_expert & (row_order[None, :] < row_order[:, None])[None], 2)
    x_turn = (expert_ids // 2 - x + x_count) % x_count
    core_turn = (expert_ids % 2 + core) % 2
    column = (
        ((core_turn * x_count + x_turn) * 2 + jnp.arange(2, dtype=jnp.int32)[:, None]) * capacity
        + slot
    ).reshape(-1)
    core_slots = x_count * 2 * capacity
    onehot = (column[:, None] == jnp.arange(2 * core_slots, dtype=jnp.int32)[None, :]).astype(bf16)

    def slots(which):
        chosen = onehot[:, which * core_slots : (which + 1) * core_slots]
        filled = jnp.einsum("rc,rd->cd", chosen, routed_in, preferred_element_type=f32)
        return filled.astype(bf16).reshape(x_count, 1, 2 * capacity, model_width)

    swapped = lax.ppermute(slots(1), "exp", other_core)
    by_x = jnp.concatenate([slots(0), swapped], 1)

    near_block = by_x[0].reshape(-1, model_width)
    near_in = {1: (ahead(near_block), back(near_block))}
    later_block = jnp.concatenate(
        [
            lax.ppermute(by_x[k], "exp", shift_x(k)).reshape(-1, model_width)
            for k in range(1, x_count)
        ]
    )
    near_rows, later_rows = near_block.shape[0], later_block.shape[0]
    half_near, half_later = near_rows // 2, later_rows // 2
    later_in = {1: (ahead(later_block), back(later_block))}
    near_in[2] = ahead(near_in[1][0]), back(near_in[1][1])

    def pair(arrived):
        return [arrived[1], arrived[0]]

    hidden = {1: expert_in([near_block, later_block] + pair(near_in[1]), w_gate, w_up)}
    straight = [((0, 0, near_rows),), ((1, 0, near_rows),)]
    cut_near = [((0, 0, half_near),), ((1, half_near, near_rows),)]
    cut_later = [((0, 0, half_later),), ((1, half_later, later_rows),)]
    for step in range(2, half):
        sent = relay(near_in[step], straight if step < near else cut_near, [hidden[step - 1]])
        near_in[step + 1] = ahead(sent[0]), back(sent[1])
        sent = relay(later_in[step - 1], [((0, 0, later_rows),), ((1, 0, later_rows),)], [hidden[step - 1]])
        later_in[step] = ahead(sent[0]), back(sent[1])
        hidden[step] = expert_in(pair(near_in[step]) + pair(later_in[step - 1]), w_gate, w_up)
    sent = relay(later_in[near], cut_later, [hidden[near]])
    later_in[half] = ahead(sent[0]), back(sent[1])
    last = [*later_in[half], *near_in[half], *pair(later_in[near])]

    near_spots = {half: (half, 2 * half_later, 2 * half_later + half_near)}
    later_spots = {half: (half, 0, half_later)}
    start = 2 * half_later + 2 * half_near
    later_spots[near] = (half, start, start + later_rows)
    for step in range(2, half):
        near_spots[step] = (step, 0, near_rows)
        start = 2 * near_rows
        later_spots[step - 1] = (step, start, start + later_rows)
    near_spots[1] = (1, near_rows + later_rows, 2 * near_rows + later_rows)
    outs = {half: expert_both(last, w_gate, w_up, w_down, [hidden[near]])}
    outs[near] = expert_out(hidden[near], w_down, [outs[half]])

    def home_step(spots, rows, moving, step, offset):
        call, first, second = spots[step]
        half_rows = rows // 2
        if step == near:
            plans = [
                ((first, half_rows, ((0, offset),)), (first + half_rows, half_rows, ())),
                ((second, half_rows, ()), (second + half_rows, half_rows, ((1, offset),))),
            ]
        else:
            plans = [((first, rows, ((0, 0),)),), ((second, rows, ((1, 0),)),)]
        sent = blend(outs[call], moving, plans)
        return ahead(sent[0]), back(sent[1])

    plans = [
        tuple((spots[half][way], rows // 2, ()) for spots, rows in ((later_spots, later_rows), (near_spots, near_rows)))
        for way in (1, 2)
    ]
    sent = blend(outs[half], (), plans)
    later_moving = near_moving = ahead(sent[0]), back(sent[1])
    for step in range(near, 0, -1):
        later_moving = home_step(later_spots, later_rows, later_moving, step, 0)
        if step > 1:
            outs[step - 1] = expert_out(hidden[step - 1], w_down, [later_moving[0]])
        near_moving = home_step(near_spots, near_rows, near_moving, step, half_later)
    (later_sum,) = blend(outs[1], later_moving, [((near_rows, later_rows, ((0, 0), (1, 0))),)])
    (near_sum,) = blend(outs[1], near_moving, [((0, near_rows, ((0, 0), (1, 0))),)])

    later_sum = later_sum.reshape(x_count - 1, 2, 2 * capacity, model_width)
    home = [
        lax.ppermute(later_sum[k - 1], "exp", shift_x(-k)) for k in range(1, x_count)
    ]
    home = jnp.stack([near_sum.reshape(2, 2 * capacity, model_width)] + home)
    swapped = lax.ppermute(home[:, 1], "exp", other_core)
    returned = jnp.stack([home[:, 0], swapped]).reshape(-1, model_width)
    routed = jnp.dot(onehot, returned, preferred_element_type=f32)
    result = (stream + routed).astype(bf16)
    return (result[:rows_here], result[rows_here:])


def solution(mesh):
    in_specs = (
        P("ctx", "exp"),
        P("ctx", "exp"),
        P("ctx", "exp"),
        P("ctx", "exp"),
        P("ctx", "exp"),
        P("ctx", "exp"),
        P("ctx", "exp"),
        P("ctx", "exp"),
        P(),
        P("exp", None),
        P(("ctx", "exp"), None),
        P(("ctx", "exp"), None),
        P(),
        P(),
        P(("ctx", "exp"), None),
        P(("ctx", "exp"), None),
        P("exp", None, "ctx"),
        P("exp", None, "ctx"),
        P("exp", "ctx", None),
    )
    out_specs = (P(("ctx", "exp"), None), P(("ctx", "exp"), None))
    return jax.shard_map(
        on_device, mesh=mesh, in_specs=in_specs, out_specs=out_specs, check_vma=False
    )
```

```python
import functools
import math

import jax
import jax.numpy as jnp
from jax import lax
from jax.experimental import pallas as pl
from jax.experimental.pallas import tpu as pltpu
from jax.sharding import PartitionSpec as P

HEADS = 40
KV_HEADS = 8
HEAD = 128

NEG = -1e30
EPS = 1e-05
SCALE = HEAD ** (-0.5)
EXP2_SCALE = SCALE * math.log2(math.e)
EXTRA = 128
PART = 32
KEY_CHUNK = 256
VALUE_CHUNK = 1024
TILE = 512
VMEM_LIMIT = 48 * 1024 * 1024


def ring_order(count):
    if count % 8:
        return list(range(count))
    major, minor = 4, count // 4
    path = [(0, 0)]
    for b in range(minor):
        span = range(1, major) if b % 2 == 0 else range(major - 1, 0, -1)
        path += [(a, b) for a in span]
    path += [(0, b) for b in range(minor - 1, 0, -1)]
    return [a * minor + b for a, b in path]


def attend_kernel(info_ref, *refs, offsets, after, kv, group):
    owners = len(offsets)
    q_refs = refs[:owners]
    pos_ref, k_ref, v_ref, ks_ref, vs_ref = refs[owners : owners + 5]
    o_ref, q_scr, s_scr = refs[owners + 5 + after :]
    owner = pl.program_id(0)
    _, rows, _ = q_scr.shape
    pre, span_keys = k_ref.shape[0], ks_ref.shape[0]
    key_chunk, value_chunk = math.gcd(pre, KEY_CHUNK), math.gcd(pre, VALUE_CHUNK)
    stacked = rows * group
    contract = (((1,), (1,)), ((), ()))
    for i in range(owners):

        @pl.when(owner == i)
        def _(i=i):
            q_scr[...] = q_refs[i][...]

    ctx = info_ref[info_ref.shape[0] - 1]
    step = offsets[1] - offsets[0] if owners > 1 else 0
    from_here = (info_ref[offsets[0] + owner * step] - ctx) * rows
    limits = [
        from_here + 1 + lax.broadcasted_iota(jnp.int32, (rows, 1), 0),
        pos_ref[...] - ctx * pre,
    ]
    limits = [jnp.concatenate([limit] * group, axis=0) for limit in limits]
    lane = lax.broadcasted_iota(jnp.int32, (rows, EXTRA), 1)
    packed = [jnp.full((rows, EXTRA), NEG, jnp.float32)] * 2
    halves = slice(0, stacked), slice(stacked, 2 * stacked)

    def scores(h):
        q = jnp.concatenate(
            [
                q_scr[stream, :, (h * group + g) * HEAD : (h * group + g + 1) * HEAD]
                for stream in range(2)
                for g in range(group)
            ],
            axis=0,
        )
        tops = [jnp.full((stacked, HEAD), NEG, jnp.float32)] * 2
        for j in range(pre // key_chunk):
            here = slice(j * key_chunk, (j + 1) * key_chunk)
            key = k_ref[here, h * HEAD : (h + 1) * HEAD]
            both = lax.dot_general(q, key, contract, preferred_element_type=jnp.float32)
            for stream in range(2):
                s = both[halves[stream]]
                if stream == 1:
                    pos = j * key_chunk + lax.broadcasted_iota(jnp.int32, s.shape, 1)
                    s = jnp.where(pos < limits[1], s, NEG)
                s_scr[h, halves[stream], here] = s
                for t in range(key_chunk // HEAD):
                    tops[stream] = jnp.maximum(tops[stream], s[:, t * HEAD : (t + 1) * HEAD])
        largest = [jnp.max(top, axis=1, keepdims=True) for top in tops]
        key = ks_ref[:, h * HEAD : (h + 1) * HEAD]
        s_own = lax.dot_general(q[halves[0]], key, contract, preferred_element_type=jnp.float32)
        pos = lax.broadcasted_iota(jnp.int32, s_own.shape, 1)
        s_own = jnp.where(pos < limits[0], s_own, NEG)
        largest[0] = jnp.maximum(largest[0], jnp.max(s_own, axis=1, keepdims=True))
        return [jnp.maximum(m, -1e29) for m in largest], s_own

    def values(h, largest, s_own):
        m = jnp.concatenate(largest, axis=0)
        acc = jnp.zeros((2 * stacked, 2 * HEAD), jnp.float32)
        for j in range(pre // value_chunk):
            here = slice(j * value_chunk, (j + 1) * value_chunk)
            w = jnp.exp2((s_scr[h, :, here] - m) * EXP2_SCALE).astype(jnp.bfloat16)
            val = v_ref[here, h * HEAD : (h + 1) * HEAD]
            val = jnp.concatenate([val, jnp.ones_like(val)], axis=1)
            acc = acc + jnp.dot(w, val, preferred_element_type=jnp.float32)
        w = jnp.exp2((s_own - largest[0]) * EXP2_SCALE).astype(jnp.bfloat16)
        val = vs_ref[:, h * HEAD : (h + 1) * HEAD]
        val = jnp.concatenate([val, jnp.ones_like(val)], axis=1)
        accs = [acc[halves[0]], acc[halves[1]]]
        accs[0] = accs[0] + jnp.dot(w, val, preferred_element_type=jnp.float32)
        results = []
        for acc, m in zip(accs, largest):
            total = acc[:, HEAD:]
            seen = total > 0.0
            safe = jnp.where(seen, total, 1.0)
            out = (acc[:, :HEAD] / safe).astype(jnp.bfloat16)
            results.append((out, jnp.where(seen, m * SCALE + jnp.log(safe), NEG)))
        return results

    state = scores(0)
    for h in range(kv):
        following = scores(h + 1) if h + 1 < kv else None
        for stream, (out, lse) in enumerate(values(h, *state)):
            for g in range(group):
                head = h * group + g
                mine = slice(g * rows, (g + 1) * rows)
                o_ref[0, stream, :, head * HEAD : (head + 1) * HEAD] = out[mine]
                packed[stream] = jnp.where(lane % PART == head, lse[mine], packed[stream])
        state = following
    for stream in range(2):
        o_ref[0, stream, :, kv * group * HEAD :] = pack_lse(packed[stream], lane)


def pack_lse(value, lane):
    first = value.astype(jnp.bfloat16)
    rest = value - first.astype(jnp.float32)
    second = rest.astype(jnp.bfloat16)
    third = rest - second.astype(jnp.float32)
    picked = jnp.where(
        lane < PART,
        first.astype(jnp.float32),
        jnp.where(lane < 2 * PART, second.astype(jnp.float32), third),
    )
    return picked.astype(jnp.bfloat16)


def unpack_lse(extra):
    value = extra.astype(jnp.float32)
    return value[:, :PART] + value[:, PART : 2 * PART] + value[:, 2 * PART : 3 * PART]


def attend(queries, offsets, info, positions, caches, kv, group, after=()):
    owners = len(queries)
    _, rows, width = queries[0].shape
    pre = caches[0].shape[0]
    step = offsets[1] - offsets[0] if owners > 1 else 0
    whole = lambda a: pl.BlockSpec(a.shape, lambda o, info: (0,) * a.ndim)
    flops = 4 * owners * 2 * rows * group * kv * pre * HEAD
    return pl.pallas_call(
        functools.partial(
            attend_kernel, offsets=offsets, after=len(after), kv=kv, group=group
        ),
        out_shape=jax.ShapeDtypeStruct((owners, 2, rows, width + EXTRA), jnp.bfloat16),
        grid_spec=pltpu.PrefetchScalarGridSpec(
            num_scalar_prefetch=1,
            grid=(owners,),
            in_specs=[pl.BlockSpec((2, rows, width), lambda o, info: (0, 0, 0)) for _ in queries]
            + [pl.BlockSpec((rows, 1), lambda o, info: (info[offsets[0] + o * step], 0))]
            + [whole(a) for a in caches]
            + [pl.BlockSpec(memory_space=pl.ANY) for _ in after],
            out_specs=pl.BlockSpec(
                (1, 2, rows, width + EXTRA), lambda o, info: (o, 0, 0, 0)
            ),
            scratch_shapes=[
                pltpu.VMEM((2, rows, width), jnp.bfloat16),
                pltpu.VMEM((kv, 2 * rows * group, pre), jnp.float32),
            ],
        ),
        compiler_params=pltpu.CompilerParams(vmem_limit_bytes=VMEM_LIMIT),
        cost_estimate=pl.CostEstimate(
            flops=2 * flops,
            bytes_accessed=4 * pre * kv * HEAD,
            transcendentals=owners * 2 * rows * group * kv * pre,
        ),
        name="attend",
    )(info, *queries, positions, *caches, *after)


def relay_kernel(*refs, plans, arrays, after):
    outs = refs[arrays + after :]
    for out, plan in zip(outs, plans):
        done = 0
        for index, start, stop in plan:
            out[done : done + stop - start] = refs[index][start:stop]
            done += stop - start


def relay(arrays, plans, after=()):
    rows = [sum(stop - start for _, start, stop in plan) for plan in plans]
    outs = [jax.ShapeDtypeStruct((r, *arrays[0].shape[1:]), arrays[0].dtype) for r in rows]
    return pl.pallas_call(
        functools.partial(relay_kernel, plans=plans, arrays=len(arrays), after=len(after)),
        out_shape=outs,
        in_specs=[pl.BlockSpec(memory_space=pltpu.VMEM)] * len(arrays)
        + [pl.BlockSpec(memory_space=pl.ANY)] * len(after),
        out_specs=[pl.BlockSpec(memory_space=pltpu.VMEM)] * len(outs),
        compiler_params=pltpu.CompilerParams(vmem_limit_bytes=VMEM_LIMIT),
        cost_estimate=pl.CostEstimate(
            flops=0, bytes_accessed=4 * sum(math.prod(o.shape) for o in outs), transcendentals=0
        ),
        name="relay",
    )(*arrays, *after)


def blend_kernel(base_ref, *refs, plans, arrived):
    for out, plan in zip(refs[arrived:], plans):
        done = 0
        for start, rows, adds in plan:
            value = base_ref[start : start + rows].astype(jnp.float32)
            for index, offset in adds:
                value = value + refs[index][offset : offset + rows].astype(jnp.float32)
            out[done : done + rows] = value.astype(jnp.bfloat16)
            done += rows


def blend(base, arrived, plans):
    outs = [
        jax.ShapeDtypeStruct((sum(part[1] for part in plan), base.shape[1]), base.dtype)
        for plan in plans
    ]
    return pl.pallas_call(
        functools.partial(blend_kernel, plans=plans, arrived=len(arrived)),
        out_shape=outs,
        in_specs=[pl.BlockSpec(memory_space=pltpu.VMEM)] * (1 + len(arrived)),
        out_specs=[pl.BlockSpec(memory_space=pltpu.VMEM)] * len(outs),
        compiler_params=pltpu.CompilerParams(vmem_limit_bytes=VMEM_LIMIT),
        cost_estimate=pl.CostEstimate(
            flops=0, bytes_accessed=6 * sum(math.prod(o.shape) for o in outs), transcendentals=0
        ),
        name="blend",
    )(base, *arrived)


def fetch(parts, axis):
    def copy(n, i):
        source, target, sems = parts[n]
        size = target.shape[1 + axis]
        tile = pl.ds(pl.multiple_of(i * size, size), size)
        view = source.at[tile] if axis == 0 else source.at[:, tile]
        return pltpu.make_async_copy(view, target.at[i], sems.at[i])

    def start(i, carry):
        for n in range(len(parts)):
            copy(n, i).start()
        return carry

    lax.fori_loop(0, parts[0][1].shape[0], start, 0)
    return lambda n, i: copy(n, i).wait()


def project_kernel(rows_ref, weight_ref, away_ref, kept_ref, tiles, sems):
    count, _, size = tiles.shape
    wait = fetch([(weight_ref, tiles, sems)], 1)
    half = away_ref.shape[0]

    def step(i, carry):
        wait(0, i)
        out = jnp.dot(rows_ref[...], tiles[i], preferred_element_type=jnp.float32)
        part = pl.ds(pl.multiple_of(i * size, size), size)
        away_ref[:, part] = out[:half].astype(jnp.bfloat16)
        kept_ref[:, part] = out[half:]
        return carry

    lax.fori_loop(0, count, step, 0)


def project(rows, weight):
    count, depth = rows.shape
    width = weight.shape[1]
    tile = math.gcd(width, TILE)
    return pl.pallas_call(
        project_kernel,
        out_shape=[
            jax.ShapeDtypeStruct((count // 2, width), jnp.bfloat16),
            jax.ShapeDtypeStruct((count // 2, width), jnp.float32),
        ],
        in_specs=[
            pl.BlockSpec(memory_space=pltpu.VMEM),
            pl.BlockSpec(memory_space=pltpu.HBM),
        ],
        out_specs=[pl.BlockSpec(memory_space=pltpu.VMEM)] * 2,
        scratch_shapes=[
            pltpu.VMEM((width // tile, depth, tile), jnp.bfloat16),
            pltpu.SemaphoreType.DMA((width // tile,)),
        ],
        compiler_params=pltpu.CompilerParams(vmem_limit_bytes=VMEM_LIMIT),
        cost_estimate=pl.CostEstimate(
            flops=2 * count * depth * width, bytes_accessed=2 * depth * width, transcendentals=0
        ),
        name="project",
    )(rows, weight)


def expert_in_kernel(*refs, blocks, follow=None):
    gate_ref, up_ref, o_ref, rows_ref, gate, up, gate_acc, up_acc, gate_sems, up_sems = refs[blocks:]
    count, size, _ = gate.shape
    wait = fetch([(gate_ref.at[0], gate, gate_sems), (up_ref.at[0], up, up_sems)], 0)
    if follow:
        follow()
    done = 0
    for block in refs[:blocks]:
        rows_ref[done : done + block.shape[0]] = block[...]
        done += block.shape[0]
    gate_acc[...] = jnp.zeros_like(gate_acc)
    up_acc[...] = jnp.zeros_like(up_acc)

    def step(i, carry):
        rows = rows_ref[:, pl.ds(pl.multiple_of(i * size, size), size)]
        wait(0, i)
        gate_acc[...] += jnp.dot(rows, gate[i], preferred_element_type=jnp.float32)
        wait(1, i)
        up_acc[...] += jnp.dot(rows, up[i], preferred_element_type=jnp.float32)
        return carry

    lax.fori_loop(0, count, step, 0)
    gate_h = gate_acc[...]
    hidden = gate_h / (1.0 + jnp.exp(-gate_h)) * up_acc[...]
    o_ref[...] = hidden.astype(jnp.bfloat16)


def expert_in(blocks, w_gate, w_up):
    depth, units = w_gate.shape[1:]
    if any(b.shape[0] % 16 for b in blocks):
        blocks = [jnp.concatenate(blocks)]
    rows = sum(b.shape[0] for b in blocks)
    tile = math.gcd(depth, TILE)
    return pl.pallas_call(
        functools.partial(expert_in_kernel, blocks=len(blocks)),
        out_shape=jax.ShapeDtypeStruct((rows, units), jnp.bfloat16),
        in_specs=[pl.BlockSpec(memory_space=pltpu.VMEM)] * len(blocks)
        + [pl.BlockSpec(memory_space=pltpu.HBM)] * 2,
        out_specs=pl.BlockSpec(memory_space=pltpu.VMEM),
        scratch_shapes=[pltpu.VMEM((rows, depth), jnp.bfloat16)]
        + [pltpu.VMEM((depth // tile, tile, units), jnp.bfloat16)] * 2
        + [pltpu.VMEM((rows, units), jnp.float32)] * 2
        + [pltpu.SemaphoreType.DMA((depth // tile,))] * 2,
        compiler_params=pltpu.CompilerParams(vmem_limit_bytes=VMEM_LIMIT),
        cost_estimate=pl.CostEstimate(
            flops=4 * rows * depth * units,
            bytes_accessed=4 * depth * units,
            transcendentals=rows * units,
        ),
        name="expert_in",
    )(*blocks, w_gate, w_up)


def expert_both_kernel(*refs, blocks):
    gate_ref, up_ref, down_ref, o_ref, hidden_ref, down, down_sems = refs[blocks : blocks + 7]
    inner = refs[:blocks] + (gate_ref, up_ref, hidden_ref) + refs[blocks + 7 :]
    holder = {}

    def follow():
        holder["wait"] = fetch([(down_ref.at[0], down, down_sems)], 1)

    expert_in_kernel(*inner, blocks=blocks, follow=follow)
    count, _, size = down.shape

    def step(i, carry):
        holder["wait"](0, i)
        out = jnp.dot(hidden_ref[...], down[i], preferred_element_type=jnp.float32)
        o_ref[:, pl.ds(pl.multiple_of(i * size, size), size)] = out.astype(jnp.bfloat16)
        return carry

    lax.fori_loop(0, count, step, 0)


def expert_both(blocks, w_gate, w_up, w_down, after=()):
    depth, units = w_gate.shape[1:]
    width = w_down.shape[2]
    if any(b.shape[0] % 16 for b in blocks):
        blocks = [jnp.concatenate(blocks)]
    rows = sum(b.shape[0] for b in blocks)
    tile, out_tile = math.gcd(depth, TILE), math.gcd(width, TILE)

    def kernel(*refs):
        count = len(blocks) + 3
        expert_both_kernel(*refs[:count], *refs[count + len(after) :], blocks=len(blocks))

    return pl.pallas_call(
        kernel,
        out_shape=jax.ShapeDtypeStruct((rows, width), jnp.bfloat16),
        in_specs=[pl.BlockSpec(memory_space=pltpu.VMEM)] * len(blocks)
        + [pl.BlockSpec(memory_space=pltpu.HBM)] * 3
        + [pl.BlockSpec(memory_space=pl.ANY)] * len(after),
        out_specs=pl.BlockSpec(memory_space=pltpu.VMEM),
        scratch_shapes=[
            pltpu.VMEM((rows, units), jnp.bfloat16),
            pltpu.VMEM((width // out_tile, units, out_tile), jnp.bfloat16),
            pltpu.SemaphoreType.DMA((width // out_tile,)),
            pltpu.VMEM((rows, depth), jnp.bfloat16),
        ]
        + [pltpu.VMEM((depth // tile, tile, units), jnp.bfloat16)] * 2
        + [pltpu.VMEM((rows, units), jnp.float32)] * 2
        + [pltpu.SemaphoreType.DMA((depth // tile,))] * 2,
        compiler_params=pltpu.CompilerParams(vmem_limit_bytes=VMEM_LIMIT),
        cost_estimate=pl.CostEstimate(
            flops=4 * rows * depth * units + 2 * rows * units * width,
            bytes_accessed=4 * depth * units + 2 * units * width,
            transcendentals=rows * units,
        ),
        name="expert_both",
    )(*blocks, w_gate, w_up, w_down, *after)


def expert_out_kernel(hidden_ref, down_ref, *refs):
    o_ref, down, sems = refs[-3:]
    count, _, size = down.shape
    wait = fetch([(down_ref.at[0], down, sems)], 1)

    def step(i, carry):
        wait(0, i)
        out = jnp.dot(hidden_ref[...], down[i], preferred_element_type=jnp.float32)
        o_ref[:, pl.ds(pl.multiple_of(i * size, size), size)] = out.astype(jnp.bfloat16)
        return carry

    lax.fori_loop(0, count, step, 0)


def expert_out(hidden, w_down, after=()):
    rows, units = hidden.shape
    width = w_down.shape[2]
    tile = math.gcd(width, TILE)
    return pl.pallas_call(
        expert_out_kernel,
        out_shape=jax.ShapeDtypeStruct((rows, width), jnp.bfloat16),
        in_specs=[
            pl.BlockSpec(memory_space=pltpu.VMEM),
            pl.BlockSpec(memory_space=pltpu.HBM),
        ]
        + [pl.BlockSpec(memory_space=pl.ANY)] * len(after),
        out_specs=pl.BlockSpec(memory_space=pltpu.VMEM),
        scratch_shapes=[
            pltpu.VMEM((width // tile, units, tile), jnp.bfloat16),
            pltpu.SemaphoreType.DMA((width // tile,)),
        ],
        compiler_params=pltpu.CompilerParams(vmem_limit_bytes=VMEM_LIMIT),
        cost_estimate=pl.CostEstimate(
            flops=2 * rows * units * width, bytes_accessed=2 * units * width, transcendentals=0
        ),
        name="expert_out",
    )(hidden, w_down, *after)


def merge(parts, heads):
    for head in range(heads):
        lses = [lse[:, head : head + 1] for _, lse in parts]
        top = functools.reduce(jnp.maximum, lses)
        weights = [jnp.exp(lse - top) for lse in lses]
        total = sum(weights)
        inverse = 1.0 / total
        out = 0.0
        for (value, _), weight in zip(parts, weights):
            out = out + value(head).astype(jnp.float32) * (weight * inverse)
        yield head, out, top + jnp.log(total)


def reader(ref):
    return lambda head: ref[:, head * HEAD : (head + 1) * HEAD]


def combine_kernel(part_ref, *refs, heads, present):
    rows = part_ref.shape[2]
    width = heads * HEAD
    recv_refs, outs = refs[: sum(present)], refs[sum(present) :]
    lane = lax.broadcasted_iota(jnp.int32, (rows, EXTRA), 1)
    taken = 0
    for way, there in enumerate(present):
        part, out_ref = part_ref.at[way, 0], outs[way]
        if not there:
            out_ref[...] = part[...]
            continue
        recv = recv_refs[taken]
        taken += 1
        parts = [(reader(ref), unpack_lse(ref[:, width:])) for ref in (recv, part)]
        packed = jnp.full((rows, EXTRA), NEG, jnp.float32)
        for head, out, lse in merge(parts, heads):
            out_ref[:, head * HEAD : (head + 1) * HEAD] = out.astype(jnp.bfloat16)
            packed = jnp.where(lane % PART == head, lse, packed)
        out_ref[:, width:] = pack_lse(packed, lane)


def combine(recvs, part, stream, heads):
    _, _, rows, width = part.shape
    there = [r for r in recvs if r is not None]
    return pl.pallas_call(
        functools.partial(
            combine_kernel, heads=heads, present=tuple(r is not None for r in recvs)
        ),
        out_shape=[jax.ShapeDtypeStruct((rows, width), jnp.bfloat16)] * 2,
        grid=(1,),
        in_specs=[pl.BlockSpec((2, 1, rows, width), lambda i: (0, stream, 0, 0))]
        + [pl.BlockSpec((rows, width), lambda i: (0, 0)) for _ in there],
        out_specs=[pl.BlockSpec((rows, width), lambda i: (0, 0))] * 2,
        compiler_params=pltpu.CompilerParams(vmem_limit_bytes=VMEM_LIMIT),
        cost_estimate=pl.CostEstimate(
            flops=16 * rows * width, bytes_accessed=12 * rows * width, transcendentals=0
        ),
        name="combine",
    )(part, *there)


def finish_kernel(own_ref, s_left, s_right, d_left, d_right, q_ref, k_ref, v_ref, o_ref, *, heads, group):
    width = heads * HEAD
    for stream, arrived in enumerate([(s_left, s_right), (d_left, d_right)]):
        refs = [own_ref.at[0, stream], *arrived]
        parts = [(reader(ref), unpack_lse(ref[:, width:])) for ref in refs]
        if stream == 1:
            scores = []
            for head in range(heads):
                kv = head // group
                q = q_ref[:, head * HEAD : (head + 1) * HEAD].astype(jnp.float32)
                k = k_ref[:, kv * HEAD : (kv + 1) * HEAD].astype(jnp.float32)
                scores.append(jnp.sum(q * k, axis=1, keepdims=True) * SCALE)
            own_value = lambda head: v_ref[:, (head // group) * HEAD : (head // group + 1) * HEAD]
            parts.append((own_value, jnp.concatenate(scores, axis=1)))
        for head, out, _ in merge(parts, heads):
            o_ref[stream, :, head * HEAD : (head + 1) * HEAD] = out.astype(jnp.bfloat16)


def finish(own, span_arrived, decode_arrived, decode_q, decode_k, decode_v, heads, group):
    _, _, rows, width = own.shape
    return pl.pallas_call(
        functools.partial(finish_kernel, heads=heads, group=group),
        out_shape=jax.ShapeDtypeStruct((2, rows, heads * HEAD), jnp.bfloat16),
        in_specs=[pl.BlockSpec(memory_space=pltpu.VMEM)] * 8,
        out_specs=pl.BlockSpec(memory_space=pltpu.VMEM),
        compiler_params=pltpu.CompilerParams(vmem_limit_bytes=VMEM_LIMIT),
        cost_estimate=pl.CostEstimate(
            flops=16 * rows * width, bytes_accessed=16 * rows * width, transcendentals=0
        ),
        name="finish",
    )(own, *span_arrived, *decode_arrived, decode_q, decode_k, decode_v)


def on_device(
    span_q,
    decode_q,
    k_cache,
    v_cache,
    span_k,
    span_v,
    decode_k,
    decode_v,
    decode_pos,
    out_weight,
    span_resid,
    decode_resid,
    norm_gain,
    router,
    span_expert,
    decode_expert,
    w_gate,
    w_up,
    w_down,
):
    f32, bf16 = jnp.float32, jnp.bfloat16
    tok_rows, row_width = span_q.shape
    pre_rows = k_cache.shape[0]
    kv = k_cache.shape[1] // HEAD
    group = HEADS // KV_HEADS
    heads = kv * group
    model_width = span_resid.shape[1]
    ctx_count, exp_count = lax.axis_size("ctx"), lax.axis_size("exp")
    ctx, exp = lax.axis_index("ctx"), lax.axis_index("exp")
    x_count = exp_count // 2
    x, core = exp // 2, exp % 2

    ring = ring_order(ctx_count)
    half = ctx_count // 2
    forward = [(ring[i], ring[(i + 1) % ctx_count]) for i in range(ctx_count)]
    backward = [(b, a) for a, b in forward]
    place = [0] * ctx_count
    for i, c in enumerate(ring):
        place[c] = i
    here = sum(jnp.where(ctx == c, i, 0) for c, i in enumerate(place) if i)
    spot = (here + jnp.arange(ctx_count + 1, dtype=jnp.int32)) % ctx_count
    owner = sum(jnp.where(spot == i, c, 0) for i, c in enumerate(ring) if c)
    info = jnp.where(jnp.arange(ctx_count + 1) == ctx_count, ctx, owner).astype(jnp.int32)
    positions = decode_pos[:, None]
    caches = (k_cache, v_cache, span_k, span_v)

    def ahead(value):
        return lax.ppermute(value, "ctx", forward)

    def back(value):
        return lax.ppermute(value, "ctx", backward)

    other_core = [(e, e ^ 1) for e in range(exp_count)]

    def shift_x(step):
        return [(e, ((e // 2 + step) % x_count) * 2 + e % 2) for e in range(exp_count)]

    def attend_for(queries, offsets, after=()):
        offsets = tuple(offset % ctx_count for offset in offsets)
        return attend(queries, offsets, info, positions, caches, kv, group, after)

    queries = jnp.stack([span_q, decode_q])
    both = [((0, 0, 2),), ((1, 0, 2),)]
    from_back, from_ahead = ahead(queries), back(queries)
    own_part = attend_for([queries], [0])
    from_back, from_ahead = relay([from_back, from_ahead], both, [own_part])
    parts = {}
    for step in range(1, half - 1):
        arrived = ahead(from_back), back(from_ahead)
        done = attend_for([from_ahead, from_back], [step, -step])
        plans = both if step < half - 2 else both + [((0, 0, 1),), ((1, 1, 2),)]
        from_back, from_ahead, *sent = relay(arrived, plans, [done])
        parts[step] = done
    arrived = ahead(sent[0]), back(sent[1])
    near = half - 1
    (far,) = relay(arrived, [((0, 0, 1), (1, 0, 1))], [done])
    far_part = attend_for([far], [half])
    parts[near] = attend_for([from_ahead, from_back], [near, -near])

    moving = [(ahead(far_part[0, 0]), None), (None, back(far_part[0, 1]))]
    for step in range(near, 0, -1):
        for stream in range(2):
            sent = combine(moving[stream], parts[step], stream, heads)
            moving[stream] = ahead(sent[0]), back(sent[1])
    attn = finish(own_part, *moving, decode_q, decode_k, decode_v, heads, group)

    rows_here = span_resid.shape[0]
    by_owner = attn.reshape(2, x_count, 2, rows_here, row_width)

    def rows_for(core_index):
        picked = lax.dynamic_index_in_dim(by_owner, core_index, 2, keepdims=False)
        turned = [
            lax.dynamic_index_in_dim(picked, (x + k) % x_count, 1, keepdims=False)
            for k in range(x_count)
        ]
        return turned

    ordered = jnp.stack(rows_for(1 - core) + rows_for(core))
    away, kept = project(ordered.reshape(-1, row_width), out_weight)
    arrived = lax.ppermute(away, "exp", other_core)
    chip_sum = (kept + arrived.astype(f32)).reshape(x_count, 2 * rows_here, model_width)
    total = chip_sum[x_count - 1]
    for k in range(x_count - 2, -1, -1):
        moved = lax.ppermute(total.astype(bf16), "exp", shift_x(1))
        total = chip_sum[k] + moved.astype(f32)
    resid = jnp.concatenate([span_resid, decode_resid]).astype(f32)
    stream = total + resid
    normed = (
        stream
        * lax.rsqrt(jnp.mean(stream * stream, -1, keepdims=True) + EPS)
        * norm_gain.astype(f32)
    ).astype(bf16)

    expert_ids = jnp.stack([span_expert[:, 0], decode_expert[:, 0]])
    expert_total = router.shape[1]
    logits = jnp.dot(normed, router, preferred_element_type=f32)
    flat_ids = expert_ids.reshape(-1)
    expert_iota = jnp.arange(expert_total, dtype=jnp.int32)
    picked = jnp.sum(jnp.where(flat_ids[:, None] == expert_iota, logits, 0.0), -1)
    routed_in = (normed.astype(f32) * jax.nn.sigmoid(picked)[:, None]).astype(bf16)
    capacity = 2 * tok_rows // (exp_count * exp_count)
    row_order = jnp.arange(rows_here, dtype=jnp.int32)
    same_expert = expert_ids[:, :, None] == expert_ids[:, None, :]
    slot = jnp.sum(same_expert & (row_order[None, :] < row_order[:, None])[None], 2)
    x_turn = (expert_ids // 2 - x + x_count) % x_count
    core_turn = (expert_ids % 2 + core) % 2
    column = (
        ((core_turn * x_count + x_turn) * 2 + jnp.arange(2, dtype=jnp.int32)[:, None]) * capacity
        + slot
    ).reshape(-1)
    core_slots = x_count * 2 * capacity
    onehot = (column[:, None] == jnp.arange(2 * core_slots, dtype=jnp.int32)[None, :]).astype(bf16)

    def slots(which):
        chosen = onehot[:, which * core_slots : (which + 1) * core_slots]
        filled = jnp.einsum("rc,rd->cd", chosen, routed_in, preferred_element_type=f32)
        return filled.astype(bf16).reshape(x_count, 1, 2 * capacity, model_width)

    swapped = lax.ppermute(slots(1), "exp", other_core)
    by_x = jnp.concatenate([slots(0), swapped], 1)

    near_block = by_x[0].reshape(-1, model_width)
    near_in = {1: (ahead(near_block), back(near_block))}
    later_block = jnp.concatenate(
        [
            lax.ppermute(by_x[k], "exp", shift_x(k)).reshape(-1, model_width)
            for k in range(1, x_count)
        ]
    )
    near_rows, later_rows = near_block.shape[0], later_block.shape[0]
    half_near, half_later = near_rows // 2, later_rows // 2
    later_in = {1: (ahead(later_block), back(later_block))}
    near_in[2] = ahead(near_in[1][0]), back(near_in[1][1])

    def pair(arrived):
        return [arrived[1], arrived[0]]

    hidden = {1: expert_in([near_block, later_block] + pair(near_in[1]), w_gate, w_up)}
    straight = [((0, 0, near_rows),), ((1, 0, near_rows),)]
    cut_near = [((0, 0, half_near),), ((1, half_near, near_rows),)]
    cut_later = [((0, 0, half_later),), ((1, half_later, later_rows),)]
    for step in range(2, half):
        sent = relay(near_in[step], straight if step < near else cut_near, [hidden[step - 1]])
        near_in[step + 1] = ahead(sent[0]), back(sent[1])
        sent = relay(later_in[step - 1], [((0, 0, later_rows),), ((1, 0, later_rows),)], [hidden[step - 1]])
        later_in[step] = ahead(sent[0]), back(sent[1])
        hidden[step] = expert_in(pair(near_in[step]) + pair(later_in[step - 1]), w_gate, w_up)
    sent = relay(later_in[near], cut_later, [hidden[near]])
    later_in[half] = ahead(sent[0]), back(sent[1])
    last = [*later_in[half], *near_in[half], *pair(later_in[near])]

    near_spots = {half: (half, 2 * half_later, 2 * half_later + half_near)}
    later_spots = {half: (half, 0, half_later)}
    start = 2 * half_later + 2 * half_near
    later_spots[near] = (half, start, start + later_rows)
    for step in range(2, half):
        near_spots[step] = (step, 0, near_rows)
        start = 2 * near_rows
        later_spots[step - 1] = (step, start, start + later_rows)
    near_spots[1] = (1, near_rows + later_rows, 2 * near_rows + later_rows)
    outs = {half: expert_both(last, w_gate, w_up, w_down, [hidden[near]])}
    outs[near] = expert_out(hidden[near], w_down, [outs[half]])

    def home_step(spots, rows, moving, step, offset):
        call, first, second = spots[step]
        half_rows = rows // 2
        if step == near:
            plans = [
                ((first, half_rows, ((0, offset),)), (first + half_rows, half_rows, ())),
                ((second, half_rows, ()), (second + half_rows, half_rows, ((1, offset),))),
            ]
        else:
            plans = [((first, rows, ((0, 0),)),), ((second, rows, ((1, 0),)),)]
        sent = blend(outs[call], moving, plans)
        return ahead(sent[0]), back(sent[1])

    plans = [
        tuple((spots[half][way], rows // 2, ()) for spots, rows in ((later_spots, later_rows), (near_spots, near_rows)))
        for way in (1, 2)
    ]
    sent = blend(outs[half], (), plans)
    later_moving = near_moving = ahead(sent[0]), back(sent[1])
    for step in range(near, 0, -1):
        later_moving = home_step(later_spots, later_rows, later_moving, step, 0)
        if step > 1:
            outs[step - 1] = expert_out(hidden[step - 1], w_down, [later_moving[0]])
        near_moving = home_step(near_spots, near_rows, near_moving, step, half_later)
    (later_sum,) = blend(outs[1], later_moving, [((near_rows, later_rows, ((0, 0), (1, 0))),)])
    (near_sum,) = blend(outs[1], near_moving, [((0, near_rows, ((0, 0), (1, 0))),)])

    later_sum = later_sum.reshape(x_count - 1, 2, 2 * capacity, model_width)
    home = [
        lax.ppermute(later_sum[k - 1], "exp", shift_x(-k)) for k in range(1, x_count)
    ]
    home = jnp.stack([near_sum.reshape(2, 2 * capacity, model_width)] + home)
    swapped = lax.ppermute(home[:, 1], "exp", other_core)
    returned = jnp.stack([home[:, 0], swapped]).reshape(-1, model_width)
    routed = jnp.dot(onehot, returned, preferred_element_type=f32)
    result = (stream + routed).astype(bf16)
    return (result[:rows_here], result[rows_here:])


def solution(mesh):
    in_specs = (
        P("ctx", "exp"),
        P("ctx", "exp"),
        P("ctx", "exp"),
        P("ctx", "exp"),
        P("ctx", "exp"),
        P("ctx", "exp"),
        P("ctx", "exp"),
        P("ctx", "exp"),
        P(),
        P("exp", None),
        P(("ctx", "exp"), None),
        P(("ctx", "exp"), None),
        P(),
        P(),
        P(("ctx", "exp"), None),
        P(("ctx", "exp"), None),
        P("exp", None, "ctx"),
        P("exp", None, "ctx"),
        P("exp", "ctx", None),
    )
    out_specs = (P(("ctx", "exp"), None), P(("ctx", "exp"), None))
    return jax.shard_map(
        on_device, mesh=mesh, in_specs=in_specs, out_specs=out_specs, check_vma=False
    )
```

```python
import functools
import math

import jax
import jax.numpy as jnp
from jax import lax
from jax.experimental import pallas as pl
from jax.experimental.pallas import tpu as pltpu
from jax.sharding import PartitionSpec as P

HEADS = 40
KV_HEADS = 8
HEAD = 128

NEG = -1e30
EPS = 1e-05
SCALE = HEAD ** (-0.5)
EXP2_SCALE = SCALE * math.log2(math.e)
EXTRA = 128
PART = 32
KEY_CHUNK = 256
VALUE_CHUNK = 1024
TILE = 512
VMEM_LIMIT = 48 * 1024 * 1024


def ring_order(count):
    if count % 8:
        return list(range(count))
    major, minor = 4, count // 4
    path = [(0, 0)]
    for b in range(minor):
        span = range(1, major) if b % 2 == 0 else range(major - 1, 0, -1)
        path += [(a, b) for a in span]
    path += [(0, b) for b in range(minor - 1, 0, -1)]
    return [a * minor + b for a, b in path]


def attend_kernel(info_ref, *refs, offsets, after, kv, group):
    owners = len(offsets)
    q_refs = refs[:owners]
    pos_ref, k_ref, v_ref, ks_ref, vs_ref = refs[owners : owners + 5]
    o_ref, q_scr, s_scr = refs[owners + 5 + after :]
    owner = pl.program_id(0)
    stream = pl.program_id(1)
    rows = q_scr.shape[0]
    pre = k_ref.shape[0]
    key_chunk, value_chunk = math.gcd(pre, KEY_CHUNK), math.gcd(pre, VALUE_CHUNK)
    stacked = rows * group
    span_keys = ks_ref.shape[0]
    contract = (((1,), (1,)), ((), ()))
    for i in range(owners):

        @pl.when(owner == i)
        def _(i=i):
            q_scr[...] = q_refs[i][0]

    def run(is_span):
        ctx = info_ref[info_ref.shape[0] - 1]
        if is_span:
            step = offsets[1] - offsets[0] if owners > 1 else 0
            from_here = (info_ref[offsets[0] + owner * step] - ctx) * rows
            lim = from_here + 1 + lax.broadcasted_iota(jnp.int32, (rows, 1), 0)
        else:
            lim = pos_ref[...] - ctx * pre
        lim = jnp.concatenate([lim] * group, axis=0)
        lane = lax.broadcasted_iota(jnp.int32, (rows, EXTRA), 1)
        packed = jnp.full((rows, EXTRA), NEG, jnp.float32)

        def scores(h):
            q = jnp.concatenate(
                [q_scr[:, (h * group + g) * HEAD : (h * group + g + 1) * HEAD] for g in range(group)],
                axis=0,
            )
            top = jnp.full((stacked, HEAD), NEG, jnp.float32)
            for j in range(pre // key_chunk):
                key = k_ref[j * key_chunk : (j + 1) * key_chunk, h * HEAD : (h + 1) * HEAD]
                s = lax.dot_general(q, key, contract, preferred_element_type=jnp.float32)
                if not is_span:
                    pos = j * key_chunk + lax.broadcasted_iota(jnp.int32, (stacked, key_chunk), 1)
                    s = jnp.where(pos < lim, s, NEG)
                s_scr[h, :, j * key_chunk : (j + 1) * key_chunk] = s
                for t in range(key_chunk // HEAD):
                    top = jnp.maximum(top, s[:, t * HEAD : (t + 1) * HEAD])
            m = jnp.max(top, axis=1, keepdims=True)
            s_own = None
            if is_span:
                key = ks_ref[:, h * HEAD : (h + 1) * HEAD]
                s_own = lax.dot_general(q, key, contract, preferred_element_type=jnp.float32)
                pos = lax.broadcasted_iota(jnp.int32, (stacked, span_keys), 1)
                s_own = jnp.where(pos < lim, s_own, NEG)
                m = jnp.maximum(m, jnp.max(s_own, axis=1, keepdims=True))
            return jnp.maximum(m, -1e29), s_own

        def values(h, m, s_own):
            acc = jnp.zeros((stacked, 2 * HEAD), jnp.float32)
            for j in range(pre // value_chunk):
                s = s_scr[h, :, j * value_chunk : (j + 1) * value_chunk]
                w = jnp.exp2((s - m) * EXP2_SCALE).astype(jnp.bfloat16)
                val = v_ref[j * value_chunk : (j + 1) * value_chunk, h * HEAD : (h + 1) * HEAD]
                val = jnp.concatenate([val, jnp.ones_like(val)], axis=1)
                acc = acc + jnp.dot(w, val, preferred_element_type=jnp.float32)
            if is_span:
                w = jnp.exp2((s_own - m) * EXP2_SCALE).astype(jnp.bfloat16)
                val = vs_ref[:, h * HEAD : (h + 1) * HEAD]
                val = jnp.concatenate([val, jnp.ones_like(val)], axis=1)
                acc = acc + jnp.dot(w, val, preferred_element_type=jnp.float32)
            total = acc[:, HEAD:]
            seen = total > 0.0
            safe = jnp.where(seen, total, 1.0)
            out = (acc[:, :HEAD] / safe).astype(jnp.bfloat16)
            lse = jnp.where(seen, m * SCALE + jnp.log(safe), NEG)
            return out, lse

        state = scores(0)
        for h in range(kv):
            following = scores(h + 1) if h + 1 < kv else None
            out, lse = values(h, *state)
            for g in range(group):
                head = h * group + g
                o_ref[0, 0, :, head * HEAD : (head + 1) * HEAD] = out[g * rows : (g + 1) * rows]
                packed = jnp.where(lane % PART == head, lse[g * rows : (g + 1) * rows], packed)
            state = following
        o_ref[0, 0, :, kv * group * HEAD :] = pack_lse(packed, lane)

    @pl.when(stream == 0)
    def _():
        run(True)

    @pl.when(stream == 1)
    def _():
        run(False)


def pack_lse(value, lane):
    first = value.astype(jnp.bfloat16)
    rest = value - first.astype(jnp.float32)
    second = rest.astype(jnp.bfloat16)
    third = rest - second.astype(jnp.float32)
    picked = jnp.where(
        lane < PART,
        first.astype(jnp.float32),
        jnp.where(lane < 2 * PART, second.astype(jnp.float32), third),
    )
    return picked.astype(jnp.bfloat16)


def unpack_lse(extra):
    value = extra.astype(jnp.float32)
    return value[:, :PART] + value[:, PART : 2 * PART] + value[:, 2 * PART : 3 * PART]


def attend(queries, offsets, info, positions, caches, kv, group, after=()):
    owners = len(queries)
    _, rows, width = queries[0].shape
    pre = caches[0].shape[0]
    step = offsets[1] - offsets[0] if owners > 1 else 0
    whole = lambda a: pl.BlockSpec(a.shape, lambda o, s, info: (0,) * a.ndim)
    flops = 4 * owners * 2 * rows * group * kv * pre * HEAD
    return pl.pallas_call(
        functools.partial(
            attend_kernel, offsets=offsets, after=len(after), kv=kv, group=group
        ),
        out_shape=jax.ShapeDtypeStruct((owners, 2, rows, width + EXTRA), jnp.bfloat16),
        grid_spec=pltpu.PrefetchScalarGridSpec(
            num_scalar_prefetch=1,
            grid=(owners, 2),
            in_specs=[pl.BlockSpec((1, rows, width), lambda o, s, info: (s, 0, 0)) for _ in queries]
            + [pl.BlockSpec((rows, 1), lambda o, s, info: (info[offsets[0] + o * step], 0))]
            + [whole(a) for a in caches]
            + [pl.BlockSpec(memory_space=pl.ANY) for _ in after],
            out_specs=pl.BlockSpec(
                (1, 1, rows, width + EXTRA), lambda o, s, info: (o, s, 0, 0)
            ),
            scratch_shapes=[
                pltpu.VMEM((rows, width), jnp.bfloat16),
                pltpu.VMEM((kv, rows * group, pre), jnp.float32),
            ],
        ),
        compiler_params=pltpu.CompilerParams(vmem_limit_bytes=VMEM_LIMIT),
        cost_estimate=pl.CostEstimate(
            flops=2 * flops,
            bytes_accessed=4 * pre * kv * HEAD,
            transcendentals=owners * 2 * rows * group * kv * pre,
        ),
        name="attend",
    )(info, *queries, positions, *caches, *after)


def relay_kernel(*refs, plans, arrays, after):
    outs = refs[arrays + after :]
    for out, plan in zip(outs, plans):
        done = 0
        for index, start, stop in plan:
            out[done : done + stop - start] = refs[index][start:stop]
            done += stop - start


def relay(arrays, plans, after=()):
    rows = [sum(stop - start for _, start, stop in plan) for plan in plans]
    outs = [jax.ShapeDtypeStruct((r, *arrays[0].shape[1:]), arrays[0].dtype) for r in rows]
    return pl.pallas_call(
        functools.partial(relay_kernel, plans=plans, arrays=len(arrays), after=len(after)),
        out_shape=outs,
        in_specs=[pl.BlockSpec(memory_space=pltpu.VMEM)] * len(arrays)
        + [pl.BlockSpec(memory_space=pl.ANY)] * len(after),
        out_specs=[pl.BlockSpec(memory_space=pltpu.VMEM)] * len(outs),
        compiler_params=pltpu.CompilerParams(vmem_limit_bytes=VMEM_LIMIT),
        cost_estimate=pl.CostEstimate(
            flops=0, bytes_accessed=4 * sum(math.prod(o.shape) for o in outs), transcendentals=0
        ),
        name="relay",
    )(*arrays, *after)


def blend_kernel(base_ref, *refs, plans, arrived):
    for out, plan in zip(refs[arrived:], plans):
        done = 0
        for start, rows, adds in plan:
            value = base_ref[start : start + rows].astype(jnp.float32)
            for index, offset in adds:
                value = value + refs[index][offset : offset + rows].astype(jnp.float32)
            out[done : done + rows] = value.astype(jnp.bfloat16)
            done += rows


def blend(base, arrived, plans):
    outs = [
        jax.ShapeDtypeStruct((sum(part[1] for part in plan), base.shape[1]), base.dtype)
        for plan in plans
    ]
    return pl.pallas_call(
        functools.partial(blend_kernel, plans=plans, arrived=len(arrived)),
        out_shape=outs,
        in_specs=[pl.BlockSpec(memory_space=pltpu.VMEM)] * (1 + len(arrived)),
        out_specs=[pl.BlockSpec(memory_space=pltpu.VMEM)] * len(outs),
        compiler_params=pltpu.CompilerParams(vmem_limit_bytes=VMEM_LIMIT),
        cost_estimate=pl.CostEstimate(
            flops=0, bytes_accessed=6 * sum(math.prod(o.shape) for o in outs), transcendentals=0
        ),
        name="blend",
    )(base, *arrived)


def fetch(parts, axis):
    def copy(n, i):
        source, target, sems = parts[n]
        size = target.shape[1 + axis]
        tile = pl.ds(pl.multiple_of(i * size, size), size)
        view = source.at[tile] if axis == 0 else source.at[:, tile]
        return pltpu.make_async_copy(view, target.at[i], sems.at[i])

    def start(i, carry):
        for n in range(len(parts)):
            copy(n, i).start()
        return carry

    lax.fori_loop(0, parts[0][1].shape[0], start, 0)
    return lambda n, i: copy(n, i).wait()


def project_kernel(rows_ref, weight_ref, away_ref, kept_ref, tiles, sems):
    count, _, size = tiles.shape
    wait = fetch([(weight_ref, tiles, sems)], 1)
    half = away_ref.shape[0]

    def step(i, carry):
        wait(0, i)
        out = jnp.dot(rows_ref[...], tiles[i], preferred_element_type=jnp.float32)
        part = pl.ds(pl.multiple_of(i * size, size), size)
        away_ref[:, part] = out[:half].astype(jnp.bfloat16)
        kept_ref[:, part] = out[half:]
        return carry

    lax.fori_loop(0, count, step, 0)


def project(rows, weight):
    count, depth = rows.shape
    width = weight.shape[1]
    tile = math.gcd(width, TILE)
    return pl.pallas_call(
        project_kernel,
        out_shape=[
            jax.ShapeDtypeStruct((count // 2, width), jnp.bfloat16),
            jax.ShapeDtypeStruct((count // 2, width), jnp.float32),
        ],
        in_specs=[
            pl.BlockSpec(memory_space=pltpu.VMEM),
            pl.BlockSpec(memory_space=pltpu.HBM),
        ],
        out_specs=[pl.BlockSpec(memory_space=pltpu.VMEM)] * 2,
        scratch_shapes=[
            pltpu.VMEM((width // tile, depth, tile), jnp.bfloat16),
            pltpu.SemaphoreType.DMA((width // tile,)),
        ],
        compiler_params=pltpu.CompilerParams(vmem_limit_bytes=VMEM_LIMIT),
        cost_estimate=pl.CostEstimate(
            flops=2 * count * depth * width, bytes_accessed=2 * depth * width, transcendentals=0
        ),
        name="project",
    )(rows, weight)


def expert_in_kernel(*refs, blocks, follow=None):
    gate_ref, up_ref, o_ref, rows_ref, gate, up, gate_acc, up_acc, gate_sems, up_sems = refs[blocks:]
    count, size, _ = gate.shape
    wait = fetch([(gate_ref.at[0], gate, gate_sems), (up_ref.at[0], up, up_sems)], 0)
    if follow:
        follow()
    done = 0
    for block in refs[:blocks]:
        rows_ref[done : done + block.shape[0]] = block[...]
        done += block.shape[0]
    gate_acc[...] = jnp.zeros_like(gate_acc)
    up_acc[...] = jnp.zeros_like(up_acc)

    def step(i, carry):
        rows = rows_ref[:, pl.ds(pl.multiple_of(i * size, size), size)]
        wait(0, i)
        gate_acc[...] += jnp.dot(rows, gate[i], preferred_element_type=jnp.float32)
        wait(1, i)
        up_acc[...] += jnp.dot(rows, up[i], preferred_element_type=jnp.float32)
        return carry

    lax.fori_loop(0, count, step, 0)
    gate_h = gate_acc[...]
    hidden = gate_h / (1.0 + jnp.exp(-gate_h)) * up_acc[...]
    o_ref[...] = hidden.astype(jnp.bfloat16)


def expert_in(blocks, w_gate, w_up):
    depth, units = w_gate.shape[1:]
    if any(b.shape[0] % 16 for b in blocks):
        blocks = [jnp.concatenate(blocks)]
    rows = sum(b.shape[0] for b in blocks)
    tile = math.gcd(depth, TILE)
    return pl.pallas_call(
        functools.partial(expert_in_kernel, blocks=len(blocks)),
        out_shape=jax.ShapeDtypeStruct((rows, units), jnp.bfloat16),
        in_specs=[pl.BlockSpec(memory_space=pltpu.VMEM)] * len(blocks)
        + [pl.BlockSpec(memory_space=pltpu.HBM)] * 2,
        out_specs=pl.BlockSpec(memory_space=pltpu.VMEM),
        scratch_shapes=[pltpu.VMEM((rows, depth), jnp.bfloat16)]
        + [pltpu.VMEM((depth // tile, tile, units), jnp.bfloat16)] * 2
        + [pltpu.VMEM((rows, units), jnp.float32)] * 2
        + [pltpu.SemaphoreType.DMA((depth // tile,))] * 2,
        compiler_params=pltpu.CompilerParams(vmem_limit_bytes=VMEM_LIMIT),
        cost_estimate=pl.CostEstimate(
            flops=4 * rows * depth * units,
            bytes_accessed=4 * depth * units,
            transcendentals=rows * units,
        ),
        name="expert_in",
    )(*blocks, w_gate, w_up)


def expert_both_kernel(*refs, blocks):
    gate_ref, up_ref, down_ref, o_ref, hidden_ref, down, down_sems = refs[blocks : blocks + 7]
    inner = refs[:blocks] + (gate_ref, up_ref, hidden_ref) + refs[blocks + 7 :]
    holder = {}

    def follow():
        holder["wait"] = fetch([(down_ref.at[0], down, down_sems)], 1)

    expert_in_kernel(*inner, blocks=blocks, follow=follow)
    count, _, size = down.shape

    def step(i, carry):
        holder["wait"](0, i)
        out = jnp.dot(hidden_ref[...], down[i], preferred_element_type=jnp.float32)
        o_ref[:, pl.ds(pl.multiple_of(i * size, size), size)] = out.astype(jnp.bfloat16)
        return carry

    lax.fori_loop(0, count, step, 0)


def expert_both(blocks, w_gate, w_up, w_down, after=()):
    depth, units = w_gate.shape[1:]
    width = w_down.shape[2]
    if any(b.shape[0] % 16 for b in blocks):
        blocks = [jnp.concatenate(blocks)]
    rows = sum(b.shape[0] for b in blocks)
    tile, out_tile = math.gcd(depth, TILE), math.gcd(width, TILE)

    def kernel(*refs):
        count = len(blocks) + 3
        expert_both_kernel(*refs[:count], *refs[count + len(after) :], blocks=len(blocks))

    return pl.pallas_call(
        kernel,
        out_shape=jax.ShapeDtypeStruct((rows, width), jnp.bfloat16),
        in_specs=[pl.BlockSpec(memory_space=pltpu.VMEM)] * len(blocks)
        + [pl.BlockSpec(memory_space=pltpu.HBM)] * 3
        + [pl.BlockSpec(memory_space=pl.ANY)] * len(after),
        out_specs=pl.BlockSpec(memory_space=pltpu.VMEM),
        scratch_shapes=[
            pltpu.VMEM((rows, units), jnp.bfloat16),
            pltpu.VMEM((width // out_tile, units, out_tile), jnp.bfloat16),
            pltpu.SemaphoreType.DMA((width // out_tile,)),
            pltpu.VMEM((rows, depth), jnp.bfloat16),
        ]
        + [pltpu.VMEM((depth // tile, tile, units), jnp.bfloat16)] * 2
        + [pltpu.VMEM((rows, units), jnp.float32)] * 2
        + [pltpu.SemaphoreType.DMA((depth // tile,))] * 2,
        compiler_params=pltpu.CompilerParams(vmem_limit_bytes=VMEM_LIMIT),
        cost_estimate=pl.CostEstimate(
            flops=4 * rows * depth * units + 2 * rows * units * width,
            bytes_accessed=4 * depth * units + 2 * units * width,
            transcendentals=rows * units,
        ),
        name="expert_both",
    )(*blocks, w_gate, w_up, w_down, *after)


def expert_out_kernel(hidden_ref, down_ref, *refs):
    o_ref, down, sems = refs[-3:]
    count, _, size = down.shape
    wait = fetch([(down_ref.at[0], down, sems)], 1)

    def step(i, carry):
        wait(0, i)
        out = jnp.dot(hidden_ref[...], down[i], preferred_element_type=jnp.float32)
        o_ref[:, pl.ds(pl.multiple_of(i * size, size), size)] = out.astype(jnp.bfloat16)
        return carry

    lax.fori_loop(0, count, step, 0)


def expert_out(hidden, w_down, after=()):
    rows, units = hidden.shape
    width = w_down.shape[2]
    tile = math.gcd(width, TILE)
    return pl.pallas_call(
        expert_out_kernel,
        out_shape=jax.ShapeDtypeStruct((rows, width), jnp.bfloat16),
        in_specs=[
            pl.BlockSpec(memory_space=pltpu.VMEM),
            pl.BlockSpec(memory_space=pltpu.HBM),
        ]
        + [pl.BlockSpec(memory_space=pl.ANY)] * len(after),
        out_specs=pl.BlockSpec(memory_space=pltpu.VMEM),
        scratch_shapes=[
            pltpu.VMEM((width // tile, units, tile), jnp.bfloat16),
            pltpu.SemaphoreType.DMA((width // tile,)),
        ],
        compiler_params=pltpu.CompilerParams(vmem_limit_bytes=VMEM_LIMIT),
        cost_estimate=pl.CostEstimate(
            flops=2 * rows * units * width, bytes_accessed=2 * units * width, transcendentals=0
        ),
        name="expert_out",
    )(hidden, w_down, *after)


def merge(parts, heads):
    for head in range(heads):
        lses = [lse[:, head : head + 1] for _, lse in parts]
        top = functools.reduce(jnp.maximum, lses)
        weights = [jnp.exp(lse - top) for lse in lses]
        total = sum(weights)
        inverse = 1.0 / total
        out = 0.0
        for (value, _), weight in zip(parts, weights):
            out = out + value(head).astype(jnp.float32) * (weight * inverse)
        yield head, out, top + jnp.log(total)


def reader(ref):
    return lambda head: ref[:, head * HEAD : (head + 1) * HEAD]


def combine_kernel(part_ref, *refs, heads, present):
    rows = part_ref.shape[2]
    width = heads * HEAD
    recv_refs, outs = refs[: sum(present)], refs[sum(present) :]
    lane = lax.broadcasted_iota(jnp.int32, (rows, EXTRA), 1)
    taken = 0
    for way, there in enumerate(present):
        part, out_ref = part_ref.at[way, 0], outs[way]
        if not there:
            out_ref[...] = part[...]
            continue
        recv = recv_refs[taken]
        taken += 1
        parts = [(reader(ref), unpack_lse(ref[:, width:])) for ref in (recv, part)]
        packed = jnp.full((rows, EXTRA), NEG, jnp.float32)
        for head, out, lse in merge(parts, heads):
            out_ref[:, head * HEAD : (head + 1) * HEAD] = out.astype(jnp.bfloat16)
            packed = jnp.where(lane % PART == head, lse, packed)
        out_ref[:, width:] = pack_lse(packed, lane)


def combine(recvs, part, stream, heads):
    _, _, rows, width = part.shape
    there = [r for r in recvs if r is not None]
    return pl.pallas_call(
        functools.partial(
            combine_kernel, heads=heads, present=tuple(r is not None for r in recvs)
        ),
        out_shape=[jax.ShapeDtypeStruct((rows, width), jnp.bfloat16)] * 2,
        grid=(1,),
        in_specs=[pl.BlockSpec((2, 1, rows, width), lambda i: (0, stream, 0, 0))]
        + [pl.BlockSpec((rows, width), lambda i: (0, 0)) for _ in there],
        out_specs=[pl.BlockSpec((rows, width), lambda i: (0, 0))] * 2,
        compiler_params=pltpu.CompilerParams(vmem_limit_bytes=VMEM_LIMIT),
        cost_estimate=pl.CostEstimate(
            flops=16 * rows * width, bytes_accessed=12 * rows * width, transcendentals=0
        ),
        name="combine",
    )(part, *there)


def finish_kernel(own_ref, s_left, s_right, d_left, d_right, q_ref, k_ref, v_ref, o_ref, *, heads, group):
    width = heads * HEAD
    for stream, arrived in enumerate([(s_left, s_right), (d_left, d_right)]):
        refs = [own_ref.at[0, stream], *arrived]
        parts = [(reader(ref), unpack_lse(ref[:, width:])) for ref in refs]
        if stream == 1:
            scores = []
            for head in range(heads):
                kv = head // group
                q = q_ref[:, head * HEAD : (head + 1) * HEAD].astype(jnp.float32)
                k = k_ref[:, kv * HEAD : (kv + 1) * HEAD].astype(jnp.float32)
                scores.append(jnp.sum(q * k, axis=1, keepdims=True) * SCALE)
            own_value = lambda head: v_ref[:, (head // group) * HEAD : (head // group + 1) * HEAD]
            parts.append((own_value, jnp.concatenate(scores, axis=1)))
        for head, out, _ in merge(parts, heads):
            o_ref[stream, :, head * HEAD : (head + 1) * HEAD] = out.astype(jnp.bfloat16)


def finish(own, span_arrived, decode_arrived, decode_q, decode_k, decode_v, heads, group):
    _, _, rows, width = own.shape
    return pl.pallas_call(
        functools.partial(finish_kernel, heads=heads, group=group),
        out_shape=jax.ShapeDtypeStruct((2, rows, heads * HEAD), jnp.bfloat16),
        in_specs=[pl.BlockSpec(memory_space=pltpu.VMEM)] * 8,
        out_specs=pl.BlockSpec(memory_space=pltpu.VMEM),
        compiler_params=pltpu.CompilerParams(vmem_limit_bytes=VMEM_LIMIT),
        cost_estimate=pl.CostEstimate(
            flops=16 * rows * width, bytes_accessed=16 * rows * width, transcendentals=0
        ),
        name="finish",
    )(own, *span_arrived, *decode_arrived, decode_q, decode_k, decode_v)


def on_device(
    span_q,
    decode_q,
    k_cache,
    v_cache,
    span_k,
    span_v,
    decode_k,
    decode_v,
    decode_pos,
    out_weight,
    span_resid,
    decode_resid,
    norm_gain,
    router,
    span_expert,
    decode_expert,
    w_gate,
    w_up,
    w_down,
):
    f32, bf16 = jnp.float32, jnp.bfloat16
    tok_rows, row_width = span_q.shape
    pre_rows = k_cache.shape[0]
    kv = k_cache.shape[1] // HEAD
    group = HEADS // KV_HEADS
    heads = kv * group
    model_width = span_resid.shape[1]
    ctx_count, exp_count = lax.axis_size("ctx"), lax.axis_size("exp")
    ctx, exp = lax.axis_index("ctx"), lax.axis_index("exp")
    x_count = exp_count // 2
    x, core = exp // 2, exp % 2

    ring = ring_order(ctx_count)
    half = ctx_count // 2
    forward = [(ring[i], ring[(i + 1) % ctx_count]) for i in range(ctx_count)]
    backward = [(b, a) for a, b in forward]
    place = [0] * ctx_count
    for i, c in enumerate(ring):
        place[c] = i
    here = sum(jnp.where(ctx == c, i, 0) for c, i in enumerate(place) if i)
    spot = (here + jnp.arange(ctx_count + 1, dtype=jnp.int32)) % ctx_count
    owner = sum(jnp.where(spot == i, c, 0) for i, c in enumerate(ring) if c)
    info = jnp.where(jnp.arange(ctx_count + 1) == ctx_count, ctx, owner).astype(jnp.int32)
    positions = decode_pos[:, None]
    caches = (k_cache, v_cache, span_k, span_v)

    def ahead(value):
        return lax.ppermute(value, "ctx", forward)

    def back(value):
        return lax.ppermute(value, "ctx", backward)

    other_core = [(e, e ^ 1) for e in range(exp_count)]

    def shift_x(step):
        return [(e, ((e // 2 + step) % x_count) * 2 + e % 2) for e in range(exp_count)]

    def attend_for(queries, offsets, after=()):
        offsets = tuple(offset % ctx_count for offset in offsets)
        return attend(queries, offsets, info, positions, caches, kv, group, after)

    queries = jnp.stack([span_q, decode_q])
    both = [((0, 0, 2),), ((1, 0, 2),)]
    from_back, from_ahead = ahead(queries), back(queries)
    own_part = attend_for([queries], [0])
    from_back, from_ahead = relay([from_back, from_ahead], both, [own_part])
    parts = {}
    for step in range(1, half - 1):
        arrived = ahead(from_back), back(from_ahead)
        done = attend_for([from_ahead, from_back], [step, -step])
        plans = both if step < half - 2 else both + [((0, 0, 1),), ((1, 1, 2),)]
        from_back, from_ahead, *sent = relay(arrived, plans, [done])
        parts[step] = done
    arrived = ahead(sent[0]), back(sent[1])
    near = half - 1
    (far,) = relay(arrived, [((0, 0, 1), (1, 0, 1))], [done])
    far_part = attend_for([far], [half])
    parts[near] = attend_for([from_ahead, from_back], [near, -near])

    moving = [(ahead(far_part[0, 0]), None), (None, back(far_part[0, 1]))]
    for step in range(near, 0, -1):
        for stream in range(2):
            sent = combine(moving[stream], parts[step], stream, heads)
            moving[stream] = ahead(sent[0]), back(sent[1])
    attn = finish(own_part, *moving, decode_q, decode_k, decode_v, heads, group)

    rows_here = span_resid.shape[0]
    by_owner = attn.reshape(2, x_count, 2, rows_here, row_width)

    def rows_for(core_index):
        picked = lax.dynamic_index_in_dim(by_owner, core_index, 2, keepdims=False)
        turned = [
            lax.dynamic_index_in_dim(picked, (x + k) % x_count, 1, keepdims=False)
            for k in range(x_count)
        ]
        return turned

    ordered = jnp.stack(rows_for(1 - core) + rows_for(core))
    away, kept = project(ordered.reshape(-1, row_width), out_weight)
    arrived = lax.ppermute(away, "exp", other_core)
    chip_sum = (kept + arrived.astype(f32)).reshape(x_count, 2 * rows_here, model_width)
    total = chip_sum[x_count - 1]
    for k in range(x_count - 2, -1, -1):
        moved = lax.ppermute(total.astype(bf16), "exp", shift_x(1))
        total = chip_sum[k] + moved.astype(f32)
    resid = jnp.concatenate([span_resid, decode_resid]).astype(f32)
    stream = total + resid
    normed = (
        stream
        * lax.rsqrt(jnp.mean(stream * stream, -1, keepdims=True) + EPS)
        * norm_gain.astype(f32)
    ).astype(bf16)

    expert_ids = jnp.stack([span_expert[:, 0], decode_expert[:, 0]])
    expert_total = router.shape[1]
    logits = jnp.dot(normed, router, preferred_element_type=f32)
    flat_ids = expert_ids.reshape(-1)
    expert_iota = jnp.arange(expert_total, dtype=jnp.int32)
    picked = jnp.sum(jnp.where(flat_ids[:, None] == expert_iota, logits, 0.0), -1)
    routed_in = (normed.astype(f32) * jax.nn.sigmoid(picked)[:, None]).astype(bf16)
    capacity = 2 * tok_rows // (exp_count * exp_count)
    row_order = jnp.arange(rows_here, dtype=jnp.int32)
    same_expert = expert_ids[:, :, None] == expert_ids[:, None, :]
    slot = jnp.sum(same_expert & (row_order[None, :] < row_order[:, None])[None], 2)
    x_turn = (expert_ids // 2 - x + x_count) % x_count
    core_turn = (expert_ids % 2 + core) % 2
    column = (
        ((core_turn * x_count + x_turn) * 2 + jnp.arange(2, dtype=jnp.int32)[:, None]) * capacity
        + slot
    ).reshape(-1)
    core_slots = x_count * 2 * capacity
    onehot = (column[:, None] == jnp.arange(2 * core_slots, dtype=jnp.int32)[None, :]).astype(bf16)

    def slots(which):
        chosen = onehot[:, which * core_slots : (which + 1) * core_slots]
        filled = jnp.einsum("rc,rd->cd", chosen, routed_in, preferred_element_type=f32)
        return filled.astype(bf16).reshape(x_count, 1, 2 * capacity, model_width)

    swapped = lax.ppermute(slots(1), "exp", other_core)
    by_x = jnp.concatenate([slots(0), swapped], 1)

    near_block = by_x[0].reshape(-1, model_width)
    near_in = {1: (ahead(near_block), back(near_block))}
    later_block = jnp.concatenate(
        [
            lax.ppermute(by_x[k], "exp", shift_x(k)).reshape(-1, model_width)
            for k in range(1, x_count)
        ]
    )
    near_rows, later_rows = near_block.shape[0], later_block.shape[0]
    half_near, half_later = near_rows // 2, later_rows // 2
    later_in = {1: (ahead(later_block), back(later_block))}
    near_in[2] = ahead(near_in[1][0]), back(near_in[1][1])

    def pair(arrived):
        return [arrived[1], arrived[0]]

    hidden = {1: expert_in([near_block, later_block] + pair(near_in[1]), w_gate, w_up)}
    straight = [((0, 0, near_rows),), ((1, 0, near_rows),)]
    cut_near = [((0, 0, half_near),), ((1, half_near, near_rows),)]
    cut_later = [((0, 0, half_later),), ((1, half_later, later_rows),)]
    for step in range(2, half):
        sent = relay(near_in[step], straight if step < near else cut_near, [hidden[step - 1]])
        near_in[step + 1] = ahead(sent[0]), back(sent[1])
        sent = relay(later_in[step - 1], [((0, 0, later_rows),), ((1, 0, later_rows),)], [hidden[step - 1]])
        later_in[step] = ahead(sent[0]), back(sent[1])
        hidden[step] = expert_in(pair(near_in[step]) + pair(later_in[step - 1]), w_gate, w_up)
    sent = relay(later_in[near], cut_later, [hidden[near - 1]])
    later_in[half] = ahead(sent[0]), back(sent[1])
    last = [*later_in[half], *near_in[half], *pair(later_in[near])]

    near_spots = {half: (half, 2 * half_later, 2 * half_later + half_near)}
    later_spots = {half: (half, 0, half_later)}
    start = 2 * half_later + 2 * half_near
    later_spots[near] = (half, start, start + later_rows)
    for step in range(2, half):
        near_spots[step] = (step, 0, near_rows)
        start = 2 * near_rows
        later_spots[step - 1] = (step, start, start + later_rows)
    near_spots[1] = (1, near_rows + later_rows, 2 * near_rows + later_rows)
    outs = {half: expert_both(last, w_gate, w_up, w_down, [hidden[near]])}
    outs[near] = expert_out(hidden[near], w_down, [outs[half]])

    def home_step(spots, rows, moving, step, offset):
        call, first, second = spots[step]
        half_rows = rows // 2
        if step == near:
            plans = [
                ((first, half_rows, ((0, offset),)), (first + half_rows, half_rows, ())),
                ((second, half_rows, ()), (second + half_rows, half_rows, ((1, offset),))),
            ]
        else:
            plans = [((first, rows, ((0, 0),)),), ((second, rows, ((1, 0),)),)]
        sent = blend(outs[call], moving, plans)
        return ahead(sent[0]), back(sent[1])

    plans = [
        tuple((spots[half][way], rows // 2, ()) for spots, rows in ((later_spots, later_rows), (near_spots, near_rows)))
        for way in (1, 2)
    ]
    sent = blend(outs[half], (), plans)
    later_moving = near_moving = ahead(sent[0]), back(sent[1])
    for step in range(near, 0, -1):
        later_moving = home_step(later_spots, later_rows, later_moving, step, 0)
        if step > 1:
            outs[step - 1] = expert_out(hidden[step - 1], w_down, [later_moving[0]])
        near_moving = home_step(near_spots, near_rows, near_moving, step, half_later)
    (later_sum,) = blend(outs[1], later_moving, [((near_rows, later_rows, ((0, 0), (1, 0))),)])
    (near_sum,) = blend(outs[1], near_moving, [((0, near_rows, ((0, 0), (1, 0))),)])

    later_sum = later_sum.reshape(x_count - 1, 2, 2 * capacity, model_width)
    home = [
        lax.ppermute(later_sum[k - 1], "exp", shift_x(-k)) for k in range(1, x_count)
    ]
    home = jnp.stack([near_sum.reshape(2, 2 * capacity, model_width)] + home)
    swapped = lax.ppermute(home[:, 1], "exp", other_core)
    returned = jnp.stack([home[:, 0], swapped]).reshape(-1, model_width)
    routed = jnp.dot(onehot, returned, preferred_element_type=f32)
    result = (stream + routed).astype(bf16)
    return (result[:rows_here], result[rows_here:])


def solution(mesh):
    in_specs = (
        P("ctx", "exp"),
        P("ctx", "exp"),
        P("ctx", "exp"),
        P("ctx", "exp"),
        P("ctx", "exp"),
        P("ctx", "exp"),
        P("ctx", "exp"),
        P("ctx", "exp"),
        P(),
        P("exp", None),
        P(("ctx", "exp"), None),
        P(("ctx", "exp"), None),
        P(),
        P(),
        P(("ctx", "exp"), None),
        P(("ctx", "exp"), None),
        P("exp", None, "ctx"),
        P("exp", None, "ctx"),
        P("exp", "ctx", None),
    )
    out_specs = (P(("ctx", "exp"), None), P(("ctx", "exp"), None))
    return jax.shard_map(
        on_device, mesh=mesh, in_specs=in_specs, out_specs=out_specs, check_vma=False
    )
```
